128 devices in a mesh: grp: 4 (over x_hi, core), tile: 32 (over x_lo, y, z).
Axes of the slice: x: 4 (x_hi: 2, x_lo: 2; x = x_hi * 2 + x_lo), y: 4, z: 4, core: 2. Of those that a mesh axis runs over, the one named last changes fastest.
Arguments:
- start_field: float32 [512, 512, 512], P('grp', 'tile'), may hold values from -4 to 4
- class_ids: int32 [512, 512], P('tile'), may hold values from 0 to 7
- run_levels: int32 [512, 8], replicated, may hold values from 0 to 7
- steepness: float32 [512], replicated, may hold values from 0.1 to 1
- step_pick: int32 [512], replicated, may hold values from 1 to 4
- input_layer: float32 [69, 2048], replicated, may hold values from -2 to 2
- output_layer: bfloat16 [2048, 262144], P(None, ('grp', 'tile')), may hold values from -0.125 to 0.125
- output_bias: float32 [262144], P(('grp', 'tile')), may hold values from -1.5 to 1.5
Outputs:
- misfit: bfloat16 [512, 262144], P(None, ('grp', 'tile'))
- output_next: bfloat16 [2048, 262144], P(None, ('grp', 'tile'))
- bias_next: float32 [262144], P(('grp', 'tile'))
- input_next: float32 [69, 2048], replicated
The draws below stay inside these ranges and needn't reach their ends.
All inputs are finite; a program needn't handle non-finite values.
Results may differ from the reference program's by a relative error of at most 0.0029.
The reference program's roundings to bfloat16 on the way (of `hidden` and `slope`) count: a program that leaves them out, or rounds other values in their place, can miss the bound.
Values sent between devices are 32-bit elements; how exact they have to be, the bound alone decides.
A program may use at most 128 MiB of HBM per device.

```python
import math
import jax
import jax.numpy as jnp
from jax import lax

GY = 512
STEPS = 4
HID = 2048
NCLASS = 8
LEVELS = 8
RUNS = 512
GX = 512
CELLS = 262144
CS = 2048
FEAT = 69
N_GRP = 4
N_TILE = 32
DEVICES = 128


def set_ends(result, stream_key, smallest, largest):
    dims = result.shape
    place = [jax.random.randint(jax.random.fold_in(stream_key, axis), (), 0, dims[axis]) for axis in range(len(dims))]
    result = result.at[tuple(place)].set(smallest)
    longest = dims.index(max(dims))
    place[longest] = (place[longest] + 1) % dims[longest]
    return result.at[tuple(place)].set(largest)


def levels(key, extent, pieces, low, largest):
    level, own = 1.0, jax.random.fold_in(key, 6)
    for axis_at, shards_of in pieces:
        heights = jnp.exp(jax.random.uniform(jax.random.fold_in(own, axis_at), (shards_of,), jnp.float32, low / len(pieces), largest / len(pieces)))
        level = level * jnp.repeat(heights, extent[axis_at] // shards_of).reshape([-1 if axis == axis_at else 1 for axis in range(len(extent))])
    return level


def noise(key, dims, deviation, most, cuts=(), held_as=jnp.bfloat16):
    factor_of = levels(key, dims, cuts, -0.22, 0.18) if cuts else 1.0
    values = jax.random.normal(key, dims, jnp.float32) * deviation * factor_of
    return jnp.minimum(jnp.maximum(values, -most), most).astype(held_as)


def setup_inputs(seed: int = 0) -> dict:
    key_list = jax.random.split(jax.random.key(seed), 9)
    start_field = noise(key_list[0], (RUNS, GX, GY), 1.0, 4.0, ((0, 4), (1, 32)), jnp.float32)
    class_ids = set_ends(jax.random.randint(key_list[1], (GX, GY), 0, NCLASS), jax.random.fold_in(key_list[1], 1), 0, NCLASS - 1).astype(jnp.int32)
    run_levels = set_ends(jax.random.randint(key_list[2], (RUNS, NCLASS), 0, LEVELS), jax.random.fold_in(key_list[2], 1), 0, LEVELS - 1).astype(jnp.int32)
    steepness = jnp.clip(jnp.exp(jax.random.uniform(key_list[3], (RUNS,), jnp.float32, math.log(0.1), math.log(1.0))), 0.1, 1.0)
    step_pick = set_ends(jax.random.randint(key_list[4], (RUNS,), 1, STEPS + 1), jax.random.fold_in(key_list[4], 1), 1, STEPS).astype(jnp.int32)
    input_layer = noise(key_list[5], (FEAT, HID), (NCLASS + 2) ** -0.5, 2.0, (), jnp.float32)
    output_layer = noise(key_list[6], (HID, CELLS), HID ** -0.5, 0.125, ((1, 128),))
    output_bias = noise(key_list[7], (CELLS,), 0.3, 1.5, ((0, 128),), jnp.float32)
    return dict(start_field=start_field, class_ids=class_ids, run_levels=run_levels, steepness=steepness, step_pick=step_pick, input_layer=input_layer, output_layer=output_layer, output_bias=output_bias)


def coefficients(run_levels, class_ids):
    table = 0.03 * jnp.exp(run_levels.astype(jnp.float32) * jnp.log(jnp.float32(1.35)))
    kappa = jnp.zeros((run_levels.shape[0],) + class_ids.shape, jnp.float32)
    for klass in range(run_levels.shape[1]):
        picked = jnp.where(class_ids == klass, 1.0, 0.0).astype(jnp.float32)
        kappa = kappa + picked[None] * table[:, klass][:, None, None]
    return kappa


def advance(field, kappa, steep):
    ratio = field * field
    spread = kappa * (1.0 + steep * ratio) / (1.0 + ratio)
    fpad = jnp.pad(field, ((0, 0), (0, 0), (1, 1)))
    spad = jnp.pad(spread, ((0, 0), (0, 0), (1, 1)))
    centre = field[:, 1:-1]
    middle = spread[:, 1:-1]
    total = centre + 0.5 * (middle + spread[:, :-2]) * (field[:, :-2] - centre)
    total = total + 0.5 * (middle + spread[:, 2:]) * (field[:, 2:] - centre)
    total = total + 0.5 * (middle + spad[:, 1:-1, :-2]) * (fpad[:, 1:-1, :-2] - centre)
    total = total + 0.5 * (middle + spad[:, 1:-1, 2:]) * (fpad[:, 1:-1, 2:] - centre)
    return total


def features(run_levels, step_pick, steepness):
    count = run_levels.shape[0]
    onehot = (run_levels[:, :, None] == jnp.arange(LEVELS, dtype=jnp.int32)[None, None, :]).astype(jnp.float32)
    onehot = onehot.reshape(count, -1)
    moment = (step_pick[:, None] == jnp.arange(1, STEPS + 1, dtype=jnp.int32)[None, :]).astype(jnp.float32)
    return jnp.concatenate([onehot, moment, steepness[:, None]], axis=1)


def dsilu(pre):
    logistic = jax.nn.sigmoid(pre)
    return logistic * (1.0 + pre * (1.0 - logistic))


def reference(start_field, class_ids, run_levels, steepness, step_pick, input_layer, output_layer, output_bias):
    kappa = coefficients(run_levels, class_ids)
    kappa_pad = jnp.pad(kappa, ((0, 0), (1, 1), (0, 0)))
    steep = steepness[:, None, None]
    field = start_field
    snapshot = jnp.zeros_like(start_field)
    for step in range(STEPS):
        wide = jnp.pad(field, ((0, 0), (1, 1), (0, 0)))
        field = advance(wide, kappa_pad, steep)
        snapshot = jnp.where(step_pick[:, None, None] == step + 1, field, snapshot)
    target = snapshot.reshape(RUNS, N_TILE, N_GRP, CS).transpose(2, 1, 0, 3).reshape(DEVICES, RUNS, CS)
    feats = features(run_levels, step_pick, steepness)
    pre = jnp.dot(feats, input_layer, precision=lax.Precision.HIGHEST)
    hidden = jax.nn.silu(pre).astype(jnp.bfloat16)
    weights = output_layer.reshape(HID, DEVICES, CS).transpose(1, 0, 2)
    biases = output_bias.reshape(DEVICES, CS)

    def learn_block(back, blocks):
        weight, bias, goal = blocks
        error = jnp.dot(hidden, weight, preferred_element_type=jnp.float32) + bias[None, :] - goal
        slope = (error * (2.0 / RUNS)).astype(jnp.bfloat16)
        grad = lax.dot_general(hidden, slope, (((0,), (0,)), ((), ())), preferred_element_type=jnp.float32)
        new_weight = (weight.astype(jnp.float32) - 0.5 * grad).astype(jnp.bfloat16)
        new_bias = bias - 0.5 * jnp.sum(slope.astype(jnp.float32), axis=0)
        back = back + lax.dot_general(slope, weight, (((1,), (1,)), ((), ())), preferred_element_type=jnp.float32)
        return back, (error.astype(jnp.bfloat16), new_weight, new_bias)

    back, outputs = lax.scan(learn_block, jnp.zeros((RUNS, HID), jnp.float32), (weights, biases, target))
    errors, new_weights, new_biases = outputs
    misfit = errors.transpose(1, 0, 2).reshape(RUNS, CELLS)
    output_next = new_weights.transpose(1, 0, 2).reshape(HID, CELLS)
    bias_next = new_biases.reshape(CELLS)
    slope_in = back * dsilu(pre)
    grad_in = lax.dot_general(feats, slope_in, (((0,), (0,)), ((), ())), precision=lax.Precision.HIGHEST)
    input_next = input_layer - 2.0 * grad_in
    return misfit, output_next, bias_next, input_next
```

```python
import jax
import jax.numpy as jnp
from jax import lax
from jax.sharding import Mesh
from jax.sharding import PartitionSpec as P

STEPS = 4
LEVELS = 8
GRP = ("grp_0", "grp_1")
GRP_TILE = ("grp_0", "grp_1", "tile")


def with_halo(value, sides, width):
    for axis, dim in sides:
        size, length = (lax.axis_size(axis), value.shape[dim])
        up = [(i, (i + 1) % size) for i in range(size - 1)]
        down = [(j, i) for i, j in up]
        last = lax.slice_in_dim(value, length - width, length, axis=dim)
        initial = lax.slice_in_dim(value, 0, width, axis=dim)
        before = lax.ppermute(last, axis, up)
        after = lax.ppermute(initial, axis, down)
        value = jnp.concatenate([before, value, after], axis=dim)
    return value


def in_blocks(value, dim, length):
    shape = value.shape
    tiles = value.reshape(*shape[:dim], length, shape[dim] // length, *shape[dim + 1 :])
    return jnp.moveaxis(tiles, dim, 0)


def in_order(tiles, dim):
    tiles = jnp.moveaxis(tiles, 0, dim)
    shape = tiles.shape
    return tiles.reshape(*shape[:dim], shape[dim] * shape[dim + 1], *shape[dim + 2 :])


def turned_blocks(tiles, axes, order):
    inside = tiles.shape[1:]
    out = tiles.reshape(*(lax.axis_size(a) for a in axes), *inside)
    for k in order:
        out = lax.all_to_all(out, axes[k], k, k, tiled=True)
    return out.reshape(-1, *inside)


def core_and_chips(value, groups, order, split_dim, concat_dim):
    length = lax.axis_size(groups[0]) * lax.axis_size(groups[1])
    tiles = in_blocks(value, split_dim, length)
    return in_order(turned_blocks(tiles, groups, order), concat_dim)


def coefficients(run_levels, class_ids):
    table = 0.03 * jnp.exp(run_levels.astype(jnp.float32) * jnp.log(jnp.float32(1.35)))
    kappa = jnp.zeros((run_levels.shape[0],) + class_ids.shape, jnp.float32)
    for klass in range(run_levels.shape[1]):
        picked = jnp.where(class_ids == klass, 1.0, 0.0).astype(jnp.float32)
        kappa = kappa + picked[None] * table[:, klass][:, None, None]
    return kappa


def advance(field, kappa, steep):
    ratio = field * field
    spread = kappa * (1.0 + steep * ratio) / (1.0 + ratio)
    fpad = jnp.pad(field, ((0, 0), (0, 0), (1, 1)))
    spad = jnp.pad(spread, ((0, 0), (0, 0), (1, 1)))
    centre = field[:, 1:-1]
    middle = spread[:, 1:-1]
    total = centre + 0.5 * (middle + spread[:, :-2]) * (field[:, :-2] - centre)
    total = total + 0.5 * (middle + spread[:, 2:]) * (field[:, 2:] - centre)
    total = total + 0.5 * (middle + spad[:, 1:-1, :-2]) * (fpad[:, 1:-1, :-2] - centre)
    total = total + 0.5 * (middle + spad[:, 1:-1, 2:]) * (fpad[:, 1:-1, 2:] - centre)
    return total


def features(run_levels, step_pick, steepness):
    count = run_levels.shape[0]
    onehot = (run_levels[:, :, None] == jnp.arange(LEVELS, dtype=jnp.int32)[None, None, :]).astype(
        jnp.float32
    )
    onehot = onehot.reshape(count, -1)
    moment = (step_pick[:, None] == jnp.arange(1, STEPS + 1, dtype=jnp.int32)[None, :]).astype(
        jnp.float32
    )
    return jnp.concatenate([onehot, moment, steepness[:, None]], axis=1)


def dsilu(pre):
    logistic = jax.nn.sigmoid(pre)
    return logistic * (1.0 + pre * (1.0 - logistic))


def on_device(
    start_field, class_ids, run_levels, steepness, step_pick, input_layer, output_layer, output_bias
):
    local_runs, rows, columns = start_field.shape
    first_run = lax.axis_index(GRP) * local_runs
    levels_here = lax.dynamic_slice_in_dim(run_levels, first_run, local_runs, 0)
    steep = lax.dynamic_slice_in_dim(steepness, first_run, local_runs, 0)[:, None, None]
    pick_here = lax.dynamic_slice_in_dim(step_pick, first_run, local_runs, 0)[:, None, None]
    snapshot = jnp.zeros_like(start_field)
    class_wide = with_halo(class_ids + 1, (("tile", 0),), STEPS)
    kappa_wide = coefficients(levels_here, class_wide - 1)
    wide = with_halo(start_field, (("tile", 1),), STEPS)
    first_row = lax.axis_index("tile") * rows - STEPS
    total_rows = rows * lax.axis_size("tile")
    span = kappa_wide.shape[1]
    for step in range(STEPS):
        margin = STEPS - step - 1
        kappa_now = kappa_wide[:, step : span - step]
        wide = advance(wide, kappa_now, steep)
        row_ids = first_row + step + 1 + jnp.arange(wide.shape[1], dtype=jnp.int32)
        inside = (row_ids >= 0) & (row_ids < total_rows)
        wide = jnp.where(inside[None, :, None], wide, 0.0)
        snapshot = jnp.where(pick_here == step + 1, wide[:, margin : margin + rows], snapshot)
    flat = snapshot.reshape(local_runs, rows * columns)
    target = core_and_chips(flat, ("grp_0", "grp_1"), (0, 1), 1, 0)
    runs_total = target.shape[0]
    feats = features(run_levels, step_pick, steepness)
    pre = jnp.dot(feats, input_layer, precision=lax.Precision.HIGHEST)
    hidden = jax.nn.silu(pre).astype(jnp.bfloat16)
    error = (
        jnp.dot(hidden, output_layer, preferred_element_type=jnp.float32)
        + output_bias[None, :]
        - target
    )
    slope = (error * (2.0 / runs_total)).astype(jnp.bfloat16)
    grad = lax.dot_general(
        hidden, slope, (((0,), (0,)), ((), ())), preferred_element_type=jnp.float32
    )
    output_next = (output_layer.astype(jnp.float32) - 0.5 * grad).astype(jnp.bfloat16)
    bias_next = output_bias - 0.5 * jnp.sum(slope.astype(jnp.float32), axis=0)
    gain_slope = dsilu(pre)
    partial_back = lax.dot_general(
        slope, output_layer, (((1,), (1,)), ((), ())), preferred_element_type=jnp.float32
    )
    partial_in = lax.dot_general(
        feats, partial_back * gain_slope, (((0,), (0,)), ((), ())), precision=lax.Precision.HIGHEST
    )
    grad_in = lax.psum(partial_in, GRP_TILE)
    input_next = input_layer - 2.0 * grad_in
    return (error.astype(jnp.bfloat16), output_next, bias_next, input_next)


def solution(mesh):
    split = Mesh(mesh.devices.reshape(2, 2, mesh.shape["tile"]), ("grp_0", "grp_1", "tile"))
    return jax.shard_map(
        on_device,
        mesh=split,
        in_specs=(
            P(GRP, "tile", None),
            P("tile", None),
            P(),
            P(),
            P(),
            P(),
            P(None, GRP_TILE),
            P(GRP_TILE),
        ),
        out_specs=(P(None, GRP_TILE), P(None, GRP_TILE), P(GRP_TILE), P()),
        check_vma=False,
    )
```

```python
import functools

import jax
import jax.numpy as jnp
from jax import lax
from jax.experimental import pallas as pl
from jax.experimental.pallas import tpu as pltpu
from jax.sharding import Mesh
from jax.sharding import PartitionSpec as P

STEPS = 4
LEVELS = 8
CLASSES = 8
AXES = ("xh", "core", "xl", "y", "z")
GRP = ("xh", "core")
TILE = ("xl", "y", "z")
BY_ID = pl.DeviceIdType.MESH
MIB = 2**20
CHUNKS = 8
SUB = 8


def place():
    return {axis: lax.axis_index(axis) for axis in AXES}


def at(here, **moved):
    return tuple(moved.get(axis, here[axis]) for axis in AXES)


def beside(here, step):
    tile = here["xl"] * 16 + here["y"] * 4 + here["z"] + step
    tile = (tile + 32) % 32
    return at(here, xl=tile // 16, y=(tile // 4) % 4, z=tile % 4)


def solve_kernel(
    field_ref, class_ref, table_ref, steep_ref, pick_ref, target_ref,
    raw, rows_own, halo_up, halo_dn, class_up, class_dn, kappa, wide_a, wide_b, sent, got,
    load_sem, halo_send, halo_recv, class_send, class_recv, out_send, out_recv, keep_sem,
):
    here = place()
    runs = rows_own.shape[1]
    tile_rows = rows_own.shape[0]
    width = rows_own.shape[2]
    part = runs // CHUNKS
    tile = here["xl"] * 16 + here["y"] * 4 + here["z"]
    group = here["xh"] * 2 + here["core"]
    up, dn = beside(here, -1), beside(here, 1)
    has_up, has_dn = tile > 0, tile < 31
    mates = (
        (here["xh"] * 2 + 1 - here["core"], at(here, core=1 - here["core"])),
        ((1 - here["xh"]) * 2 + here["core"], at(here, xh=1 - here["xh"])),
        ((1 - here["xh"]) * 2 + 1 - here["core"], at(here, xh=1 - here["xh"], core=1 - here["core"])),
    )

    def load(k):
        lines = part * tile_rows
        return [
            pltpu.make_async_copy(
                field_ref.at[pl.ds(k * lines, lines), pl.ds(128 * c, 128)],
                raw.at[c, pl.ds(k * lines, lines)],
                load_sem.at[k, c],
            )
            for c in range(width // 128)
        ]

    for k in range(CHUNKS):
        for copy in load(k):
            copy.start()

    barrier = pltpu.get_barrier_semaphore()
    for _, mate in mates:
        pl.semaphore_signal(barrier, inc=1, device_id=mate, device_id_type=BY_ID)

    @pl.when(has_up)
    def _():
        pl.semaphore_signal(barrier, inc=1, device_id=up, device_id_type=BY_ID)

    @pl.when(has_dn)
    def _():
        pl.semaphore_signal(barrier, inc=1, device_id=dn, device_id_type=BY_ID)

    callers = 3 + jnp.where(has_up, 1, 0) + jnp.where(has_dn, 1, 0)
    pl.semaphore_wait(barrier, callers)

    def class_copy(upward):
        return pltpu.make_async_remote_copy(
            src_ref=class_ref.at[pl.ds(0 if upward else tile_rows - STEPS, STEPS)],
            dst_ref=class_dn if upward else class_up,
            send_sem=class_send.at[0 if upward else 1],
            recv_sem=class_recv.at[0 if upward else 1],
            device_id=up if upward else dn,
            device_id_type=BY_ID,
        )

    def halo_copy(k, upward):
        span = pl.ds(pl.multiple_of(k * part, part), part)
        return pltpu.make_async_remote_copy(
            src_ref=rows_own.at[pl.ds(0 if upward else tile_rows - STEPS, STEPS), span],
            dst_ref=(halo_dn if upward else halo_up).at[:, span],
            send_sem=halo_send.at[k, 0 if upward else 1],
            recv_sem=halo_recv.at[k, 0 if upward else 1],
            device_id=up if upward else dn,
            device_id_type=BY_ID,
        )

    def out_copy(k, j):
        span = pl.ds(pl.multiple_of(k * part, part), part)
        owner, mate = mates[j]
        return pltpu.make_async_remote_copy(
            src_ref=sent.at[owner, span],
            dst_ref=got.at[j, span],
            send_sem=out_send.at[k, j],
            recv_sem=out_recv.at[k, j],
            device_id=mate,
            device_id_type=BY_ID,
        )

    @pl.when(has_up)
    def _():
        class_copy(True).start()

    @pl.when(has_dn)
    def _():
        class_copy(False).start()

    @pl.when(jnp.logical_not(has_up))
    def _():
        halo_up[...] = jnp.zeros_like(halo_up)
        class_up[...] = jnp.full_like(class_up, -1)

    @pl.when(jnp.logical_not(has_dn))
    def _():
        halo_dn[...] = jnp.zeros_like(halo_dn)
        class_dn[...] = jnp.full_like(class_dn, -1)

    for k in range(CHUNKS):
        for copy in load(k):
            copy.wait()

        def turn(j, carry):
            first = pl.multiple_of(j * SUB, SUB)
            for i in range(tile_rows):
                for c in range(width // 128):
                    rows_own[i, pl.ds(first, SUB), pl.ds(128 * c, 128)] = raw[
                        c, pl.ds(j * (SUB * tile_rows) + i, SUB, stride=tile_rows), :
                    ]
            return carry

        lax.fori_loop(k * part // SUB, (k + 1) * part // SUB, turn, 0)

        @pl.when(has_up)
        def _():
            halo_copy(k, True).start()

        @pl.when(has_dn)
        def _():
            halo_copy(k, False).start()

    @pl.when(has_up)
    def _():
        class_copy(False).wait_recv()

    @pl.when(has_dn)
    def _():
        class_copy(True).wait_recv()

    keep_up = jnp.where(has_up, 1.0, 0.0).astype(jnp.float32)
    keep_dn = jnp.where(has_dn, 1.0, 0.0).astype(jnp.float32)
    lane = lax.broadcasted_iota(jnp.int32, (SUB, width), 1)
    left, right = lane == 0, lane == width - 1
    span_rows = tile_rows + 2 * STEPS

    def advance(s, carry):
        first = pl.multiple_of(s * SUB, SUB)
        runs_here = pl.ds(first, SUB)
        steep = jnp.broadcast_to(steep_ref[runs_here, 0:1], (SUB, width))
        rest = 1.0 - steep
        pick = jnp.broadcast_to(pick_ref[runs_here, 0:1], (SUB, width))
        half = [
            jnp.broadcast_to(table_ref[runs_here, c : c + 1], (SUB, width)) for c in range(CLASSES)
        ]
        for i in range(span_rows):
            if i < STEPS:
                klass = class_up[i]
            elif i < STEPS + tile_rows:
                klass = class_ref[i - STEPS]
            else:
                klass = class_dn[i - STEPS - tile_rows]
            value = jnp.zeros((SUB, width), jnp.float32)
            for c in range(CLASSES):
                value = jnp.where(klass == c, half[c], value)
            kappa[i] = value

        def start_row(i):
            if i < STEPS:
                return halo_up[i, runs_here]
            if i < STEPS + tile_rows:
                return rows_own[i - STEPS, runs_here]
            return halo_dn[i - STEPS - tile_rows, runs_here]

        for step in range(STEPS):
            source = (None, wide_a, wide_b, wide_a)[step]
            sink = (wide_a, wide_b, wide_a, None)[step]

            def row(i):
                return start_row(i) if step == 0 else source[i]

            def spread_of(i, value):
                bottom = 1.0 + value * value
                guess = pl.reciprocal(bottom, approx=True)
                guess = guess * (2.0 - bottom * guess)
                return kappa[i] * (steep + rest * guess)

            above = row(step)
            above_spread = spread_of(step, above)
            centre = row(step + 1)
            spread = spread_of(step + 1, centre)
            flow_in = (above_spread + spread) * (centre - above)
            for i in range(step + 1, span_rows - step - 1):
                below = row(i + 1)
                below_spread = spread_of(i + 1, below)
                flow_out = (spread + below_spread) * (below - centre)
                beyond = jnp.where(right, 0.0, pltpu.roll(centre, width - 1, 1))
                beyond_spread = jnp.where(right, 0.0, pltpu.roll(spread, width - 1, 1))
                flow = (spread + beyond_spread) * (beyond - centre)
                back = jnp.where(left, spread * centre, pltpu.roll(flow, 1, 1))
                total = centre + (flow_out - flow_in) + (flow - back)
                if i < STEPS:
                    total = total * keep_up
                if i >= STEPS + tile_rows:
                    total = total * keep_dn
                if sink is not None:
                    sink[i] = total
                if STEPS <= i < STEPS + tile_rows:
                    owner, inner = (i - STEPS) // 4, (i - STEPS) % 4
                    columns = pl.ds(inner * width, width)
                    if step > 0:
                        total = jnp.where(pick == step + 1, total, sent[owner, runs_here, columns])
                    sent[owner, runs_here, columns] = total
                flow_in, centre, spread = flow_out, below, below_spread
        return carry

    for k in range(CHUNKS):
        @pl.when(has_up)
        def _():
            halo_copy(k, False).wait_recv()

        @pl.when(has_dn)
        def _():
            halo_copy(k, True).wait_recv()

        lax.fori_loop(k * part // SUB, (k + 1) * part // SUB, advance, 0)
        for j in range(3):
            out_copy(k, j).start()

    def keep(j):
        if j == 3:
            source, owner = sent.at[group], group
        else:
            source, owner = got.at[j], mates[j][0]
        return pltpu.make_async_copy(
            source, target_ref.at[pl.ds(pl.multiple_of(owner * runs, runs), runs)], keep_sem.at[j]
        )

    keep(3).start()
    for j in range(3):
        for k in range(CHUNKS):
            out_copy(k, j).wait_recv()
        keep(j).start()
    for j in range(4):
        keep(j).wait()
    for k in range(CHUNKS):
        for j in range(3):
            out_copy(k, j).wait_send()

    @pl.when(has_up)
    def _():
        class_copy(True).wait_send()
        for k in range(CHUNKS):
            halo_copy(k, True).wait_send()

    @pl.when(has_dn)
    def _():
        class_copy(False).wait_send()
        for k in range(CHUNKS):
            halo_copy(k, False).wait_send()


def solve(field, classes, table, steep, pick):
    runs, rows, width = field.shape
    f32 = jnp.float32
    dma = pltpu.SemaphoreType.DMA
    vmem = pl.BlockSpec(memory_space=pltpu.VMEM)
    anywhere = pl.BlockSpec(memory_space=pl.ANY)
    wide = jnp.broadcast_to(classes[:, None, :], (rows, SUB, width))
    return pl.pallas_call(
        solve_kernel,
        out_shape=jax.ShapeDtypeStruct((4 * runs, 4 * width), f32),
        in_specs=[anywhere, vmem, vmem, vmem, vmem],
        out_specs=anywhere,
        scratch_shapes=[
            pltpu.VMEM((width // 128, runs * rows, 128), f32),
            pltpu.VMEM((rows, runs, width), f32),
            pltpu.VMEM((STEPS, runs, width), f32),
            pltpu.VMEM((STEPS, runs, width), f32),
            pltpu.VMEM((STEPS, SUB, width), jnp.int32),
            pltpu.VMEM((STEPS, SUB, width), jnp.int32),
            pltpu.VMEM((rows + 2 * STEPS, SUB, width), f32),
            pltpu.VMEM((rows + 2 * STEPS, SUB, width), f32),
            pltpu.VMEM((rows + 2 * STEPS, SUB, width), f32),
            pltpu.VMEM((4, runs, 4 * width), f32),
            pltpu.VMEM((3, runs, 4 * width), f32),
            dma((CHUNKS, 4)),
            dma((CHUNKS, 2)),
            dma((CHUNKS, 2)),
            dma((2,)),
            dma((2,)),
            dma((CHUNKS, 3)),
            dma((CHUNKS, 3)),
            dma((4,)),
        ],
        compiler_params=pltpu.CompilerParams(
            collective_id=1, has_side_effects=True, vmem_limit_bytes=48 * MIB
        ),
        name="solve",
    )(field.reshape(runs * rows, width), wide, table, steep, pick)


def sum_kernel(
    part_ref, out_ref, pair, own, landed, mine,
    pair_send, pair_recv, part_send, part_recv, back_send, back_recv, last_send, last_recv,
):
    here = place()
    core = here["core"]
    chips = own.shape[0]
    chip = here["xh"] * 32 + here["xl"] * 16 + here["y"] * 4 + here["z"]
    mate = at(here, core=1 - core)

    def device(k):
        return (k // 32, core, (k // 16) % 2, (k // 4) % 4, k % 4)

    barrier = pltpu.get_barrier_semaphore()
    pl.semaphore_signal(barrier, inc=1, device_id=mate, device_id_type=BY_ID)

    def greet(j, carry):
        pl.semaphore_signal(
            barrier, inc=1, device_id=device((chip + j) % chips), device_id_type=BY_ID
        )
        return carry

    lax.fori_loop(1, chips, greet, 0)
    pl.semaphore_wait(barrier, chips)

    swap = pltpu.make_async_remote_copy(
        src_ref=part_ref.at[pl.ds((1 - core) * chips, chips)],
        dst_ref=pair,
        send_sem=pair_send,
        recv_sem=pair_recv,
        device_id=mate,
        device_id_type=BY_ID,
    )
    swap.start()
    swap.wait_recv()
    own[...] = part_ref[pl.ds(core * chips, chips)] + pair[...]

    def scatter(j, carry):
        other = (chip + j) % chips
        pltpu.make_async_remote_copy(
            src_ref=own.at[other],
            dst_ref=landed.at[j - 1],
            send_sem=part_send,
            recv_sem=part_recv,
            device_id=device(other),
            device_id_type=BY_ID,
        ).start()
        return carry

    lax.fori_loop(1, chips, scatter, 0)
    total = own[chip]
    whole = pltpu.make_async_remote_copy(
        src_ref=own.at[pl.ds(0, chips - 1)],
        dst_ref=landed,
        send_sem=part_send,
        recv_sem=part_recv,
        device_id=mate,
        device_id_type=BY_ID,
    )
    whole.wait_recv()
    mine[...] = total + jnp.sum(landed[...], axis=0)

    slot = core * chips + chip
    out_ref[slot] = mine[...]

    def spread(j, carry):
        pltpu.make_async_remote_copy(
            src_ref=mine,
            dst_ref=out_ref.at[slot],
            send_sem=back_send,
            recv_sem=back_recv,
            device_id=device((chip + j) % chips),
            device_id_type=BY_ID,
        ).start()
        return carry

    lax.fori_loop(1, chips, spread, 0)
    gathered = pltpu.make_async_remote_copy(
        src_ref=own.at[pl.ds(0, chips - 1)],
        dst_ref=landed,
        send_sem=back_send,
        recv_sem=back_recv,
        device_id=mate,
        device_id_type=BY_ID,
    )
    gathered.wait_recv()
    half = pl.ds(core * chips, chips)
    last = pltpu.make_async_remote_copy(
        src_ref=out_ref.at[half],
        dst_ref=out_ref.at[half],
        send_sem=last_send,
        recv_sem=last_recv,
        device_id=mate,
        device_id_type=BY_ID,
    )
    last.start()
    last.wait()
    swap.wait_send()
    whole.wait_send()
    gathered.wait_send()


def sum_everywhere(part):
    tiles = part.shape[0]
    f32 = jnp.float32
    dma = pltpu.SemaphoreType.DMA
    vmem = pl.BlockSpec(memory_space=pltpu.VMEM)
    tile = part.shape[1:]
    return pl.pallas_call(
        sum_kernel,
        out_shape=jax.ShapeDtypeStruct(part.shape, f32),
        in_specs=[vmem],
        out_specs=vmem,
        scratch_shapes=[
            pltpu.VMEM((tiles // 2,) + tile, f32),
            pltpu.VMEM((tiles // 2,) + tile, f32),
            pltpu.VMEM((tiles // 2 - 1,) + tile, f32),
            pltpu.VMEM(tile, f32),
        ] + [dma] * 8,
        compiler_params=pltpu.CompilerParams(
            collective_id=2, has_side_effects=True, vmem_limit_bytes=16 * MIB
        ),
        name="sum_everywhere",
    )(part)


def features(run_levels, step_pick, steepness):
    count = run_levels.shape[0]
    onehot = (run_levels[:, :, None] == jnp.arange(LEVELS, dtype=jnp.int32)[None, None, :]).astype(
        jnp.float32
    )
    onehot = onehot.reshape(count, -1)
    moment = (step_pick[:, None] == jnp.arange(1, STEPS + 1, dtype=jnp.int32)[None, :]).astype(
        jnp.float32
    )
    return jnp.concatenate([onehot, moment, steepness[:, None]], axis=1)


def independent(run_levels, step_pick, steepness):
    count = run_levels.shape[0]
    f32 = jnp.float32
    onehot = (run_levels[:, :, None] == jnp.arange(LEVELS - 1, dtype=jnp.int32)).astype(f32)
    moment = (step_pick[:, None] == jnp.arange(1, STEPS, dtype=jnp.int32)).astype(f32)
    return jnp.concatenate(
        [
            onehot.reshape(count, -1),
            moment,
            steepness[:, None],
            jnp.ones((count, 1), f32),
            jnp.zeros((count, 3), f32),
        ],
        axis=1,
    )


def all_features(sums):
    width = sums.shape[1]
    classes = sums[: CLASSES * (LEVELS - 1)].reshape(CLASSES, LEVELS - 1, width)
    first = CLASSES * (LEVELS - 1)
    moment = sums[first : first + STEPS - 1]
    steep = sums[first + STEPS - 1 : first + STEPS]
    ones = sums[first + STEPS : first + STEPS + 1]
    last = ones[None] - jnp.sum(classes, axis=1, keepdims=True)
    classes = jnp.concatenate([classes, last], axis=1).reshape(CLASSES * LEVELS, width)
    final = ones - jnp.sum(moment, axis=0, keepdims=True)
    return jnp.concatenate([classes, moment, final, steep], axis=0)


def dsilu(pre):
    logistic = jax.nn.sigmoid(pre)
    return logistic * (1.0 + pre * (1.0 - logistic))


def on_device(
    start_field, class_ids, run_levels, steepness, step_pick, input_layer, output_layer, output_bias
):
    local_runs = start_field.shape[0]
    first_run = lax.axis_index(GRP) * local_runs
    levels_here = lax.dynamic_slice_in_dim(run_levels, first_run, local_runs, 0)
    steep = lax.dynamic_slice_in_dim(steepness, first_run, local_runs, 0)[:, None]
    pick_here = lax.dynamic_slice_in_dim(step_pick, first_run, local_runs, 0)[:, None]
    table = 0.015 * jnp.exp(levels_here.astype(jnp.float32) * jnp.log(jnp.float32(1.35)))
    target = solve(start_field, class_ids, table, steep, pick_here)
    runs_total = target.shape[0]
    feats = features(run_levels, step_pick, steepness)
    pre = jnp.dot(feats, input_layer, precision=lax.Precision.HIGHEST)
    hidden = jax.nn.silu(pre).astype(jnp.bfloat16)
    error = (
        jnp.dot(hidden, output_layer, preferred_element_type=jnp.float32)
        + output_bias[None, :]
        - target
    )
    slope = (error * (2.0 / runs_total)).astype(jnp.bfloat16)
    grad = lax.dot_general(
        hidden, slope, (((0,), (0,)), ((), ())), preferred_element_type=jnp.float32
    )
    output_next = (output_layer.astype(jnp.float32) - 0.5 * grad).astype(jnp.bfloat16)
    bias_next = output_bias - 0.5 * jnp.sum(slope.astype(jnp.float32), axis=0)
    gain_slope = dsilu(pre)
    partial_back = lax.dot_general(
        slope, output_layer, (((1,), (1,)), ((), ())), preferred_element_type=jnp.float32
    )
    basis = independent(run_levels, step_pick, steepness)
    partial_in = lax.dot_general(
        basis, partial_back * gain_slope, (((0,), (0,)), ((), ())), precision=lax.Precision.HIGHEST
    )
    width = partial_in.shape[1]
    tiles = partial_in.reshape(8, 8, width // 128, 128).transpose(0, 2, 1, 3).reshape(-1, 8, 128)
    tiles = sum_everywhere(tiles)
    sums = tiles.reshape(8, width // 128, 8, 128).transpose(0, 2, 1, 3).reshape(64, width)
    input_next = input_layer - 2.0 * all_features(sums)
    return (error.astype(jnp.bfloat16), output_next, bias_next, input_next)


def solution(mesh):
    split = Mesh(mesh.devices.reshape(2, 2, 2, 4, 4), AXES)
    return jax.shard_map(
        on_device,
        mesh=split,
        in_specs=(
            P(GRP, TILE, None),
            P(TILE, None),
            P(),
            P(),
            P(),
            P(),
            P(None, GRP + TILE),
            P(GRP + TILE),
        ),
        out_specs=(P(None, GRP + TILE), P(None, GRP + TILE), P(GRP + TILE), P()),
        check_vma=False,
    )
```

```python
import functools

import jax
import jax.numpy as jnp
from jax import lax
from jax.experimental import pallas as pl
from jax.experimental.pallas import tpu as pltpu
from jax.sharding import Mesh
from jax.sharding import PartitionSpec as P

STEPS = 4
LEVELS = 8
CLASSES = 8
AXES = ("xh", "core", "xl", "y", "z")
GRP = ("xh", "core")
TILE = ("xl", "y", "z")
BY_ID = pl.DeviceIdType.MESH
MIB = 2**20
CHUNKS = 8
SUB = 8


def place():
    return {axis: lax.axis_index(axis) for axis in AXES}


def at(here, **moved):
    return tuple(moved.get(axis, here[axis]) for axis in AXES)


def beside(here, step):
    tile = here["xl"] * 16 + here["y"] * 4 + here["z"] + step
    tile = (tile + 32) % 32
    return at(here, xl=tile // 16, y=(tile // 4) % 4, z=tile % 4)


def dot(a, b):
    return lax.dot_general(a, b, (((1,), (0,)), ((), ())), preferred_element_type=jnp.float32)


def dot_turned(a, b):
    return lax.dot_general(a, b, (((1,), (1,)), ((), ())), preferred_element_type=jnp.float32)


def two_parts(x):
    high = x.astype(jnp.bfloat16)
    return high, (x - high.astype(jnp.float32)).astype(jnp.bfloat16)


def dot_parts(x, order):
    high, low = two_parts(x)
    return dot(high, order) + dot(low, order)


def solve_kernel(
    field_ref, class_ref, table_ref, steep_ref, pick_ref,
    onehot_ref, steep_all_ref, input_ref, near_ref, far_ref, bias_ref, weight_ref,
    misfit_ref, turned_ref, part_ref,
    raw, rows_own, halo_up, halo_dn, class_up, class_dn, kappa, wide_a, wide_b, picked, sent, got,
    weight, hidden, turned, gain, pred, misfit, misfit_far, grad,
    load_sem, halo_send, halo_recv, class_send, class_recv, out_send, out_recv, keep_sem, weight_sem,
):
    here = place()
    runs = rows_own.shape[1]
    tile_rows = rows_own.shape[0]
    width = rows_own.shape[2]
    part = runs // CHUNKS
    tile = here["xl"] * 16 + here["y"] * 4 + here["z"]
    group = here["xh"] * 2 + here["core"]
    up, dn = beside(here, -1), beside(here, 1)
    has_up, has_dn = tile > 0, tile < 31
    mates = (
        (here["xh"] * 2 + 1 - here["core"], at(here, core=1 - here["core"])),
        ((1 - here["xh"]) * 2 + here["core"], at(here, xh=1 - here["xh"])),
        ((1 - here["xh"]) * 2 + 1 - here["core"], at(here, xh=1 - here["xh"], core=1 - here["core"])),
    )

    def load(k):
        lines = part * tile_rows
        return [
            pltpu.make_async_copy(
                field_ref.at[pl.ds(k * lines, lines), pl.ds(128 * c, 128)],
                raw.at[c, pl.ds(k * lines, lines)],
                load_sem.at[k, c],
            )
            for c in range(width // 128)
        ]

    for k in range(CHUNKS):
        for copy in load(k):
            copy.start()
    weight_load = pltpu.make_async_copy(weight_ref, weight, weight_sem)
    weight_load.start()

    barrier = pltpu.get_barrier_semaphore()
    for _, mate in mates:
        pl.semaphore_signal(barrier, inc=1, device_id=mate, device_id_type=BY_ID)

    @pl.when(has_up)
    def _():
        pl.semaphore_signal(barrier, inc=1, device_id=up, device_id_type=BY_ID)

    @pl.when(has_dn)
    def _():
        pl.semaphore_signal(barrier, inc=1, device_id=dn, device_id_type=BY_ID)

    callers = 3 + jnp.where(has_up, 1, 0) + jnp.where(has_dn, 1, 0)
    pl.semaphore_wait(barrier, callers)

    def class_copy(upward):
        return pltpu.make_async_remote_copy(
            src_ref=class_ref.at[pl.ds(0 if upward else tile_rows - STEPS, STEPS)],
            dst_ref=class_dn if upward else class_up,
            send_sem=class_send.at[0 if upward else 1],
            recv_sem=class_recv.at[0 if upward else 1],
            device_id=up if upward else dn,
            device_id_type=BY_ID,
        )

    def halo_copy(k, upward):
        span = pl.ds(pl.multiple_of(k * part, part), part)
        return pltpu.make_async_remote_copy(
            src_ref=rows_own.at[pl.ds(0 if upward else tile_rows - STEPS, STEPS), span],
            dst_ref=(halo_dn if upward else halo_up).at[:, span],
            send_sem=halo_send.at[k, 0 if upward else 1],
            recv_sem=halo_recv.at[k, 0 if upward else 1],
            device_id=up if upward else dn,
            device_id_type=BY_ID,
        )

    def out_copy(k, j):
        span = pl.ds(pl.multiple_of(k * part, part), part)
        owner, mate = mates[j]
        return pltpu.make_async_remote_copy(
            src_ref=sent.at[owner, span],
            dst_ref=got.at[j, span],
            send_sem=out_send.at[k, j],
            recv_sem=out_recv.at[k, j],
            device_id=mate,
            device_id_type=BY_ID,
        )

    @pl.when(has_up)
    def _():
        class_copy(True).start()

    @pl.when(has_dn)
    def _():
        class_copy(False).start()

    @pl.when(jnp.logical_not(has_up))
    def _():
        halo_up[...] = jnp.zeros_like(halo_up)
        class_up[...] = jnp.full_like(class_up, -1)

    @pl.when(jnp.logical_not(has_dn))
    def _():
        halo_dn[...] = jnp.zeros_like(halo_dn)
        class_dn[...] = jnp.full_like(class_dn, -1)

    first = lax.broadcasted_iota(jnp.int32, (width, width), 0)
    second = lax.broadcasted_iota(jnp.int32, (width, width), 1)
    blocks = width // 128
    order = jnp.where(first == (second % 128) * blocks + second // 128, 1.0, 0.0)
    order = order.astype(jnp.bfloat16)
    lines = part * tile_rows

    def prepare(k, none):
        for copy in load(k):
            copy.wait()
        span = pl.ds(pl.multiple_of(k * lines, lines), lines)
        lined = jnp.concatenate([raw[c, span] for c in range(blocks)], axis=1)
        lined = dot_parts(lined, order)
        for c in range(blocks):
            raw[c, span] = lined[:, 128 * c : 128 * c + 128]

        def turn(j, carry):
            first = pl.multiple_of(j * SUB, SUB)
            for i in range(tile_rows):
                for c in range(blocks):
                    rows_own[i, pl.ds(first, SUB), pl.ds(128 * c, 128)] = raw[
                        c, pl.ds(j * (SUB * tile_rows) + i, SUB, stride=tile_rows), :
                    ]
            return carry

        lax.fori_loop(k * (part // SUB), (k + 1) * (part // SUB), turn, 0)

        @pl.when(has_up)
        def _():
            halo_copy(k, True).start()

        @pl.when(has_dn)
        def _():
            halo_copy(k, False).start()

        return none

    lax.fori_loop(0, CHUNKS, prepare, 0)

    @pl.when(has_up)
    def _():
        class_copy(False).wait_recv()

    @pl.when(has_dn)
    def _():
        class_copy(True).wait_recv()

    keep_up = jnp.where(has_up, 1.0, 0.0).astype(jnp.float32)
    keep_dn = jnp.where(has_dn, 1.0, 0.0).astype(jnp.float32)
    lane = lax.broadcasted_iota(jnp.int32, (SUB, 128), 1)
    left, right = lane == 0, lane == 127
    edge = width - 128

    def next_column(x):
        turned = jnp.where(right, 0.0, pltpu.roll(x[:, :128], 127, 1))
        return jnp.concatenate([x[:, 128:], turned], axis=1)

    def last_column(x, outermost):
        turned = jnp.where(left, outermost[:, :128], pltpu.roll(x[:, edge:], 1, 1))
        return jnp.concatenate([turned, x[:, :edge]], axis=1)

    span_rows = tile_rows + 2 * STEPS

    def advance(k, half_chunk):
        first = pl.multiple_of(k * part + half_chunk * SUB, SUB)
        runs_here = pl.ds(first, SUB)
        picked_here = pl.ds(pl.multiple_of(half_chunk * SUB, SUB), SUB)
        steep = jnp.broadcast_to(steep_ref[runs_here, 0:1], (SUB, width))
        rest = 1.0 - steep
        pick = jnp.broadcast_to(pick_ref[runs_here, 0:1], (SUB, width))
        half = [
            jnp.broadcast_to(table_ref[runs_here, c : c + 1], (SUB, width)) for c in range(CLASSES)
        ]
        for i in range(span_rows):
            if i < STEPS:
                klass = class_up[i]
            elif i < STEPS + tile_rows:
                klass = class_ref[i - STEPS]
            else:
                klass = class_dn[i - STEPS - tile_rows]
            value = jnp.zeros((SUB, width), jnp.float32)
            for c in range(CLASSES):
                value = jnp.where(klass == c, half[c], value)
            kappa[i] = value

        def start_row(i):
            if i < STEPS:
                return halo_up[i, runs_here]
            if i < STEPS + tile_rows:
                return rows_own[i - STEPS, runs_here]
            return halo_dn[i - STEPS - tile_rows, runs_here]

        for step in range(STEPS):
            source = (None, wide_a, wide_b, wide_a)[step]
            sink = (wide_a, wide_b, wide_a, None)[step]

            def row(i):
                return start_row(i) if step == 0 else source[i]

            def spread_of(i, value):
                bottom = 1.0 + value * value
                guess = pl.reciprocal(bottom, approx=True)
                guess = guess * (2.0 - bottom * guess)
                return kappa[i] * (steep + rest * guess)

            above = row(step)
            above_spread = spread_of(step, above)
            centre = row(step + 1)
            spread = spread_of(step + 1, centre)
            flow_in = (above_spread + spread) * (centre - above)
            for i in range(step + 1, span_rows - step - 1):
                below = row(i + 1)
                below_spread = spread_of(i + 1, below)
                flow_out = (spread + below_spread) * (below - centre)
                flow = (spread + next_column(spread)) * (next_column(centre) - centre)
                back = last_column(flow, spread * centre)
                total = centre + (flow_out - flow_in) + (flow - back)
                if i < STEPS:
                    total = total * keep_up
                if i >= STEPS + tile_rows:
                    total = total * keep_dn
                if sink is not None:
                    sink[i] = total
                if STEPS <= i < STEPS + tile_rows:
                    if step > 0:
                        total = jnp.where(pick == step + 1, total, picked[i - STEPS, picked_here])
                    picked[i - STEPS, picked_here] = total
                flow_in, centre, spread = flow_out, below, below_spread

    back_order = jnp.where(second == (first % 128) * blocks + first // 128, 1.0, 0.0)
    back_order = back_order.astype(jnp.bfloat16)

    def one_chunk(k, none):
        @pl.when(has_up)
        def _():
            halo_copy(k, False).wait_recv()

        @pl.when(has_dn)
        def _():
            halo_copy(k, True).wait_recv()

        def half_of(half_chunk, carry):
            advance(k, half_chunk)
            return carry

        lax.fori_loop(0, part // SUB, half_of, 0)
        lined = dot_parts(picked[...].reshape(tile_rows * part, width), back_order)
        span = pl.ds(pl.multiple_of(k * part, part), part)
        for i in range(tile_rows):
            sent[i // 4, span, pl.ds((i % 4) * width, width)] = lined[i * part : (i + 1) * part]
        for j in range(3):
            out_copy(k, j).start()
        return none

    lax.fori_loop(0, CHUNKS, one_chunk, 0)

    cells = weight.shape[1]
    hid = weight.shape[0]
    all_runs = hidden.shape[0]
    block = 256
    f32, bf16 = jnp.float32, jnp.bfloat16
    eye = lax.broadcasted_iota(jnp.int32, (block, block), 0) == lax.broadcasted_iota(
        jnp.int32, (block, block), 1
    )
    eye = jnp.where(eye, 1.0, 0.0).astype(bf16)
    share = 2.0 / all_runs

    def hidden_block(n, none):
        span = pl.ds(pl.multiple_of(n * block, block), block)
        value = input_ref[:, span]
        high, low = two_parts(value)
        rest = (value - high.astype(f32) - low.astype(f32)).astype(bf16)
        onehot = onehot_ref[...]
        pre = dot(onehot, high) + (dot(onehot, low) + dot(onehot, rest))
        pre = pre + steep_all_ref[...] * value[value.shape[0] - 1 :, :]
        logistic = 1.0 / (1.0 + jnp.exp(-pre))
        active = (pre * logistic).astype(bf16)
        hidden[:, span] = active
        gain[:, span] = logistic * (1.0 + pre * (1.0 - logistic)) * share
        turned[span, :] = dot_turned(eye, active).astype(bf16)
        return none

    lax.fori_loop(0, hid // block, hidden_block, 0)
    turned_copy = pltpu.make_async_copy(turned, turned_ref, keep_sem.at[0])
    turned_copy.start()
    weight_load.wait()

    def pred_block(n, none):
        span = pl.ds(pl.multiple_of(n * block, block), block)
        pred[:, span] = dot(hidden[...], weight[:, span]) + bias_ref[:, span]
        return none

    lax.fori_loop(0, cells // block, pred_block, 0)

    def compare(source, group_at, start, count, copy_row):
        def some(b, none):
            inner = pl.multiple_of(start + b * 16, 16)
            at_run = pl.ds(pl.multiple_of(group_at * runs + inner, 16), 16)
            value = (pred[at_run] - source[pl.ds(inner, 16)]).astype(bf16)
            misfit[at_run] = value
            if copy_row is not None:
                misfit_far[pl.ds(pl.multiple_of(copy_row + b * 16, 16), 16)] = value
            return none

        lax.fori_loop(0, count // 16, some, 0)

    for k in range(CHUNKS):
        out_copy(k, 0).wait_recv()
    compare(sent.at[group], group, 0, runs, None)
    compare(got.at[0], mates[0][0], 0, runs, None)
    near = pl.ds(pl.multiple_of(here["xh"] * (2 * runs), 2 * runs), 2 * runs)
    far = (1 - here["xh"]) * (2 * runs)

    def near_block(n, none):
        span = pl.ds(pl.multiple_of(n * block, block), block)
        back = dot_turned(misfit[near], weight[span, :]) * gain[near, span]
        high, low = two_parts(back)
        grad[:, span] = dot(near_ref[here["xh"]], high) + dot(near_ref[here["xh"]], low)
        return none

    lax.fori_loop(0, hid // block, near_block, 0)
    near_copy = pltpu.make_async_copy(misfit.at[near], misfit_ref.at[near], keep_sem.at[1])
    near_copy.start()

    half = runs // 2
    for h in range(2):
        for k in range(h * CHUNKS // 2, (h + 1) * CHUNKS // 2):
            out_copy(k, 1).wait_recv()
            out_copy(k, 2).wait_recv()
        for j in (1, 2):
            at_row = here["core"] if j == 1 else 1 - here["core"]
            compare(got.at[j], mates[j][0], h * half, half, at_row * half)

        def far_block(n, none):
            span = pl.ds(pl.multiple_of(n * block, block), block)
            factor = jnp.concatenate(
                [
                    gain[pl.ds(pl.multiple_of(far + g * runs + h * half, half), half), span]
                    for g in range(2)
                ],
                axis=0,
            )
            back = dot_turned(misfit_far[...], weight[span, :]) * factor
            high, low = two_parts(back)
            mix = far_ref[1 - here["xh"], h]
            grad[:, span] += dot(mix, high) + dot(mix, low)
            return none

        lax.fori_loop(0, hid // block, far_block, 0)

    far_span = pl.ds(pl.multiple_of(far, 2 * runs), 2 * runs)
    far_copy = pltpu.make_async_copy(misfit.at[far_span], misfit_ref.at[far_span], keep_sem.at[2])
    far_copy.start()
    for i in range(part_ref.shape[0]):
        r, c = i // (hid // 128), i % (hid // 128)
        part_ref[i] = grad[8 * r : 8 * r + 8, 128 * c : 128 * c + 128]
    turned_copy.wait()
    near_copy.wait()
    far_copy.wait()
    for k in range(CHUNKS):
        for j in range(3):
            out_copy(k, j).wait_send()

    @pl.when(has_up)
    def _():
        class_copy(True).wait_send()
        for k in range(CHUNKS):
            halo_copy(k, True).wait_send()

    @pl.when(has_dn)
    def _():
        class_copy(False).wait_send()
        for k in range(CHUNKS):
            halo_copy(k, False).wait_send()


def solve(field, classes, table, steep, pick, onehot, steepness, input_layer, near, far, bias, weight):
    runs, rows, width = field.shape
    hid, cells = weight.shape
    all_runs = onehot.shape[0]
    f32, bf16 = jnp.float32, jnp.bfloat16
    dma = pltpu.SemaphoreType.DMA
    vmem = pl.BlockSpec(memory_space=pltpu.VMEM)
    anywhere = pl.BlockSpec(memory_space=pl.ANY)
    classes = classes.reshape(rows, 128, width // 128).transpose(0, 2, 1).reshape(rows, width)
    wide = jnp.broadcast_to(classes[:, None, :], (rows, SUB, width))
    span = rows + 2 * STEPS
    part = runs // CHUNKS
    return pl.pallas_call(
        solve_kernel,
        out_shape=(
            jax.ShapeDtypeStruct((all_runs, cells), bf16),
            jax.ShapeDtypeStruct((hid, all_runs), bf16),
            jax.ShapeDtypeStruct((hid // 16, 8, 128), f32),
        ),
        in_specs=[anywhere] + [vmem] * 10 + [anywhere],
        out_specs=(anywhere, anywhere, vmem),
        scratch_shapes=[
            pltpu.VMEM((width // 128, runs * rows, 128), f32),
            pltpu.VMEM((rows, runs, width), f32),
            pltpu.VMEM((STEPS, runs, width), f32),
            pltpu.VMEM((STEPS, runs, width), f32),
            pltpu.VMEM((STEPS, SUB, width), jnp.int32),
            pltpu.VMEM((STEPS, SUB, width), jnp.int32),
            pltpu.VMEM((span, SUB, width), f32),
            pltpu.VMEM((span, SUB, width), f32),
            pltpu.VMEM((span, SUB, width), f32),
            pltpu.VMEM((rows, part, width), f32),
            pltpu.VMEM((4, runs, 4 * width), f32),
            pltpu.VMEM((3, runs, 4 * width), f32),
            pltpu.VMEM((hid, cells), bf16),
            pltpu.VMEM((all_runs, hid), bf16),
            pltpu.VMEM((hid, all_runs), bf16),
            pltpu.VMEM((all_runs, hid), f32),
            pltpu.VMEM((all_runs, cells), f32),
            pltpu.VMEM((all_runs, cells), bf16),
            pltpu.VMEM((runs, cells), bf16),
            pltpu.VMEM((64, hid), f32),
            dma((CHUNKS, 4)),
            dma((CHUNKS, 2)),
            dma((CHUNKS, 2)),
            dma((2,)),
            dma((2,)),
            dma((CHUNKS, 3)),
            dma((CHUNKS, 3)),
            dma((3,)),
            dma,
        ],
        compiler_params=pltpu.CompilerParams(
            collective_id=1, has_side_effects=True, vmem_limit_bytes=58 * MIB
        ),
        name="solve",
    )(
        field.reshape(runs * rows, width), wide, table, steep, pick,
        onehot, steepness, input_layer, near, far, bias, weight,
    )


def update_kernel(turned_ref, misfit_ref, weight_ref, bias_ref, next_ref, misfit_out_ref, bias_out_ref):
    f32, bf16 = jnp.float32, jnp.bfloat16
    step = 1.0 / misfit_ref.shape[0]
    block = 256

    def columns(n, none):
        span = pl.ds(pl.multiple_of(n * block, block), block)
        grad = dot(turned_ref[...], misfit_ref[:, span])
        next_ref[:, span] = (weight_ref[:, span].astype(f32) - step * grad).astype(bf16)
        return none

    lax.fori_loop(0, misfit_ref.shape[1] // block, columns, 0)
    rows = misfit_out_ref.shape[0]
    here = pl.multiple_of(pl.program_id(0) * rows, rows)
    value = misfit_ref[pl.ds(here, rows)]
    misfit_out_ref[...] = value

    @pl.when(pl.program_id(0) == 0)
    def _():
        bias_out_ref[...] = bias_ref[...]

    bias_out_ref[...] -= step * jnp.sum(value.astype(f32), axis=0, keepdims=True)


def update(turned, misfit, weight, bias):
    hid, cells = weight.shape
    runs = misfit.shape[0]
    steps = 8
    whole = pl.BlockSpec((runs, cells), lambda i: (0, 0))
    line = pl.BlockSpec((1, cells), lambda i: (0, 0))
    tile = pl.BlockSpec((hid // steps, cells), lambda i: (i, 0))
    return pl.pallas_call(
        update_kernel,
        grid=(steps,),
        out_shape=(
            jax.ShapeDtypeStruct(weight.shape, weight.dtype),
            jax.ShapeDtypeStruct(misfit.shape, misfit.dtype),
            jax.ShapeDtypeStruct(bias.shape, bias.dtype),
        ),
        in_specs=[pl.BlockSpec((hid // steps, runs), lambda i: (i, 0)), whole, tile, line],
        out_specs=(tile, pl.BlockSpec((runs // steps, cells), lambda i: (i, 0)), line),
        compiler_params=pltpu.CompilerParams(vmem_limit_bytes=40 * MIB),
        cost_estimate=pl.CostEstimate(
            flops=2 * hid * cells * runs, bytes_accessed=4 * hid * cells, transcendentals=0
        ),
        name="update",
    )(turned, misfit, weight, bias)


def sum_kernel(
    part_ref, out_ref, pair, own, landed, mine,
    pair_send, pair_recv, part_send, part_recv, back_send, back_recv, last_send, last_recv,
):
    here = place()
    core = here["core"]
    chips = own.shape[0]
    chip = here["xh"] * 32 + here["xl"] * 16 + here["y"] * 4 + here["z"]
    mate = at(here, core=1 - core)

    def device(k):
        return (k // 32, core, (k // 16) % 2, (k // 4) % 4, k % 4)

    barrier = pltpu.get_barrier_semaphore()
    pl.semaphore_signal(barrier, inc=1, device_id=mate, device_id_type=BY_ID)

    def greet(j, carry):
        pl.semaphore_signal(
            barrier, inc=1, device_id=device((chip + j) % chips), device_id_type=BY_ID
        )
        return carry

    lax.fori_loop(1, chips, greet, 0)
    pl.semaphore_wait(barrier, chips)

    swap = pltpu.make_async_remote_copy(
        src_ref=part_ref.at[pl.ds((1 - core) * chips, chips)],
        dst_ref=pair,
        send_sem=pair_send,
        recv_sem=pair_recv,
        device_id=mate,
        device_id_type=BY_ID,
    )
    swap.start()
    swap.wait_recv()
    own[...] = part_ref[pl.ds(core * chips, chips)] + pair[...]

    def scatter(j, carry):
        other = (chip + j) % chips
        pltpu.make_async_remote_copy(
            src_ref=own.at[other],
            dst_ref=landed.at[j - 1],
            send_sem=part_send,
            recv_sem=part_recv,
            device_id=device(other),
            device_id_type=BY_ID,
        ).start()
        return carry

    lax.fori_loop(1, chips, scatter, 0)
    total = own[chip]
    whole = pltpu.make_async_remote_copy(
        src_ref=own.at[pl.ds(0, chips - 1)],
        dst_ref=landed,
        send_sem=part_send,
        recv_sem=part_recv,
        device_id=mate,
        device_id_type=BY_ID,
    )
    whole.wait_recv()
    mine[...] = total + jnp.sum(landed[...], axis=0)

    slot = core * chips + chip
    out_ref[slot] = mine[...]

    def spread(j, carry):
        pltpu.make_async_remote_copy(
            src_ref=mine,
            dst_ref=out_ref.at[slot],
            send_sem=back_send,
            recv_sem=back_recv,
            device_id=device((chip + j) % chips),
            device_id_type=BY_ID,
        ).start()
        return carry

    lax.fori_loop(1, chips, spread, 0)
    gathered = pltpu.make_async_remote_copy(
        src_ref=own.at[pl.ds(0, chips - 1)],
        dst_ref=landed,
        send_sem=back_send,
        recv_sem=back_recv,
        device_id=mate,
        device_id_type=BY_ID,
    )
    gathered.wait_recv()
    half = pl.ds(core * chips, chips)
    last = pltpu.make_async_remote_copy(
        src_ref=out_ref.at[half],
        dst_ref=out_ref.at[half],
        send_sem=last_send,
        recv_sem=last_recv,
        device_id=mate,
        device_id_type=BY_ID,
    )
    last.start()
    last.wait()
    swap.wait_send()
    whole.wait_send()
    gathered.wait_send()


def sum_everywhere(part):
    tiles = part.shape[0]
    f32 = jnp.float32
    dma = pltpu.SemaphoreType.DMA
    vmem = pl.BlockSpec(memory_space=pltpu.VMEM)
    tile = part.shape[1:]
    return pl.pallas_call(
        sum_kernel,
        out_shape=jax.ShapeDtypeStruct(part.shape, f32),
        in_specs=[vmem],
        out_specs=vmem,
        scratch_shapes=[
            pltpu.VMEM((tiles // 2,) + tile, f32),
            pltpu.VMEM((tiles // 2,) + tile, f32),
            pltpu.VMEM((tiles // 2 - 1,) + tile, f32),
            pltpu.VMEM(tile, f32),
        ] + [dma] * 8,
        compiler_params=pltpu.CompilerParams(
            collective_id=2, has_side_effects=True, vmem_limit_bytes=16 * MIB
        ),
        name="sum_everywhere",
    )(part)


def onehots(run_levels, step_pick):
    count = run_levels.shape[0]
    onehot = (run_levels[:, :, None] == jnp.arange(LEVELS, dtype=jnp.int32)).reshape(count, -1)
    moment = step_pick[:, None] == jnp.arange(1, STEPS + 2, dtype=jnp.int32)
    return jnp.concatenate([onehot, moment], axis=1).astype(jnp.bfloat16)


def independent(run_levels, step_pick, steepness):
    f32, bf16 = jnp.float32, jnp.bfloat16
    count = run_levels.shape[0]
    level = jnp.arange(LEVELS - 1, dtype=jnp.int32)
    onehot = (run_levels.T[:, None, :] == level[None, :, None]).reshape(-1, count)
    moment = step_pick[None, :] == jnp.arange(1, STEPS, dtype=jnp.int32)[:, None]
    high = lax.reduce_precision(steepness, 8, 7)
    middle = lax.reduce_precision(steepness - high, 8, 7)
    low = steepness - high - middle
    return jnp.concatenate(
        [
            onehot.astype(bf16),
            moment.astype(bf16),
            jnp.ones((1, count), bf16),
            jnp.stack([high, middle, low, jnp.zeros_like(low)]).astype(bf16),
            jnp.zeros((64 - CLASSES * (LEVELS - 1) - STEPS - 4, count), bf16),
        ],
        axis=0,
    )


def all_features(sums):
    width = sums.shape[1]
    first = CLASSES * (LEVELS - 1)
    classes = sums[:first].reshape(CLASSES, LEVELS - 1, width)
    moment = sums[first : first + STEPS - 1]
    ones = sums[first + STEPS - 1 : first + STEPS]
    steep = jnp.sum(sums[first + STEPS : first + STEPS + 3], axis=0, keepdims=True)
    last = ones[None] - jnp.sum(classes, axis=1, keepdims=True)
    classes = jnp.concatenate([classes, last], axis=1).reshape(CLASSES * LEVELS, width)
    final = ones - jnp.sum(moment, axis=0, keepdims=True)
    return jnp.concatenate([classes, moment, final, steep], axis=0)


def on_device(
    start_field, class_ids, run_levels, steepness, step_pick, input_layer, output_layer, output_bias
):
    local_runs = start_field.shape[0]
    total_runs = run_levels.shape[0]
    first_run = lax.axis_index(GRP) * local_runs
    levels_here = lax.dynamic_slice_in_dim(run_levels, first_run, local_runs, 0)
    steep = lax.dynamic_slice_in_dim(steepness, first_run, local_runs, 0)[:, None]
    pick_here = lax.dynamic_slice_in_dim(step_pick, first_run, local_runs, 0)[:, None]
    table = 0.015 * jnp.exp(levels_here.astype(jnp.float32) * jnp.log(jnp.float32(1.35)))
    basis = independent(run_levels, step_pick, steepness)
    near = basis.reshape(64, 2, total_runs // 2).transpose(1, 0, 2)
    far = basis.reshape(64, 2, 2, 2, local_runs // 2).transpose(1, 3, 0, 2, 4)
    far = far.reshape(2, 2, 64, local_runs)
    bias = output_bias[None, :]
    misfit, turned, tiles = solve(
        start_field, class_ids, table, steep, pick_here,
        onehots(run_levels, step_pick), steepness[:, None], input_layer, near, far, bias, output_layer,
    )
    tiles = sum_everywhere(tiles)
    width = input_layer.shape[1]
    sums = tiles.reshape(8, width // 128, 8, 128).transpose(0, 2, 1, 3).reshape(64, width)
    input_next = input_layer - 2.0 * all_features(sums)
    output_next, misfit, bias_next = update(turned, misfit, output_layer, bias)
    return (misfit, output_next, bias_next[0], input_next)


def solution(mesh):
    split = Mesh(mesh.devices.reshape(2, 2, 2, 4, 4), AXES)
    return jax.shard_map(
        on_device,
        mesh=split,
        in_specs=(
            P(GRP, TILE, None),
            P(TILE, None),
            P(),
            P(),
            P(),
            P(),
            P(None, GRP + TILE),
            P(GRP + TILE),
        ),
        out_specs=(P(None, GRP + TILE), P(None, GRP + TILE), P(GRP + TILE), P()),
        check_vma=False,
    )
```

```python
import math

import jax
import jax.numpy as jnp
from jax import lax
from jax.experimental import pallas as pl
from jax.experimental.pallas import tpu as pltpu
from jax.sharding import Mesh
from jax.sharding import PartitionSpec as P

STEPS = 4
LEVELS = 8
CLASSES = 8
AXES = ("xh", "core", "xl", "y", "z")
GRP = ("xh", "core")
TILE = ("xl", "y", "z")
BY_ID = pl.DeviceIdType.MESH
MIB = 2**20
CHUNKS = 8
SUB = 8


def place():
    return {axis: lax.axis_index(axis) for axis in AXES}


def at(here, **moved):
    return tuple(moved.get(axis, here[axis]) for axis in AXES)


def beside(here, step):
    tile = here["xl"] * 16 + here["y"] * 4 + here["z"] + step
    tile = (tile + 32) % 32
    return at(here, xl=tile // 16, y=(tile // 4) % 4, z=tile % 4)


def dot(a, b):
    return lax.dot_general(a, b, (((1,), (0,)), ((), ())), preferred_element_type=jnp.float32)


def dot_turned(a, b):
    return lax.dot_general(a, b, (((1,), (1,)), ((), ())), preferred_element_type=jnp.float32)


def two_parts(x):
    high = x.astype(jnp.bfloat16)
    return high, (x - high.astype(jnp.float32)).astype(jnp.bfloat16)


def dot_parts(x, order):
    high, low = two_parts(x)
    return dot(high, order) + dot(low, order)


def solve_kernel(
    field_ref, ids_ref, about_ref, input_ref, bias_ref, weight_ref,
    misfit_ref, turned_ref, part_ref,
    raw, rows_own, class_ref, halo_up, halo_dn, class_up, class_dn, kappa, wide_a, wide_b, picked, sent, got,
    relay, weight, hidden, turned, gain, pred, misfit, misfit_far, grad,
    load_sem, halo_send, halo_recv, class_send, class_recv, out_send, out_recv, keep_sem, weight_sem,
    relay_send, relay_recv,
):
    here = place()
    runs = rows_own.shape[1]
    tile_rows = rows_own.shape[0]
    width = rows_own.shape[2]
    part = runs // CHUNKS
    tile = here["xl"] * 16 + here["y"] * 4 + here["z"]
    group = here["xh"] * 2 + here["core"]
    up, dn = beside(here, -1), beside(here, 1)
    has_up, has_dn = tile > 0, tile < 31
    mates = (
        (here["xh"] * 2 + 1 - here["core"], at(here, core=1 - here["core"])),
        ((1 - here["xh"]) * 2 + here["core"], at(here, xh=1 - here["xh"])),
        ((1 - here["xh"]) * 2 + 1 - here["core"], at(here, xh=1 - here["xh"], core=1 - here["core"])),
    )

    def load(k):
        lines = part * tile_rows
        return [
            pltpu.make_async_copy(
                field_ref.at[pl.ds(k * lines, lines), pl.ds(128 * c, 128)],
                raw.at[c, pl.ds(k * lines, lines)],
                load_sem.at[k, c],
            )
            for c in range(width // 128)
        ]

    for k in range(CHUNKS):
        for copy in load(k):
            copy.start()
    weight_load = pltpu.make_async_copy(weight_ref, weight, weight_sem)
    weight_load.start()

    barrier = pltpu.get_barrier_semaphore()
    for _, mate in mates:
        pl.semaphore_signal(barrier, inc=1, device_id=mate, device_id_type=BY_ID)

    @pl.when(has_up)
    def _():
        pl.semaphore_signal(barrier, inc=1, device_id=up, device_id_type=BY_ID)

    @pl.when(has_dn)
    def _():
        pl.semaphore_signal(barrier, inc=1, device_id=dn, device_id_type=BY_ID)

    xl = here["xl"]
    ends_dn, ends_up = tile == 15, tile == 16
    corner = 3 * (1 - xl)
    relay_path = (here["y"] - corner + 4) % 4
    is_relay = (here["z"] == corner) & (relay_path > 0)
    relay_from = at(here, y=corner)
    relay_to = at(here, xl=1 - xl, y=3 * xl, z=3 * xl)

    @pl.when(is_relay)
    def _():
        for other in (relay_from, relay_to):
            pl.semaphore_signal(barrier, inc=1, device_id=other, device_id_type=BY_ID)

    @pl.when(ends_dn | ends_up)
    def _():
        for side in range(2):
            for p in range(1, 4):
                edge_at = 3 * (1 - side)
                other = at(here, xl=side, y=(edge_at + p) % 4, z=edge_at)
                pl.semaphore_signal(barrier, inc=1, device_id=other, device_id_type=BY_ID)

    callers = 3 + jnp.where(has_up, 1, 0) + jnp.where(has_dn, 1, 0)
    callers = callers + jnp.where(is_relay, 2, 0)
    callers = callers + jnp.where(ends_dn | ends_up, 6, 0)
    pl.semaphore_wait(barrier, callers)

    def class_copy(upward):
        return pltpu.make_async_remote_copy(
            src_ref=class_ref.at[pl.ds(0 if upward else tile_rows - STEPS, STEPS)],
            dst_ref=class_dn if upward else class_up,
            send_sem=class_send.at[0 if upward else 1],
            recv_sem=class_recv.at[0 if upward else 1],
            device_id=up if upward else dn,
            device_id_type=BY_ID,
        )

    def halo_copy(k, upward):
        span = pl.ds(pl.multiple_of(k * part, part), part)
        return pltpu.make_async_remote_copy(
            src_ref=rows_own.at[pl.ds(0 if upward else tile_rows - STEPS, STEPS), span],
            dst_ref=(halo_dn if upward else halo_up).at[:, span],
            send_sem=halo_send.at[k, 0 if upward else 1],
            recv_sem=halo_recv.at[k, 0 if upward else 1],
            device_id=up if upward else dn,
            device_id_type=BY_ID,
        )

    def detour_copy(k, upward):
        span = pl.ds(pl.multiple_of(k * part, part), part)
        return pltpu.make_async_remote_copy(
            src_ref=rows_own.at[pl.ds(0 if upward else tile_rows - STEPS, STEPS), span],
            dst_ref=relay.at[k // 4],
            send_sem=halo_send.at[k, 0 if upward else 1],
            recv_sem=relay_recv.at[k // 4],
            device_id=at(here, y=(here["y"] + k % 4) % 4),
            device_id_type=BY_ID,
        )

    def forward_copy(k, upward):
        span = pl.ds(pl.multiple_of(k * part, part), part)
        return pltpu.make_async_remote_copy(
            src_ref=relay.at[k // 4],
            dst_ref=(halo_dn if upward else halo_up).at[:, span],
            send_sem=relay_send.at[k // 4],
            recv_sem=halo_recv.at[k, 0 if upward else 1],
            device_id=relay_to,
            device_id_type=BY_ID,
        )

    def send_halo(k, upward):
        detour = (ends_up if upward else ends_dn) & (k % 4 > 0)

        @pl.when((has_up if upward else has_dn) & jnp.logical_not(detour))
        def _():
            halo_copy(k, upward).start()

        @pl.when(detour)
        def _():
            detour_copy(k, upward).start()

    def out_copy(k, j):
        span = pl.ds(pl.multiple_of(k * part, part), part)
        owner, mate = mates[j]
        return pltpu.make_async_remote_copy(
            src_ref=sent.at[owner, span],
            dst_ref=got.at[j, span],
            send_sem=out_send.at[k, j],
            recv_sem=out_recv.at[k, j],
            device_id=mate,
            device_id_type=BY_ID,
        )

    @pl.when(jnp.logical_not(has_up))
    def _():
        halo_up[...] = jnp.zeros_like(halo_up)
        class_up[...] = jnp.full_like(class_up, -1.0)

    @pl.when(jnp.logical_not(has_dn))
    def _():
        halo_dn[...] = jnp.zeros_like(halo_dn)
        class_dn[...] = jnp.full_like(class_dn, -1.0)

    first = lax.broadcasted_iota(jnp.int32, (width, width), 0)
    second = lax.broadcasted_iota(jnp.int32, (width, width), 1)
    blocks = width // 128
    order = jnp.where(first == (second % 128) * blocks + second // 128, 1.0, 0.0)
    order = order.astype(jnp.bfloat16)
    lines = part * tile_rows
    class_rows = dot(ids_ref[...].astype(jnp.float32).astype(jnp.bfloat16), order)
    for i in range(tile_rows):
        class_ref[i] = jnp.broadcast_to(class_rows[i : i + 1], (SUB, width))

    @pl.when(has_up)
    def _():
        class_copy(True).start()

    @pl.when(has_dn)
    def _():
        class_copy(False).start()

    def prepare(k, none):
        for copy in load(k):
            copy.wait()
        span = pl.ds(pl.multiple_of(k * lines, lines), lines)
        lined = jnp.concatenate([raw[c, span] for c in range(blocks)], axis=1)
        lined = dot_parts(lined, order)
        for c in range(blocks):
            raw[c, span] = lined[:, 128 * c : 128 * c + 128]

        def turn(j, carry):
            first = pl.multiple_of(j * SUB, SUB)
            for i in range(tile_rows):
                for c in range(blocks):
                    rows_own[i, pl.ds(first, SUB), pl.ds(128 * c, 128)] = raw[
                        c, pl.ds(j * (SUB * tile_rows) + i, SUB, stride=tile_rows), :
                    ]
            return carry

        lax.fori_loop(k * (part // SUB), (k + 1) * (part // SUB), turn, 0)

        send_halo(k, True)
        send_halo(k, False)
        return none

    lax.fori_loop(0, CHUNKS, prepare, 0)

    @pl.when(has_up)
    def _():
        class_copy(False).wait_recv()

    @pl.when(has_dn)
    def _():
        class_copy(True).wait_recv()

    keep_up = jnp.where(has_up, 1.0, 0.0).astype(jnp.float32)
    keep_dn = jnp.where(has_dn, 1.0, 0.0).astype(jnp.float32)
    lane = lax.broadcasted_iota(jnp.int32, (SUB, 128), 1)
    left, right = lane == 0, lane == 127
    edge = width - 128

    def next_column(x):
        turned = jnp.where(right, 0.0, pltpu.roll(x[:, :128], 127, 1))
        return jnp.concatenate([x[:, 128:], turned], axis=1)

    def last_column(x, outermost):
        turned = jnp.where(left, outermost[:, :128], pltpu.roll(x[:, edge:], 1, 1))
        return jnp.concatenate([turned, x[:, :edge]], axis=1)

    span_rows = tile_rows + 2 * STEPS

    def advance(k, half_chunk):
        first = pl.multiple_of(k * part + half_chunk * SUB, SUB)
        runs_here = pl.ds(first, SUB)
        picked_here = pl.ds(pl.multiple_of(half_chunk * SUB, SUB), SUB)
        about = about_ref[pl.ds(pl.multiple_of(group * runs + first, SUB), SUB)]
        table = 0.015 * jnp.exp(about[:, :CLASSES] * math.log(1.35))
        steep = jnp.broadcast_to(about[:, CLASSES : CLASSES + 1], (SUB, width))
        pick = jnp.broadcast_to(about[:, CLASSES + 1 : CLASSES + 2], (SUB, width))
        rest = 1.0 - steep
        half = [jnp.broadcast_to(table[:, c : c + 1], (SUB, width)) for c in range(CLASSES)]
        for i in range(span_rows):
            if i < STEPS:
                klass = class_up[i]
            elif i < STEPS + tile_rows:
                klass = class_ref[i - STEPS]
            else:
                klass = class_dn[i - STEPS - tile_rows]
            value = jnp.zeros((SUB, width), jnp.float32)
            for c in range(CLASSES):
                value = jnp.where(klass == float(c), half[c], value)
            kappa[i] = value

        def start_row(i):
            if i < STEPS:
                return halo_up[i, runs_here]
            if i < STEPS + tile_rows:
                return rows_own[i - STEPS, runs_here]
            return halo_dn[i - STEPS - tile_rows, runs_here]

        for step in range(STEPS):
            source = (None, wide_a, wide_b, wide_a)[step]
            sink = (wide_a, wide_b, wide_a, None)[step]

            def row(i):
                return start_row(i) if step == 0 else source[i]

            def spread_of(i, value):
                bottom = 1.0 + value * value
                guess = pl.reciprocal(bottom, approx=True)
                guess = guess * (2.0 - bottom * guess)
                return kappa[i] * (steep + rest * guess)

            above = row(step)
            above_spread = spread_of(step, above)
            centre = row(step + 1)
            spread = spread_of(step + 1, centre)
            flow_in = (above_spread + spread) * (centre - above)
            for i in range(step + 1, span_rows - step - 1):
                below = row(i + 1)
                below_spread = spread_of(i + 1, below)
                flow_out = (spread + below_spread) * (below - centre)
                flow = (spread + next_column(spread)) * (next_column(centre) - centre)
                back = last_column(flow, spread * centre)
                total = centre + (flow_out - flow_in) + (flow - back)
                if i < STEPS:
                    total = total * keep_up
                if i >= STEPS + tile_rows:
                    total = total * keep_dn
                if sink is not None:
                    sink[i] = total
                if STEPS <= i < STEPS + tile_rows:
                    if step > 0:
                        total = jnp.where(pick == step + 1.0, total, picked[i - STEPS, picked_here])
                    picked[i - STEPS, picked_here] = total
                flow_in, centre, spread = flow_out, below, below_spread

    back_order = jnp.where(second == (first % 128) * blocks + first // 128, 1.0, 0.0)
    back_order = back_order.astype(jnp.bfloat16)

    def one_chunk(k, none):
        for upward in (False, True):
            for slot in range(2):
                @pl.when(is_relay & (xl == int(upward)) & (k == 2 * slot))
                def _():
                    passed = relay_path + 4 * slot
                    forward = forward_copy(passed, upward)
                    detour_copy(passed, upward).wait_recv()
                    forward.start()

        @pl.when(has_up)
        def _():
            halo_copy(k, False).wait_recv()

        @pl.when(has_dn)
        def _():
            halo_copy(k, True).wait_recv()

        def half_of(half_chunk, carry):
            advance(k, half_chunk)
            return carry

        lax.fori_loop(0, part // SUB, half_of, 0)
        lined = dot_parts(picked[...].reshape(tile_rows * part, width), back_order)
        span = pl.ds(pl.multiple_of(k * part, part), part)
        for i in range(tile_rows):
            sent[i // 4, span, pl.ds((i % 4) * width, width)] = lined[i * part : (i + 1) * part]
        for j in range(3):
            out_copy(k, j).start()
        return none

    lax.fori_loop(0, CHUNKS, one_chunk, 0)

    cells = weight.shape[1]
    hid = weight.shape[0]
    all_runs = hidden.shape[0]
    block = 256
    f32, bf16 = jnp.float32, jnp.bfloat16
    eye = lax.broadcasted_iota(jnp.int32, (block, block), 0) == lax.broadcasted_iota(
        jnp.int32, (block, block), 1
    )
    eye = jnp.where(eye, 1.0, 0.0).astype(bf16)
    share = 2.0 / all_runs
    about = about_ref[...]
    steep_all = about[:, CLASSES : CLASSES + 1]
    feats = input_ref.shape[0]
    onehots = CLASSES * LEVELS
    entry = lax.broadcasted_iota(jnp.int32, (16, feats), 0)
    column = lax.broadcasted_iota(jnp.int32, (16, feats), 1)
    source = jnp.where(column < onehots, column // LEVELS, CLASSES + 1)
    spread_out = dot(about.astype(bf16), jnp.where(entry == source, 1.0, 0.0).astype(bf16))
    column = lax.broadcasted_iota(jnp.int32, (all_runs, feats), 1)
    wanted = jnp.where(column < onehots, column % LEVELS, column - onehots + 1)
    wanted = jnp.where(column < onehots + STEPS, wanted, -1).astype(f32)
    onehot = jnp.where(spread_out == wanted, 1.0, 0.0).astype(bf16)

    def independent(rows):
        count = rows.shape[0]
        kept = LEVELS - 1
        levels_end, moments_end = CLASSES * kept, CLASSES * kept + STEPS - 1
        high, middle = two_parts(rows)
        low = (rows - high.astype(f32) - middle.astype(f32)).astype(bf16)
        line = lax.broadcasted_iota(jnp.int32, (64, 16), 0)
        entry = lax.broadcasted_iota(jnp.int32, (64, 16), 1)
        source = jnp.where(line < levels_end, line // kept, CLASSES + 1)
        source = jnp.where(line > moments_end, CLASSES, source)

        def chosen(last, extra):
            keep = (entry == source) & ((line < last) | (line == extra))
            return jnp.where(keep, 1.0, 0.0).astype(bf16)

        value = (
            dot_turned(chosen(moments_end, moments_end + 1), high)
            + dot_turned(chosen(0, moments_end + 2), middle)
            + dot_turned(chosen(0, moments_end + 3), low)
        )
        line = lax.broadcasted_iota(jnp.int32, (64, count), 0)
        wanted = jnp.where(line < levels_end, line % kept, line - levels_end + 1).astype(f32)
        marks = jnp.where(value == wanted, 1.0, 0.0)
        value = jnp.where(line < moments_end, marks, value)
        return jnp.where(line == moments_end, 1.0, value).astype(bf16)

    def hidden_block(n, none):
        span = pl.ds(pl.multiple_of(n * block, block), block)
        value = input_ref[:, span]
        high, low = two_parts(value)
        rest = (value - high.astype(f32) - low.astype(f32)).astype(bf16)
        pre = dot(onehot, high) + (dot(onehot, low) + dot(onehot, rest))
        pre = pre + steep_all * value[value.shape[0] - 1 :, :]
        logistic = 1.0 / (1.0 + jnp.exp(-pre))
        active = (pre * logistic).astype(bf16)
        hidden[:, span] = active
        gain[:, span] = logistic * (1.0 + pre * (1.0 - logistic)) * share
        turned[span, :] = dot_turned(eye, active).astype(bf16)
        return none

    lax.fori_loop(0, hid // block, hidden_block, 0)
    turned_copy = pltpu.make_async_copy(turned, turned_ref, keep_sem.at[0])
    turned_copy.start()
    weight_load.wait()

    def pred_block(n, none):
        span = pl.ds(pl.multiple_of(n * block, block), block)
        pred[:, span] = dot(hidden[...], weight[:, span]) + bias_ref[:, span]
        return none

    lax.fori_loop(0, cells // block, pred_block, 0)

    def compare(source, group_at, start, count, copy_row):
        def some(b, none):
            inner = pl.multiple_of(start + b * 16, 16)
            at_run = pl.ds(pl.multiple_of(group_at * runs + inner, 16), 16)
            value = (pred[at_run] - source[pl.ds(inner, 16)]).astype(bf16)
            misfit[at_run] = value
            if copy_row is not None:
                misfit_far[pl.ds(pl.multiple_of(copy_row + b * 16, 16), 16)] = value
            return none

        lax.fori_loop(0, count // 16, some, 0)

    for k in range(CHUNKS):
        out_copy(k, 0).wait_recv()
    compare(sent.at[group], group, 0, runs, None)
    compare(got.at[0], mates[0][0], 0, runs, None)
    near = pl.ds(pl.multiple_of(here["xh"] * (2 * runs), 2 * runs), 2 * runs)
    far = (1 - here["xh"]) * (2 * runs)

    near_mix = independent(about_ref[near])

    def near_block(n, none):
        span = pl.ds(pl.multiple_of(n * block, block), block)
        back = dot_turned(misfit[near], weight[span, :]) * gain[near, span]
        high, low = two_parts(back)
        grad[:, span] = dot(near_mix, high) + dot(near_mix, low)
        return none

    lax.fori_loop(0, hid // block, near_block, 0)
    near_copy = pltpu.make_async_copy(misfit.at[near], misfit_ref.at[near], keep_sem.at[1])
    near_copy.start()

    half = runs // 2
    for h in range(2):
        for k in range(h * CHUNKS // 2, (h + 1) * CHUNKS // 2):
            out_copy(k, 1).wait_recv()
            out_copy(k, 2).wait_recv()
        for j in (1, 2):
            at_row = here["core"] if j == 1 else 1 - here["core"]
            compare(got.at[j], mates[j][0], h * half, half, at_row * half)

        far_rows = [pl.ds(pl.multiple_of(far + g * runs + h * half, half), half) for g in range(2)]
        mix = independent(jnp.concatenate([about_ref[rows] for rows in far_rows], axis=0))

        def far_block(n, none):
            span = pl.ds(pl.multiple_of(n * block, block), block)
            factor = jnp.concatenate([gain[rows, span] for rows in far_rows], axis=0)
            back = dot_turned(misfit_far[...], weight[span, :]) * factor
            high, low = two_parts(back)
            grad[:, span] += dot(mix, high) + dot(mix, low)
            return none

        lax.fori_loop(0, hid // block, far_block, 0)

    far_span = pl.ds(pl.multiple_of(far, 2 * runs), 2 * runs)
    far_copy = pltpu.make_async_copy(misfit.at[far_span], misfit_ref.at[far_span], keep_sem.at[2])
    far_copy.start()
    for i in range(part_ref.shape[0]):
        r, c = i // (hid // 128), i % (hid // 128)
        part_ref[i] = grad[8 * r : 8 * r + 8, 128 * c : 128 * c + 128]
    @pl.when(is_relay)
    def _():
        for slot in range(2):
            forward_copy(relay_path + 4 * slot, False).wait_send()

    turned_copy.wait()
    near_copy.wait()
    far_copy.wait()
    for k in range(CHUNKS):
        for j in range(3):
            out_copy(k, j).wait_send()

    @pl.when(has_up)
    def _():
        class_copy(True).wait_send()
        for k in range(CHUNKS):
            halo_copy(k, True).wait_send()

    @pl.when(has_dn)
    def _():
        class_copy(False).wait_send()
        for k in range(CHUNKS):
            halo_copy(k, False).wait_send()


def solve(field, classes, about, input_layer, bias, weight):
    runs, rows, width = field.shape
    hid, cells = weight.shape
    all_runs = about.shape[0]
    f32, bf16 = jnp.float32, jnp.bfloat16
    dma = pltpu.SemaphoreType.DMA
    vmem = pl.BlockSpec(memory_space=pltpu.VMEM)
    anywhere = pl.BlockSpec(memory_space=pl.ANY)
    span = rows + 2 * STEPS
    part = runs // CHUNKS
    return pl.pallas_call(
        solve_kernel,
        out_shape=(
            jax.ShapeDtypeStruct((all_runs, cells), bf16),
            jax.ShapeDtypeStruct((hid, all_runs), bf16),
            jax.ShapeDtypeStruct((hid // 16, 8, 128), f32),
        ),
        in_specs=[anywhere] + [vmem] * 4 + [anywhere],
        out_specs=(anywhere, anywhere, vmem),
        scratch_shapes=[
            pltpu.VMEM((width // 128, runs * rows, 128), f32),
            pltpu.VMEM((rows, runs, width), f32),
            pltpu.VMEM((rows, SUB, width), f32),
            pltpu.VMEM((STEPS, runs, width), f32),
            pltpu.VMEM((STEPS, runs, width), f32),
            pltpu.VMEM((STEPS, SUB, width), f32),
            pltpu.VMEM((STEPS, SUB, width), f32),
            pltpu.VMEM((span, SUB, width), f32),
            pltpu.VMEM((span, SUB, width), f32),
            pltpu.VMEM((span, SUB, width), f32),
            pltpu.VMEM((rows, part, width), f32),
            pltpu.VMEM((4, runs, 4 * width), f32),
            pltpu.VMEM((3, runs, 4 * width), f32),
            pltpu.VMEM((2, STEPS, part, width), f32),
            pltpu.VMEM((hid, cells), bf16),
            pltpu.VMEM((all_runs, hid), bf16),
            pltpu.VMEM((hid, all_runs), bf16),
            pltpu.VMEM((all_runs, hid), f32),
            pltpu.VMEM((all_runs, cells), f32),
            pltpu.VMEM((all_runs, cells), bf16),
            pltpu.VMEM((runs, cells), bf16),
            pltpu.VMEM((64, hid), f32),
            dma((CHUNKS, 4)),
            dma((CHUNKS, 2)),
            dma((CHUNKS, 2)),
            dma((2,)),
            dma((2,)),
            dma((CHUNKS, 3)),
            dma((CHUNKS, 3)),
            dma((3,)),
            dma,
            dma((2,)),
            dma((2,)),
        ],
        compiler_params=pltpu.CompilerParams(
            collective_id=1, has_side_effects=True, vmem_limit_bytes=58 * MIB
        ),
        name="solve",
    )(
        field.reshape(runs * rows, width), classes, about, input_layer, bias, weight,
    )


def update_kernel(turned_ref, misfit_ref, weight_ref, bias_ref, next_ref, misfit_out_ref, bias_out_ref):
    f32, bf16 = jnp.float32, jnp.bfloat16
    step = 1.0 / misfit_ref.shape[0]
    block = 256

    def columns(n, none):
        span = pl.ds(pl.multiple_of(n * block, block), block)
        grad = dot(turned_ref[...], misfit_ref[:, span])
        next_ref[:, span] = (weight_ref[:, span].astype(f32) - step * grad).astype(bf16)
        return none

    lax.fori_loop(0, misfit_ref.shape[1] // block, columns, 0, unroll=True)
    rows = misfit_out_ref.shape[0]
    here = pl.multiple_of(pl.program_id(0) * rows, rows)
    value = misfit_ref[pl.ds(here, rows)]
    misfit_out_ref[...] = value

    @pl.when(pl.program_id(0) == 0)
    def _():
        bias_out_ref[...] = bias_ref[...]

    bias_out_ref[...] -= step * jnp.sum(value.astype(f32), axis=0, keepdims=True)


def update(turned, misfit, weight, bias):
    hid, cells = weight.shape
    runs = misfit.shape[0]
    steps = 4
    whole = pl.BlockSpec((runs, cells), lambda i: (0, 0))
    line = pl.BlockSpec((1, cells), lambda i: (0, 0))
    tile = pl.BlockSpec((hid // steps, cells), lambda i: (i, 0))
    return pl.pallas_call(
        update_kernel,
        grid=(steps,),
        out_shape=(
            jax.ShapeDtypeStruct(weight.shape, weight.dtype),
            jax.ShapeDtypeStruct(misfit.shape, misfit.dtype),
            jax.ShapeDtypeStruct(bias.shape, bias.dtype),
        ),
        in_specs=[pl.BlockSpec((hid // steps, runs), lambda i: (i, 0)), whole, tile, line],
        out_specs=(tile, pl.BlockSpec((runs // steps, cells), lambda i: (i, 0)), line),
        compiler_params=pltpu.CompilerParams(vmem_limit_bytes=60 * MIB),
        cost_estimate=pl.CostEstimate(
            flops=2 * hid * cells * runs, bytes_accessed=4 * hid * cells, transcendentals=0
        ),
        name="update",
    )(turned, misfit, weight, bias)


def sum_kernel(
    part_ref, out_ref, pair, own, landed, mine,
    pair_send, pair_recv, part_send, part_recv, back_send, back_recv, last_send, last_recv,
):
    here = place()
    core = here["core"]
    chips = own.shape[0]
    chip = here["xh"] * 32 + here["xl"] * 16 + here["y"] * 4 + here["z"]
    mate = at(here, core=1 - core)

    def device(k):
        return (k // 32, core, (k // 16) % 2, (k // 4) % 4, k % 4)

    barrier = pltpu.get_barrier_semaphore()
    pl.semaphore_signal(barrier, inc=1, device_id=mate, device_id_type=BY_ID)

    def greet(j, carry):
        pl.semaphore_signal(
            barrier, inc=1, device_id=device((chip + j) % chips), device_id_type=BY_ID
        )
        return carry

    lax.fori_loop(1, chips, greet, 0)
    pl.semaphore_wait(barrier, chips)

    swap = pltpu.make_async_remote_copy(
        src_ref=part_ref.at[pl.ds((1 - core) * chips, chips)],
        dst_ref=pair,
        send_sem=pair_send,
        recv_sem=pair_recv,
        device_id=mate,
        device_id_type=BY_ID,
    )
    swap.start()
    swap.wait_recv()
    own[...] = part_ref[pl.ds(core * chips, chips)] + pair[...]

    def scatter(j, carry):
        other = (chip + j) % chips
        pltpu.make_async_remote_copy(
            src_ref=own.at[other],
            dst_ref=landed.at[j - 1],
            send_sem=part_send,
            recv_sem=part_recv,
            device_id=device(other),
            device_id_type=BY_ID,
        ).start()
        return carry

    lax.fori_loop(1, chips, scatter, 0)
    total = own[chip]
    whole = pltpu.make_async_remote_copy(
        src_ref=own.at[pl.ds(0, chips - 1)],
        dst_ref=landed,
        send_sem=part_send,
        recv_sem=part_recv,
        device_id=mate,
        device_id_type=BY_ID,
    )
    whole.wait_recv()
    mine[...] = total + jnp.sum(landed[...], axis=0)

    slot = core * chips + chip
    out_ref[slot] = mine[...]

    def spread(j, carry):
        pltpu.make_async_remote_copy(
            src_ref=mine,
            dst_ref=out_ref.at[slot],
            send_sem=back_send,
            recv_sem=back_recv,
            device_id=device((chip + j) % chips),
            device_id_type=BY_ID,
        ).start()
        return carry

    lax.fori_loop(1, chips, spread, 0)
    gathered = pltpu.make_async_remote_copy(
        src_ref=own.at[pl.ds(0, chips - 1)],
        dst_ref=landed,
        send_sem=back_send,
        recv_sem=back_recv,
        device_id=mate,
        device_id_type=BY_ID,
    )
    gathered.wait_recv()
    half = pl.ds(core * chips, chips)
    last = pltpu.make_async_remote_copy(
        src_ref=out_ref.at[half],
        dst_ref=out_ref.at[half],
        send_sem=last_send,
        recv_sem=last_recv,
        device_id=mate,
        device_id_type=BY_ID,
    )
    last.start()
    last.wait()
    swap.wait_send()
    whole.wait_send()
    gathered.wait_send()


def sum_everywhere(part):
    tiles = part.shape[0]
    f32 = jnp.float32
    dma = pltpu.SemaphoreType.DMA
    vmem = pl.BlockSpec(memory_space=pltpu.VMEM)
    tile = part.shape[1:]
    return pl.pallas_call(
        sum_kernel,
        out_shape=jax.ShapeDtypeStruct(part.shape, f32),
        in_specs=[vmem],
        out_specs=vmem,
        scratch_shapes=[
            pltpu.VMEM((tiles // 2,) + tile, f32),
            pltpu.VMEM((tiles // 2,) + tile, f32),
            pltpu.VMEM((tiles // 2 - 1,) + tile, f32),
            pltpu.VMEM(tile, f32),
        ] + [dma] * 8,
        compiler_params=pltpu.CompilerParams(
            collective_id=2, has_side_effects=True, vmem_limit_bytes=16 * MIB
        ),
        name="sum_everywhere",
    )(part)


def all_features(sums):
    width = sums.shape[1]
    first = CLASSES * (LEVELS - 1)
    classes = sums[:first].reshape(CLASSES, LEVELS - 1, width)
    moment = sums[first : first + STEPS - 1]
    ones = sums[first + STEPS - 1 : first + STEPS]
    steep = jnp.sum(sums[first + STEPS : first + STEPS + 3], axis=0, keepdims=True)
    last = ones[None] - jnp.sum(classes, axis=1, keepdims=True)
    classes = jnp.concatenate([classes, last], axis=1).reshape(CLASSES * LEVELS, width)
    final = ones - jnp.sum(moment, axis=0, keepdims=True)
    return jnp.concatenate([classes, moment, final, steep], axis=0)


def on_device(
    start_field, class_ids, run_levels, steepness, step_pick, input_layer, output_layer, output_bias
):
    f32 = jnp.float32
    about = jnp.concatenate(
        [
            run_levels.astype(f32),
            steepness[:, None],
            step_pick[:, None].astype(f32),
            jnp.zeros((run_levels.shape[0], 16 - CLASSES - 2), f32),
        ],
        axis=1,
    )
    bias = output_bias[None, :]
    misfit, turned, tiles = solve(start_field, class_ids, about, input_layer, bias, output_layer)
    tiles = sum_everywhere(tiles)
    width = input_layer.shape[1]
    sums = tiles.reshape(8, width // 128, 8, 128).transpose(0, 2, 1, 3).reshape(64, width)
    input_next = input_layer - 2.0 * all_features(sums)
    output_next, misfit, bias_next = update(turned, misfit, output_layer, bias)
    return (misfit, output_next, bias_next[0], input_next)


def solution(mesh):
    split = Mesh(mesh.devices.reshape(2, 2, 2, 4, 4), AXES)
    return jax.shard_map(
        on_device,
        mesh=split,
        in_specs=(
            P(GRP, TILE, None),
            P(TILE, None),
            P(),
            P(),
            P(),
            P(),
            P(None, GRP + TILE),
            P(GRP + TILE),
        ),
        out_specs=(P(None, GRP + TILE), P(None, GRP + TILE), P(GRP + TILE), P()),
        check_vma=False,
    )
```

```python
import math

import jax
import jax.numpy as jnp
from jax import lax
from jax.experimental import pallas as pl
from jax.experimental.pallas import tpu as pltpu
from jax.sharding import Mesh
from jax.sharding import PartitionSpec as P

STEPS = 4
LEVELS = 8
CLASSES = 8
AXES = ("xh", "core", "xl", "y", "z")
GRP = ("xh", "core")
TILE = ("xl", "y", "z")
BY_ID = pl.DeviceIdType.MESH
MIB = 2**20
CHUNKS = 8
SUB = 8


def place():
    return {axis: lax.axis_index(axis) for axis in AXES}


def at(here, **moved):
    return tuple(moved.get(axis, here[axis]) for axis in AXES)


def beside(here, step):
    tile = here["xl"] * 16 + here["y"] * 4 + here["z"] + step
    tile = (tile + 32) % 32
    return at(here, xl=tile // 16, y=(tile // 4) % 4, z=tile % 4)


def dot(a, b):
    return lax.dot_general(a, b, (((1,), (0,)), ((), ())), preferred_element_type=jnp.float32)


def dot_turned(a, b):
    return lax.dot_general(a, b, (((1,), (1,)), ((), ())), preferred_element_type=jnp.float32)


def two_parts(x):
    high = x.astype(jnp.bfloat16)
    return high, (x - high.astype(jnp.float32)).astype(jnp.bfloat16)


def dot_parts(x, order):
    high, low = two_parts(x)
    return dot(high, order) + dot(low, order)


def solve_kernel(
    field_ref, ids_ref, about_ref, input_ref, bias_ref, weight_ref,
    misfit_ref, turned_ref, sums_ref,
    raw, rows_own, class_ref, halo_up, halo_dn, class_up, class_dn, kappa, wide_a, wide_b, picked, sent, got,
    relay, weight, hidden, turned, gain, pred, misfit, misfit_far, grad,
    tiles, pair, own, landed, middle, landed_z, mine,
    load_sem, halo_send, halo_recv, class_send, class_recv, out_send, out_recv, keep_sem, weight_sem,
    relay_send, relay_recv, sum_send, sum_recv,
):
    here = place()
    runs = rows_own.shape[1]
    tile_rows = rows_own.shape[0]
    width = rows_own.shape[2]
    part = runs // CHUNKS
    tile = here["xl"] * 16 + here["y"] * 4 + here["z"]
    group = here["xh"] * 2 + here["core"]
    up, dn = beside(here, -1), beside(here, 1)
    has_up, has_dn = tile > 0, tile < 31
    mates = (
        (here["xh"] * 2 + 1 - here["core"], at(here, core=1 - here["core"])),
        ((1 - here["xh"]) * 2 + here["core"], at(here, xh=1 - here["xh"])),
        ((1 - here["xh"]) * 2 + 1 - here["core"], at(here, xh=1 - here["xh"], core=1 - here["core"])),
    )

    def load(k):
        lines = part * tile_rows
        return [
            pltpu.make_async_copy(
                field_ref.at[pl.ds(k * lines, lines), pl.ds(128 * c, 128)],
                raw.at[c, pl.ds(k * lines, lines)],
                load_sem.at[k, c],
            )
            for c in range(width // 128)
        ]

    for k in range(CHUNKS):
        for copy in load(k):
            copy.start()
    weight_load = pltpu.make_async_copy(weight_ref, weight, weight_sem)
    weight_load.start()

    barrier = pltpu.get_barrier_semaphore()
    for _, mate in mates:
        pl.semaphore_signal(barrier, inc=1, device_id=mate, device_id_type=BY_ID)

    @pl.when(has_up)
    def _():
        pl.semaphore_signal(barrier, inc=1, device_id=up, device_id_type=BY_ID)

    @pl.when(has_dn)
    def _():
        pl.semaphore_signal(barrier, inc=1, device_id=dn, device_id_type=BY_ID)

    xl = here["xl"]
    ends_dn, ends_up = tile == 15, tile == 16
    corner = 3 * (1 - xl)
    relay_path = (here["y"] - corner + 4) % 4
    is_relay = (here["z"] == corner) & (relay_path > 0)
    relay_from = at(here, y=corner)
    relay_to = at(here, xl=1 - xl, y=3 * xl, z=3 * xl)

    @pl.when(is_relay)
    def _():
        for other in (relay_from, relay_to):
            pl.semaphore_signal(barrier, inc=1, device_id=other, device_id_type=BY_ID)

    @pl.when(ends_dn | ends_up)
    def _():
        for side in range(2):
            for p in range(1, 4):
                edge_at = 3 * (1 - side)
                other = at(here, xl=side, y=(edge_at + p) % 4, z=edge_at)
                pl.semaphore_signal(barrier, inc=1, device_id=other, device_id_type=BY_ID)

    plane = here["xh"] * 8 + here["xl"] * 4 + here["y"]

    def in_plane(k):
        return at(here, xh=k // 8, xl=(k // 4) % 2, y=k % 4)

    def greet(j, none):
        other = in_plane((plane + j) % 16)
        pl.semaphore_signal(barrier, inc=1, device_id=other, device_id_type=BY_ID)
        return none

    lax.fori_loop(1, 16, greet, 0)
    for j in range(1, 4):
        other = at(here, z=(here["z"] + j) % 4)
        pl.semaphore_signal(barrier, inc=1, device_id=other, device_id_type=BY_ID)

    callers = 3 + 18 + jnp.where(has_up, 1, 0) + jnp.where(has_dn, 1, 0)
    callers = callers + jnp.where(is_relay, 2, 0)
    callers = callers + jnp.where(ends_dn | ends_up, 6, 0)
    pl.semaphore_wait(barrier, callers)

    def class_copy(upward):
        return pltpu.make_async_remote_copy(
            src_ref=class_ref.at[pl.ds(0 if upward else tile_rows - STEPS, STEPS)],
            dst_ref=class_dn if upward else class_up,
            send_sem=class_send.at[0 if upward else 1],
            recv_sem=class_recv.at[0 if upward else 1],
            device_id=up if upward else dn,
            device_id_type=BY_ID,
        )

    def halo_copy(k, upward):
        span = pl.ds(pl.multiple_of(k * part, part), part)
        return pltpu.make_async_remote_copy(
            src_ref=rows_own.at[pl.ds(0 if upward else tile_rows - STEPS, STEPS), span],
            dst_ref=(halo_dn if upward else halo_up).at[:, span],
            send_sem=halo_send.at[k, 0 if upward else 1],
            recv_sem=halo_recv.at[k, 0 if upward else 1],
            device_id=up if upward else dn,
            device_id_type=BY_ID,
        )

    def detour_copy(k, upward):
        span = pl.ds(pl.multiple_of(k * part, part), part)
        return pltpu.make_async_remote_copy(
            src_ref=rows_own.at[pl.ds(0 if upward else tile_rows - STEPS, STEPS), span],
            dst_ref=relay.at[k // 4],
            send_sem=halo_send.at[k, 0 if upward else 1],
            recv_sem=relay_recv.at[k // 4],
            device_id=at(here, y=(here["y"] + k % 4) % 4),
            device_id_type=BY_ID,
        )

    def forward_copy(k, upward):
        span = pl.ds(pl.multiple_of(k * part, part), part)
        return pltpu.make_async_remote_copy(
            src_ref=relay.at[k // 4],
            dst_ref=(halo_dn if upward else halo_up).at[:, span],
            send_sem=relay_send.at[k // 4],
            recv_sem=halo_recv.at[k, 0 if upward else 1],
            device_id=relay_to,
            device_id_type=BY_ID,
        )

    def send_halo(k, upward):
        detour = (ends_up if upward else ends_dn) & (k % 4 > 0)

        @pl.when((has_up if upward else has_dn) & jnp.logical_not(detour))
        def _():
            halo_copy(k, upward).start()

        @pl.when(detour)
        def _():
            detour_copy(k, upward).start()

    def out_copy(k, j):
        span = pl.ds(pl.multiple_of(k * part, part), part)
        owner, mate = mates[j]
        return pltpu.make_async_remote_copy(
            src_ref=sent.at[owner, span],
            dst_ref=got.at[j, span],
            send_sem=out_send.at[k, j],
            recv_sem=out_recv.at[k, j],
            device_id=mate,
            device_id_type=BY_ID,
        )

    @pl.when(jnp.logical_not(has_up))
    def _():
        halo_up[...] = jnp.zeros_like(halo_up)
        class_up[...] = jnp.full_like(class_up, -1.0)

    @pl.when(jnp.logical_not(has_dn))
    def _():
        halo_dn[...] = jnp.zeros_like(halo_dn)
        class_dn[...] = jnp.full_like(class_dn, -1.0)

    first = lax.broadcasted_iota(jnp.int32, (width, width), 0)
    second = lax.broadcasted_iota(jnp.int32, (width, width), 1)
    blocks = width // 128
    order = jnp.where(first == (second % 128) * blocks + second // 128, 1.0, 0.0)
    order = order.astype(jnp.bfloat16)
    lines = part * tile_rows
    class_rows = dot(ids_ref[...].astype(jnp.float32).astype(jnp.bfloat16), order)
    for i in range(tile_rows):
        class_ref[i] = jnp.broadcast_to(class_rows[i : i + 1], (SUB, width))

    @pl.when(has_up)
    def _():
        class_copy(True).start()

    @pl.when(has_dn)
    def _():
        class_copy(False).start()

    def prepare(k, none):
        for copy in load(k):
            copy.wait()
        span = pl.ds(pl.multiple_of(k * lines, lines), lines)
        lined = jnp.concatenate([raw[c, span] for c in range(blocks)], axis=1)
        lined = dot_parts(lined, order)
        for c in range(blocks):
            raw[c, span] = lined[:, 128 * c : 128 * c + 128]

        def turn(j, carry):
            first = pl.multiple_of(j * SUB, SUB)
            for i in range(tile_rows):
                for c in range(blocks):
                    rows_own[i, pl.ds(first, SUB), pl.ds(128 * c, 128)] = raw[
                        c, pl.ds(j * (SUB * tile_rows) + i, SUB, stride=tile_rows), :
                    ]
            return carry

        lax.fori_loop(k * (part // SUB), (k + 1) * (part // SUB), turn, 0)

        send_halo(k, True)
        send_halo(k, False)
        return none

    lax.fori_loop(0, CHUNKS, prepare, 0)

    @pl.when(has_up)
    def _():
        class_copy(False).wait_recv()

    @pl.when(has_dn)
    def _():
        class_copy(True).wait_recv()

    keep_up = jnp.where(has_up, 1.0, 0.0).astype(jnp.float32)
    keep_dn = jnp.where(has_dn, 1.0, 0.0).astype(jnp.float32)
    lane = lax.broadcasted_iota(jnp.int32, (SUB, 128), 1)
    left, right = lane == 0, lane == 127
    edge = width - 128

    def next_column(x):
        turned = jnp.where(right, 0.0, pltpu.roll(x[:, :128], 127, 1))
        return jnp.concatenate([x[:, 128:], turned], axis=1)

    def last_column(x, outermost):
        turned = jnp.where(left, outermost[:, :128], pltpu.roll(x[:, edge:], 1, 1))
        return jnp.concatenate([turned, x[:, :edge]], axis=1)

    span_rows = tile_rows + 2 * STEPS

    def advance(k, half_chunk):
        first = pl.multiple_of(k * part + half_chunk * SUB, SUB)
        runs_here = pl.ds(first, SUB)
        picked_here = pl.ds(pl.multiple_of(half_chunk * SUB, SUB), SUB)
        about = about_ref[pl.ds(pl.multiple_of(group * runs + first, SUB), SUB)]
        table = 0.015 * jnp.exp(about[:, :CLASSES] * math.log(1.35))
        steep = jnp.broadcast_to(about[:, CLASSES : CLASSES + 1], (SUB, width))
        pick = jnp.broadcast_to(about[:, CLASSES + 1 : CLASSES + 2], (SUB, width))
        rest = 1.0 - steep
        half = [jnp.broadcast_to(table[:, c : c + 1], (SUB, width)) for c in range(CLASSES)]
        for i in range(span_rows):
            if i < STEPS:
                klass = class_up[i]
            elif i < STEPS + tile_rows:
                klass = class_ref[i - STEPS]
            else:
                klass = class_dn[i - STEPS - tile_rows]
            value = jnp.zeros((SUB, width), jnp.float32)
            for c in range(CLASSES):
                value = jnp.where(klass == float(c), half[c], value)
            kappa[i] = value

        def start_row(i):
            if i < STEPS:
                return halo_up[i, runs_here]
            if i < STEPS + tile_rows:
                return rows_own[i - STEPS, runs_here]
            return halo_dn[i - STEPS - tile_rows, runs_here]

        for step in range(STEPS):
            source = (None, wide_a, wide_b, wide_a)[step]
            sink = (wide_a, wide_b, wide_a, None)[step]

            def row(i):
                return start_row(i) if step == 0 else source[i]

            def spread_of(i, value):
                bottom = 1.0 + value * value
                guess = pl.reciprocal(bottom, approx=True)
                guess = guess * (2.0 - bottom * guess)
                return kappa[i] * (steep + rest * guess)

            above = row(step)
            above_spread = spread_of(step, above)
            centre = row(step + 1)
            spread = spread_of(step + 1, centre)
            flow_in = (above_spread + spread) * (centre - above)
            for i in range(step + 1, span_rows - step - 1):
                below = row(i + 1)
                below_spread = spread_of(i + 1, below)
                flow_out = (spread + below_spread) * (below - centre)
                flow = (spread + next_column(spread)) * (next_column(centre) - centre)
                back = last_column(flow, spread * centre)
                total = centre + (flow_out - flow_in) + (flow - back)
                if i < STEPS:
                    total = total * keep_up
                if i >= STEPS + tile_rows:
                    total = total * keep_dn
                if sink is not None:
                    sink[i] = total
                if STEPS <= i < STEPS + tile_rows:
                    if step > 0:
                        total = jnp.where(pick == step + 1.0, total, picked[i - STEPS, picked_here])
                    picked[i - STEPS, picked_here] = total
                flow_in, centre, spread = flow_out, below, below_spread

    back_order = jnp.where(second == (first % 128) * blocks + first // 128, 1.0, 0.0)
    back_order = back_order.astype(jnp.bfloat16)

    def one_chunk(k, none):
        for upward in (False, True):
            for slot in range(2):
                @pl.when(is_relay & (xl == int(upward)) & (k == 2 * slot))
                def _():
                    passed = relay_path + 4 * slot
                    forward = forward_copy(passed, upward)
                    detour_copy(passed, upward).wait_recv()
                    forward.start()

        @pl.when(has_up)
        def _():
            halo_copy(k, False).wait_recv()

        @pl.when(has_dn)
        def _():
            halo_copy(k, True).wait_recv()

        def half_of(half_chunk, carry):
            advance(k, half_chunk)
            return carry

        lax.fori_loop(0, part // SUB, half_of, 0)
        lined = dot_parts(picked[...].reshape(tile_rows * part, width), back_order)
        span = pl.ds(pl.multiple_of(k * part, part), part)
        for i in range(tile_rows):
            sent[i // 4, span, pl.ds((i % 4) * width, width)] = lined[i * part : (i + 1) * part]
        for j in range(3):
            out_copy(k, j).start()
        return none

    lax.fori_loop(0, CHUNKS, one_chunk, 0)

    cells = weight.shape[1]
    hid = weight.shape[0]
    all_runs = hidden.shape[0]
    block = 256
    f32, bf16 = jnp.float32, jnp.bfloat16
    eye = lax.broadcasted_iota(jnp.int32, (block, block), 0) == lax.broadcasted_iota(
        jnp.int32, (block, block), 1
    )
    share = 2.0 / all_runs
    eye = jnp.where(eye, -0.5 * share, 0.0).astype(bf16)
    about = about_ref[...]
    steep_all = about[:, CLASSES : CLASSES + 1]
    feats = input_ref.shape[0]
    onehots = CLASSES * LEVELS
    entry = lax.broadcasted_iota(jnp.int32, (16, feats), 0)
    column = lax.broadcasted_iota(jnp.int32, (16, feats), 1)
    source = jnp.where(column < onehots, column // LEVELS, CLASSES + 1)
    spread_out = dot(about.astype(bf16), jnp.where(entry == source, 1.0, 0.0).astype(bf16))
    column = lax.broadcasted_iota(jnp.int32, (all_runs, feats), 1)
    wanted = jnp.where(column < onehots, column % LEVELS, column - onehots + 1)
    wanted = jnp.where(column < onehots + STEPS, wanted, -1).astype(f32)
    onehot = jnp.where(spread_out == wanted, 1.0, 0.0).astype(bf16)

    def independent(rows):
        count = rows.shape[0]
        kept = LEVELS - 1
        levels_end, moments_end = CLASSES * kept, CLASSES * kept + STEPS - 1
        high, middle = two_parts(rows)
        low = (rows - high.astype(f32) - middle.astype(f32)).astype(bf16)
        line = lax.broadcasted_iota(jnp.int32, (64, 16), 0)
        entry = lax.broadcasted_iota(jnp.int32, (64, 16), 1)
        source = jnp.where(line < levels_end, line // kept, CLASSES + 1)
        source = jnp.where(line > moments_end, CLASSES, source)

        def chosen(last, extra):
            keep = (entry == source) & ((line < last) | (line == extra))
            return jnp.where(keep, 1.0, 0.0).astype(bf16)

        value = (
            dot_turned(chosen(moments_end, moments_end + 1), high)
            + dot_turned(chosen(0, moments_end + 2), middle)
            + dot_turned(chosen(0, moments_end + 3), low)
        )
        line = lax.broadcasted_iota(jnp.int32, (64, count), 0)
        wanted = jnp.where(line < levels_end, line % kept, line - levels_end + 1).astype(f32)
        marks = jnp.where(value == wanted, 1.0, 0.0)
        value = jnp.where(line < moments_end, marks, value)
        return jnp.where(line == moments_end, 1.0, value).astype(bf16)

    def hidden_block(n, none):
        span = pl.ds(pl.multiple_of(n * block, block), block)
        value = input_ref[:, span]
        high, low = two_parts(value)
        rest = (value - high.astype(f32) - low.astype(f32)).astype(bf16)
        pre = dot(onehot, high) + (dot(onehot, low) + dot(onehot, rest))
        pre = pre + steep_all * value[value.shape[0] - 1 :, :]
        logistic = 1.0 / (1.0 + jnp.exp(-pre))
        active = (pre * logistic).astype(bf16)
        hidden[:, span] = active
        gain[:, span] = logistic * (1.0 + pre * (1.0 - logistic)) * share
        turned[span, :] = dot_turned(eye, active).astype(bf16)
        return none

    lax.fori_loop(0, hid // block, hidden_block, 0)
    turned_copy = pltpu.make_async_copy(turned, turned_ref, keep_sem.at[0])
    turned_copy.start()
    weight_load.wait()

    def pred_block(n, none):
        span = pl.ds(pl.multiple_of(n * block, block), block)
        pred[:, span] = dot(hidden[...], weight[:, span]) + bias_ref[:, span]
        return none

    lax.fori_loop(0, cells // block, pred_block, 0)

    def compare(source, group_at, start, count, copy_row):
        def some(b, none):
            inner = pl.multiple_of(start + b * 16, 16)
            at_run = pl.ds(pl.multiple_of(group_at * runs + inner, 16), 16)
            value = (pred[at_run] - source[pl.ds(inner, 16)]).astype(bf16)
            misfit[at_run] = value
            if copy_row is not None:
                misfit_far[pl.ds(pl.multiple_of(copy_row + b * 16, 16), 16)] = value
            return none

        lax.fori_loop(0, count // 16, some, 0)

    for k in range(CHUNKS):
        out_copy(k, 0).wait_recv()
    compare(sent.at[group], group, 0, runs, None)
    compare(got.at[0], mates[0][0], 0, runs, None)
    near = pl.ds(pl.multiple_of(here["xh"] * (2 * runs), 2 * runs), 2 * runs)
    far = (1 - here["xh"]) * (2 * runs)

    near_mix = independent(about_ref[near])

    def near_block(n, none):
        span = pl.ds(pl.multiple_of(n * block, block), block)
        back = dot_turned(misfit[near], weight[span, :]) * gain[near, span]
        high, low = two_parts(back)
        grad[:, span] = dot(near_mix, high) + dot(near_mix, low)
        return none

    lax.fori_loop(0, hid // block, near_block, 0)
    near_copy = pltpu.make_async_copy(misfit.at[near], misfit_ref.at[near], keep_sem.at[1])
    near_copy.start()

    half = runs // 2
    for h in range(2):
        for k in range(h * CHUNKS // 2, (h + 1) * CHUNKS // 2):
            out_copy(k, 1).wait_recv()
            out_copy(k, 2).wait_recv()
        for j in (1, 2):
            at_row = here["core"] if j == 1 else 1 - here["core"]
            compare(got.at[j], mates[j][0], h * half, half, at_row * half)

        far_rows = [pl.ds(pl.multiple_of(far + g * runs + h * half, half), half) for g in range(2)]
        mix = independent(jnp.concatenate([about_ref[rows] for rows in far_rows], axis=0))

        def far_block(n, none):
            span = pl.ds(pl.multiple_of(n * block, block), block)
            factor = jnp.concatenate([gain[rows, span] for rows in far_rows], axis=0)
            back = dot_turned(misfit_far[...], weight[span, :]) * factor
            high, low = two_parts(back)
            grad[:, span] += dot(mix, high) + dot(mix, low)
            return none

        lax.fori_loop(0, hid // block, far_block, 0)

    far_span = pl.ds(pl.multiple_of(far, 2 * runs), 2 * runs)
    far_copy = pltpu.make_async_copy(misfit.at[far_span], misfit_ref.at[far_span], keep_sem.at[2])
    far_copy.start()
    for i in range(tiles.shape[0]):
        r, c = i // (hid // 128), i % (hid // 128)
        tiles[i] = grad[8 * r : 8 * r + 8, 128 * c : 128 * c + 128]

    def sum_copy(stage, source, sink, device):
        return pltpu.make_async_remote_copy(
            src_ref=source,
            dst_ref=sink,
            send_sem=sum_send.at[stage],
            recv_sem=sum_recv.at[stage],
            device_id=device,
            device_id_type=BY_ID,
        )

    core, z = here["core"], here["z"]
    mate = at(here, core=1 - core)
    share_of = 4
    chips = own.shape[0]
    swap = sum_copy(0, tiles.at[pl.ds((1 - core) * chips, chips)], pair, mate)
    swap.start()
    swap.wait_recv()
    own[...] = tiles[pl.ds(core * chips, chips)] + pair[...]

    def scatter(j, none):
        other = (plane + j) % 16
        sum_copy(
            1,
            own.at[pl.ds(other * share_of, share_of)],
            landed.at[pl.ds((j - 1) * share_of, share_of)],
            in_plane(other),
        ).start()
        return none

    lax.fori_loop(1, 16, scatter, 0)
    scattered = sum_copy(1, own.at[pl.ds(0, 15 * share_of)], landed, mate)
    scattered.wait_recv()
    total = own[pl.ds(plane * share_of, share_of)]
    for j in range(15):
        total = total + landed[j * share_of : (j + 1) * share_of]
    middle[...] = total
    for j in range(1, 4):
        other = (z + j) % 4
        sum_copy(2, middle.at[other], landed_z.at[j - 1], at(here, z=other)).start()
    scattered_z = sum_copy(2, middle.at[pl.ds(0, 3)], landed_z, mate)
    scattered_z.wait_recv()
    mine[...] = middle[z] + (landed_z[0] + landed_z[1] + landed_z[2])
    slot = core * chips + plane * share_of
    sums_ref[slot + z] = mine[...]
    for j in range(1, 4):
        sum_copy(3, mine, sums_ref.at[slot + z], at(here, z=(z + j) % 4)).start()
    gathered_z = sum_copy(3, middle.at[pl.ds(0, 3)], landed_z, mate)
    gathered_z.wait_recv()
    quad = pl.ds(slot, share_of)

    def gather(j, none):
        sum_copy(4, sums_ref.at[quad], sums_ref.at[quad], in_plane((plane + j) % 16)).start()
        return none

    lax.fori_loop(1, 16, gather, 0)
    gathered = sum_copy(4, own.at[pl.ds(0, 15 * share_of)], landed, mate)
    gathered.wait_recv()
    half_sums = sums_ref.at[pl.ds(core * chips, chips)]
    last = sum_copy(5, half_sums, half_sums, mate)
    last.start()
    last.wait()
    for copy in (swap, scattered, scattered_z, gathered_z, gathered):
        copy.wait_send()

    @pl.when(is_relay)
    def _():
        for slot in range(2):
            forward_copy(relay_path + 4 * slot, False).wait_send()

    turned_copy.wait()
    near_copy.wait()
    far_copy.wait()
    for k in range(CHUNKS):
        for j in range(3):
            out_copy(k, j).wait_send()

    @pl.when(has_up)
    def _():
        class_copy(True).wait_send()
        for k in range(CHUNKS):
            halo_copy(k, True).wait_send()

    @pl.when(has_dn)
    def _():
        class_copy(False).wait_send()
        for k in range(CHUNKS):
            halo_copy(k, False).wait_send()


def solve(field, classes, about, input_layer, bias, weight):
    runs, rows, width = field.shape
    hid, cells = weight.shape
    all_runs = about.shape[0]
    f32, bf16 = jnp.float32, jnp.bfloat16
    dma = pltpu.SemaphoreType.DMA
    vmem = pl.BlockSpec(memory_space=pltpu.VMEM)
    anywhere = pl.BlockSpec(memory_space=pl.ANY)
    span = rows + 2 * STEPS
    part = runs // CHUNKS
    return pl.pallas_call(
        solve_kernel,
        out_shape=(
            jax.ShapeDtypeStruct((all_runs, cells), bf16),
            jax.ShapeDtypeStruct((hid, all_runs), bf16),
            jax.ShapeDtypeStruct((hid // 16, 8, 128), f32),
        ),
        in_specs=[anywhere] + [vmem] * 4 + [anywhere],
        out_specs=(anywhere, anywhere, vmem),
        scratch_shapes=[
            pltpu.VMEM((width // 128, runs * rows, 128), f32),
            pltpu.VMEM((rows, runs, width), f32),
            pltpu.VMEM((rows, SUB, width), f32),
            pltpu.VMEM((STEPS, runs, width), f32),
            pltpu.VMEM((STEPS, runs, width), f32),
            pltpu.VMEM((STEPS, SUB, width), f32),
            pltpu.VMEM((STEPS, SUB, width), f32),
            pltpu.VMEM((span, SUB, width), f32),
            pltpu.VMEM((span, SUB, width), f32),
            pltpu.VMEM((span, SUB, width), f32),
            pltpu.VMEM((rows, part, width), f32),
            pltpu.VMEM((4, runs, 4 * width), f32),
            pltpu.VMEM((3, runs, 4 * width), f32),
            pltpu.VMEM((2, STEPS, part, width), f32),
            pltpu.VMEM((hid, cells), bf16),
            pltpu.VMEM((all_runs, hid), bf16),
            pltpu.VMEM((hid, all_runs), bf16),
            pltpu.VMEM((all_runs, hid), f32),
            pltpu.VMEM((all_runs, cells), f32),
            pltpu.VMEM((all_runs, cells), bf16),
            pltpu.VMEM((runs, cells), bf16),
            pltpu.VMEM((64, hid), f32),
            pltpu.VMEM((hid // 16, 8, 128), f32),
            pltpu.VMEM((hid // 32, 8, 128), f32),
            pltpu.VMEM((hid // 32, 8, 128), f32),
            pltpu.VMEM((60, 8, 128), f32),
            pltpu.VMEM((4, 8, 128), f32),
            pltpu.VMEM((3, 8, 128), f32),
            pltpu.VMEM((8, 128), f32),
            dma((CHUNKS, 4)),
            dma((CHUNKS, 2)),
            dma((CHUNKS, 2)),
            dma((2,)),
            dma((2,)),
            dma((CHUNKS, 3)),
            dma((CHUNKS, 3)),
            dma((3,)),
            dma,
            dma((2,)),
            dma((2,)),
            dma((6,)),
            dma((6,)),
        ],
        compiler_params=pltpu.CompilerParams(
            collective_id=1, has_side_effects=True, vmem_limit_bytes=58 * MIB
        ),
        name="solve",
    )(
        field.reshape(runs * rows, width), classes, about, input_layer, bias, weight,
    )


def update_kernel(
    turned_ref, misfit_ref, weight_ref, bias_ref, sums_ref, input_ref,
    next_ref, misfit_out_ref, bias_out_ref, input_out_ref,
):
    f32, bf16 = jnp.float32, jnp.bfloat16
    step = 1.0 / misfit_ref.shape[0]
    block = 256

    def columns(n, none):
        span = pl.ds(pl.multiple_of(n * block, block), block)
        change = dot(turned_ref[...], misfit_ref[:, span])
        next_ref[:, span] = (weight_ref[:, span].astype(f32) + change).astype(bf16)
        return none

    lax.fori_loop(0, misfit_ref.shape[1] // block, columns, 0, unroll=True)
    rows = misfit_out_ref.shape[0]
    here = pl.multiple_of(pl.program_id(0) * rows, rows)
    value = misfit_ref[pl.ds(here, rows)]
    misfit_out_ref[...] = value

    @pl.when(pl.program_id(0) == 0)
    def _():
        bias_out_ref[...] = bias_ref[...]
        feats, hid = input_ref.shape
        kept = LEVELS - 1
        levels_end, moments_end = CLASSES * kept, CLASSES * kept + STEPS - 1
        row = lax.broadcasted_iota(jnp.int32, (feats, 64), 0)
        line = lax.broadcasted_iota(jnp.int32, (feats, 64), 1)
        group = jnp.where(row < CLASSES * LEVELS, row // LEVELS, CLASSES)
        inner = row - group * LEVELS
        length = jnp.where(group < CLASSES, kept, STEPS - 1)
        line_group = jnp.where(line < levels_end, line // kept, CLASSES)
        line_inner = line - line_group * kept
        same = (group == line_group) & (line < moments_end)
        mix = jnp.where(same & (inner == line_inner), 1.0, 0.0)
        mix = jnp.where(inner == length, jnp.where(same, -1.0, mix), mix)
        mix = jnp.where((inner == length) & (line == moments_end), 1.0, mix)
        steep = jnp.where((line > moments_end) & (line <= moments_end + 3), 1.0, 0.0)
        mix = jnp.where(row == feats - 1, steep, mix).astype(bf16)
        across = hid // 128
        for c in range(across):
            sums = jnp.concatenate([sums_ref[r * across + c] for r in range(8)], axis=0)
            high, middle = two_parts(sums)
            low = (sums - high.astype(f32) - middle.astype(f32)).astype(bf16)
            grad = dot(mix, high) + (dot(mix, middle) + dot(mix, low))
            span = slice(128 * c, 128 * c + 128)
            input_out_ref[:, span] = input_ref[:, span] - 2.0 * grad

    bias_out_ref[...] -= step * jnp.sum(value.astype(f32), axis=0, keepdims=True)


def update(turned, misfit, weight, bias, sums, input_layer):
    hid, cells = weight.shape
    runs = misfit.shape[0]
    steps = 4
    whole = pl.BlockSpec((runs, cells), lambda i: (0, 0))
    line = pl.BlockSpec((1, cells), lambda i: (0, 0))
    layer = pl.BlockSpec(input_layer.shape, lambda i: (0, 0))
    all_sums = pl.BlockSpec(sums.shape, lambda i: (0, 0, 0))
    tile = pl.BlockSpec((hid // steps, cells), lambda i: (i, 0))
    return pl.pallas_call(
        update_kernel,
        grid=(steps,),
        out_shape=(
            jax.ShapeDtypeStruct(weight.shape, weight.dtype),
            jax.ShapeDtypeStruct(misfit.shape, misfit.dtype),
            jax.ShapeDtypeStruct(bias.shape, bias.dtype),
            jax.ShapeDtypeStruct(input_layer.shape, input_layer.dtype),
        ),
        in_specs=[pl.BlockSpec((hid // steps, runs), lambda i: (i, 0)), whole, tile, line, all_sums, layer],
        out_specs=(tile, pl.BlockSpec((runs // steps, cells), lambda i: (i, 0)), line, layer),
        compiler_params=pltpu.CompilerParams(vmem_limit_bytes=60 * MIB),
        cost_estimate=pl.CostEstimate(
            flops=2 * hid * cells * runs, bytes_accessed=4 * hid * cells, transcendentals=0
        ),
        name="update",
    )(turned, misfit, weight, bias, sums, input_layer)


def update_kernel(
    turned_ref, misfit_ref, weight_ref, bias_ref, sums_ref, input_ref,
    next_ref, misfit_out_ref, bias_out_ref, input_out_ref,
):
    f32, bf16 = jnp.float32, jnp.bfloat16
    step = 1.0 / misfit_ref.shape[0]
    block = 256

    def columns(n, none):
        span = pl.ds(pl.multiple_of(n * block, block), block)
        change = dot(turned_ref[...], misfit_ref[:, span])
        next_ref[:, span] = (weight_ref[:, span].astype(f32) + change).astype(bf16)
        return none

    lax.fori_loop(0, misfit_ref.shape[1] // block, columns, 0, unroll=True)
    rows = misfit_out_ref.shape[0]
    here = pl.multiple_of(pl.program_id(0) * rows, rows)
    value = misfit_ref[pl.ds(here, rows)]
    misfit_out_ref[...] = value

    @pl.when(pl.program_id(0) == 0)
    def _():
        bias_out_ref[...] = bias_ref[...]
        feats, hid = input_ref.shape
        kept = LEVELS - 1
        levels_end, moments_end = CLASSES * kept, CLASSES * kept + STEPS - 1
        row = lax.broadcasted_iota(jnp.int32, (feats, 64), 0)
        line = lax.broadcasted_iota(jnp.int32, (feats, 64), 1)
        group = jnp.where(row < CLASSES * LEVELS, row // LEVELS, CLASSES)
        inner = row - group * LEVELS
        length = jnp.where(group < CLASSES, kept, STEPS - 1)
        line_group = jnp.where(line < levels_end, line // kept, CLASSES)
        line_inner = line - line_group * kept
        same = (group == line_group) & (line < moments_end)
        mix = jnp.where(same & (inner == line_inner), 1.0, 0.0)
        mix = jnp.where(inner == length, jnp.where(same, -1.0, mix), mix)
        mix = jnp.where((inner == length) & (line == moments_end), 1.0, mix)
        steep = jnp.where((line > moments_end) & (line <= moments_end + 3), 1.0, 0.0)
        mix = jnp.where(row == feats - 1, steep, mix).astype(bf16)
        across = hid // 128
        for c in range(across):
            sums = jnp.concatenate([sums_ref[r * across + c] for r in range(8)], axis=0)
            high, middle = two_parts(sums)
            low = (sums - high.astype(f32) - middle.astype(f32)).astype(bf16)
            grad = dot(mix, high) + (dot(mix, middle) + dot(mix, low))
            span = slice(128 * c, 128 * c + 128)
            input_out_ref[:, span] = input_ref[:, span] - 2.0 * grad

    bias_out_ref[...] -= step * jnp.sum(value.astype(f32), axis=0, keepdims=True)


def update(turned, misfit, weight, bias, sums, input_layer):
    hid, cells = weight.shape
    runs = misfit.shape[0]
    steps = 4
    whole = pl.BlockSpec((runs, cells), lambda i: (0, 0))
    line = pl.BlockSpec((1, cells), lambda i: (0, 0))
    layer = pl.BlockSpec(input_layer.shape, lambda i: (0, 0))
    all_sums = pl.BlockSpec(sums.shape, lambda i: (0, 0, 0))
    tile = pl.BlockSpec((hid // steps, cells), lambda i: (i, 0))
    return pl.pallas_call(
        update_kernel,
        grid=(steps,),
        out_shape=(
            jax.ShapeDtypeStruct(weight.shape, weight.dtype),
            jax.ShapeDtypeStruct(misfit.shape, misfit.dtype),
            jax.ShapeDtypeStruct(bias.shape, bias.dtype),
            jax.ShapeDtypeStruct(input_layer.shape, input_layer.dtype),
        ),
        in_specs=[pl.BlockSpec((hid // steps, runs), lambda i: (i, 0)), whole, tile, line, all_sums, layer],
        out_specs=(tile, pl.BlockSpec((runs // steps, cells), lambda i: (i, 0)), line, layer),
        compiler_params=pltpu.CompilerParams(vmem_limit_bytes=60 * MIB),
        cost_estimate=pl.CostEstimate(
            flops=2 * hid * cells * runs, bytes_accessed=4 * hid * cells, transcendentals=0
        ),
        name="update",
    )(turned, misfit, weight, bias, sums, input_layer)


def sum_kernel(
    part_ref, out_ref, pair, own, landed, mine,
    pair_send, pair_recv, part_send, part_recv, back_send, back_recv, last_send, last_recv,
):
    here = place()
    core = here["core"]
    chips = own.shape[0]
    chip = here["xh"] * 32 + here["xl"] * 16 + here["y"] * 4 + here["z"]
    mate = at(here, core=1 - core)

    def device(k):
        return (k // 32, core, (k // 16) % 2, (k // 4) % 4, k % 4)

    barrier = pltpu.get_barrier_semaphore()
    pl.semaphore_signal(barrier, inc=1, device_id=mate, device_id_type=BY_ID)

    def greet(j, carry):
        pl.semaphore_signal(
            barrier, inc=1, device_id=device((chip + j) % chips), device_id_type=BY_ID
        )
        return carry

    lax.fori_loop(1, chips, greet, 0)
    pl.semaphore_wait(barrier, chips)

    swap = pltpu.make_async_remote_copy(
        src_ref=part_ref.at[pl.ds((1 - core) * chips, chips)],
        dst_ref=pair,
        send_sem=pair_send,
        recv_sem=pair_recv,
        device_id=mate,
        device_id_type=BY_ID,
    )
    swap.start()
    swap.wait_recv()
    own[...] = part_ref[pl.ds(core * chips, chips)] + pair[...]

    def scatter(j, carry):
        other = (chip + j) % chips
        pltpu.make_async_remote_copy(
            src_ref=own.at[other],
            dst_ref=landed.at[j - 1],
            send_sem=part_send,
            recv_sem=part_recv,
            device_id=device(other),
            device_id_type=BY_ID,
        ).start()
        return carry

    lax.fori_loop(1, chips, scatter, 0)
    total = own[chip]
    whole = pltpu.make_async_remote_copy(
        src_ref=own.at[pl.ds(0, chips - 1)],
        dst_ref=landed,
        send_sem=part_send,
        recv_sem=part_recv,
        device_id=mate,
        device_id_type=BY_ID,
    )
    whole.wait_recv()
    mine[...] = total + jnp.sum(landed[...], axis=0)

    slot = core * chips + chip
    out_ref[slot] = mine[...]

    def spread(j, carry):
        pltpu.make_async_remote_copy(
            src_ref=mine,
            dst_ref=out_ref.at[slot],
            send_sem=back_send,
            recv_sem=back_recv,
            device_id=device((chip + j) % chips),
            device_id_type=BY_ID,
        ).start()
        return carry

    lax.fori_loop(1, chips, spread, 0)
    gathered = pltpu.make_async_remote_copy(
        src_ref=own.at[pl.ds(0, chips - 1)],
        dst_ref=landed,
        send_sem=back_send,
        recv_sem=back_recv,
        device_id=mate,
        device_id_type=BY_ID,
    )
    gathered.wait_recv()
    half = pl.ds(core * chips, chips)
    last = pltpu.make_async_remote_copy(
        src_ref=out_ref.at[half],
        dst_ref=out_ref.at[half],
        send_sem=last_send,
        recv_sem=last_recv,
        device_id=mate,
        device_id_type=BY_ID,
    )
    last.start()
    last.wait()
    swap.wait_send()
    whole.wait_send()
    gathered.wait_send()


def sum_everywhere(part):
    tiles = part.shape[0]
    f32 = jnp.float32
    dma = pltpu.SemaphoreType.DMA
    vmem = pl.BlockSpec(memory_space=pltpu.VMEM)
    tile = part.shape[1:]
    return pl.pallas_call(
        sum_kernel,
        out_shape=jax.ShapeDtypeStruct(part.shape, f32),
        in_specs=[vmem],
        out_specs=vmem,
        scratch_shapes=[
            pltpu.VMEM((tiles // 2,) + tile, f32),
            pltpu.VMEM((tiles // 2,) + tile, f32),
            pltpu.VMEM((tiles // 2 - 1,) + tile, f32),
            pltpu.VMEM(tile, f32),
        ] + [dma] * 8,
        compiler_params=pltpu.CompilerParams(
            collective_id=2, has_side_effects=True, vmem_limit_bytes=16 * MIB
        ),
        name="sum_everywhere",
    )(part)


def on_device(
    start_field, class_ids, run_levels, steepness, step_pick, input_layer, output_layer, output_bias
):
    f32 = jnp.float32
    about = jnp.concatenate(
        [
            run_levels.astype(f32),
            steepness[:, None],
            step_pick[:, None].astype(f32),
            jnp.zeros((run_levels.shape[0], 16 - CLASSES - 2), f32),
        ],
        axis=1,
    )
    bias = output_bias[None, :]
    misfit, turned, sums = solve(start_field, class_ids, about, input_layer, bias, output_layer)
    output_next, misfit, bias_next, input_next = update(
        turned, misfit, output_layer, bias, sums, input_layer
    )
    return (misfit, output_next, bias_next[0], input_next)


def solution(mesh):
    split = Mesh(mesh.devices.reshape(2, 2, 2, 4, 4), AXES)
    return jax.shard_map(
        on_device,
        mesh=split,
        in_specs=(
            P(GRP, TILE, None),
            P(TILE, None),
            P(),
            P(),
            P(),
            P(),
            P(None, GRP + TILE),
            P(GRP + TILE),
        ),
        out_specs=(P(None, GRP + TILE), P(None, GRP + TILE), P(GRP + TILE), P()),
        check_vma=False,
    )
```

```python
import math

import jax
import jax.numpy as jnp
from jax import lax
from jax.experimental import pallas as pl
from jax.experimental.pallas import tpu as pltpu
from jax.sharding import Mesh
from jax.sharding import PartitionSpec as P

STEPS = 4
LEVELS = 8
CLASSES = 8
AXES = ("xh", "core", "xl", "y", "z")
GRP = ("xh", "core")
TILE = ("xl", "y", "z")
BY_ID = pl.DeviceIdType.MESH
MIB = 2**20
CHUNKS = 8
SUB = 8


def place():
    return {axis: lax.axis_index(axis) for axis in AXES}


def at(here, **moved):
    return tuple(moved.get(axis, here[axis]) for axis in AXES)


def beside(here, step):
    tile = here["xl"] * 16 + here["y"] * 4 + here["z"] + step
    tile = (tile + 32) % 32
    return at(here, xl=tile // 16, y=(tile // 4) % 4, z=tile % 4)


def dot(a, b):
    return lax.dot_general(a, b, (((1,), (0,)), ((), ())), preferred_element_type=jnp.float32)


def dot_turned(a, b):
    return lax.dot_general(a, b, (((1,), (1,)), ((), ())), preferred_element_type=jnp.float32)


def two_parts(x):
    high = x.astype(jnp.bfloat16)
    return high, (x - high.astype(jnp.float32)).astype(jnp.bfloat16)


def dot_parts(x, order):
    high, low = two_parts(x)
    return dot(high, order) + dot(low, order)


def solve_kernel(
    field_ref, ids_ref, levels_ref, steep_ref, pick_ref, input_ref, bias_ref, weight_ref,
    misfit_ref, turned_ref, sums_ref,
    about_ref, raw, rows_own, class_ref, halo_up, halo_dn, class_up, class_dn, kappa, wide_a, wide_b, picked, sent, got,
    relay, weight, hidden, turned, gain, pred, misfit, misfit_far, grad,
    tiles, pair, own, landed, middle, landed_z, mine,
    load_sem, halo_send, halo_recv, class_send, class_recv, out_send, out_recv, keep_sem, weight_sem,
    relay_send, relay_recv, sum_send, sum_recv,
):
    here = place()
    runs = rows_own.shape[1]
    tile_rows = rows_own.shape[0]
    width = rows_own.shape[2]
    part = runs // CHUNKS
    tile = here["xl"] * 16 + here["y"] * 4 + here["z"]
    group = here["xh"] * 2 + here["core"]
    up, dn = beside(here, -1), beside(here, 1)
    has_up, has_dn = tile > 0, tile < 31
    mates = (
        (here["xh"] * 2 + 1 - here["core"], at(here, core=1 - here["core"])),
        ((1 - here["xh"]) * 2 + here["core"], at(here, xh=1 - here["xh"])),
        ((1 - here["xh"]) * 2 + 1 - here["core"], at(here, xh=1 - here["xh"], core=1 - here["core"])),
    )

    def load(k):
        lines = part * tile_rows
        return [
            pltpu.make_async_copy(
                field_ref.at[pl.ds(k * lines, lines), pl.ds(128 * c, 128)],
                raw.at[c, pl.ds(k * lines, lines)],
                load_sem.at[k, c],
            )
            for c in range(width // 128)
        ]

    for k in range(CHUNKS):
        for copy in load(k):
            copy.start()
    weight_load = pltpu.make_async_copy(weight_ref, weight, weight_sem)
    weight_load.start()

    barrier = pltpu.get_barrier_semaphore()
    for _, mate in mates:
        pl.semaphore_signal(barrier, inc=1, device_id=mate, device_id_type=BY_ID)

    @pl.when(has_up)
    def _():
        pl.semaphore_signal(barrier, inc=1, device_id=up, device_id_type=BY_ID)

    @pl.when(has_dn)
    def _():
        pl.semaphore_signal(barrier, inc=1, device_id=dn, device_id_type=BY_ID)

    xl = here["xl"]
    ends_dn, ends_up = tile == 15, tile == 16
    corner = 3 * (1 - xl)
    relay_path = (here["y"] - corner + 4) % 4
    is_relay = (here["z"] == corner) & (relay_path > 0)
    relay_from = at(here, y=corner)
    relay_to = at(here, xl=1 - xl, y=3 * xl, z=3 * xl)

    @pl.when(is_relay)
    def _():
        for other in (relay_from, relay_to):
            pl.semaphore_signal(barrier, inc=1, device_id=other, device_id_type=BY_ID)

    @pl.when(ends_dn | ends_up)
    def _():
        for side in range(2):
            for p in range(1, 4):
                edge_at = 3 * (1 - side)
                other = at(here, xl=side, y=(edge_at + p) % 4, z=edge_at)
                pl.semaphore_signal(barrier, inc=1, device_id=other, device_id_type=BY_ID)

    plane = here["xh"] * 8 + here["xl"] * 4 + here["y"]

    def in_plane(k):
        return at(here, xh=k // 8, xl=(k // 4) % 2, y=k % 4)

    def greet(j, none):
        other = in_plane((plane + j) % 16)
        pl.semaphore_signal(barrier, inc=1, device_id=other, device_id_type=BY_ID)
        return none

    lax.fori_loop(1, 16, greet, 0)
    for j in range(1, 4):
        other = at(here, z=(here["z"] + j) % 4)
        pl.semaphore_signal(barrier, inc=1, device_id=other, device_id_type=BY_ID)

    callers = 3 + 18 + jnp.where(has_up, 1, 0) + jnp.where(has_dn, 1, 0)
    callers = callers + jnp.where(is_relay, 2, 0)
    callers = callers + jnp.where(ends_dn | ends_up, 6, 0)
    pl.semaphore_wait(barrier, callers)

    def class_copy(upward):
        return pltpu.make_async_remote_copy(
            src_ref=class_ref.at[pl.ds(0 if upward else tile_rows - STEPS, STEPS)],
            dst_ref=class_dn if upward else class_up,
            send_sem=class_send.at[0 if upward else 1],
            recv_sem=class_recv.at[0 if upward else 1],
            device_id=up if upward else dn,
            device_id_type=BY_ID,
        )

    def halo_copy(k, upward):
        span = pl.ds(pl.multiple_of(k * part, part), part)
        return pltpu.make_async_remote_copy(
            src_ref=rows_own.at[pl.ds(0 if upward else tile_rows - STEPS, STEPS), span],
            dst_ref=(halo_dn if upward else halo_up).at[:, span],
            send_sem=halo_send.at[k, 0 if upward else 1],
            recv_sem=halo_recv.at[k, 0 if upward else 1],
            device_id=up if upward else dn,
            device_id_type=BY_ID,
        )

    def detour_copy(k, upward):
        span = pl.ds(pl.multiple_of(k * part, part), part)
        return pltpu.make_async_remote_copy(
            src_ref=rows_own.at[pl.ds(0 if upward else tile_rows - STEPS, STEPS), span],
            dst_ref=relay.at[k // 4],
            send_sem=halo_send.at[k, 0 if upward else 1],
            recv_sem=relay_recv.at[k // 4],
            device_id=at(here, y=(here["y"] + k % 4) % 4),
            device_id_type=BY_ID,
        )

    def forward_copy(k, upward):
        span = pl.ds(pl.multiple_of(k * part, part), part)
        return pltpu.make_async_remote_copy(
            src_ref=relay.at[k // 4],
            dst_ref=(halo_dn if upward else halo_up).at[:, span],
            send_sem=relay_send.at[k // 4],
            recv_sem=halo_recv.at[k, 0 if upward else 1],
            device_id=relay_to,
            device_id_type=BY_ID,
        )

    def send_halo(k, upward):
        detour = (ends_up if upward else ends_dn) & (k % 4 > 0)

        @pl.when((has_up if upward else has_dn) & jnp.logical_not(detour))
        def _():
            halo_copy(k, upward).start()

        @pl.when(detour)
        def _():
            detour_copy(k, upward).start()

    def out_copy(k, j):
        span = pl.ds(pl.multiple_of(k * part, part), part)
        owner, mate = mates[j]
        return pltpu.make_async_remote_copy(
            src_ref=sent.at[owner, span],
            dst_ref=got.at[j, span],
            send_sem=out_send.at[k, j],
            recv_sem=out_recv.at[k, j],
            device_id=mate,
            device_id_type=BY_ID,
        )

    @pl.when(jnp.logical_not(has_up))
    def _():
        halo_up[...] = jnp.zeros_like(halo_up)
        class_up[...] = jnp.full_like(class_up, -1.0)

    @pl.when(jnp.logical_not(has_dn))
    def _():
        halo_dn[...] = jnp.zeros_like(halo_dn)
        class_dn[...] = jnp.full_like(class_dn, -1.0)

    first = lax.broadcasted_iota(jnp.int32, (width, width), 0)
    second = lax.broadcasted_iota(jnp.int32, (width, width), 1)
    blocks = width // 128
    order = jnp.where(first == (second % 128) * blocks + second // 128, 1.0, 0.0)
    order = order.astype(jnp.bfloat16)
    lines = part * tile_rows
    of_run = [
        levels_ref[...].astype(jnp.float32),
        steep_ref[...],
        pick_ref[...].astype(jnp.float32),
        jnp.zeros((128 - CLASSES - 2, about_ref.shape[0]), jnp.float32),
    ]
    about_ref[...] = jnp.concatenate(of_run, axis=0).T[:, : about_ref.shape[1]]
    class_rows = dot(ids_ref[...].astype(jnp.float32).astype(jnp.bfloat16), order)
    for i in range(tile_rows):
        class_ref[i] = jnp.broadcast_to(class_rows[i : i + 1], (SUB, width))

    @pl.when(has_up)
    def _():
        class_copy(True).start()

    @pl.when(has_dn)
    def _():
        class_copy(False).start()

    def prepare(k, none):
        for copy in load(k):
            copy.wait()
        span = pl.ds(pl.multiple_of(k * lines, lines), lines)
        lined = jnp.concatenate([raw[c, span] for c in range(blocks)], axis=1)
        lined = dot_parts(lined, order)
        for c in range(blocks):
            raw[c, span] = lined[:, 128 * c : 128 * c + 128]

        def turn(j, carry):
            first = pl.multiple_of(j * SUB, SUB)
            for i in range(tile_rows):
                for c in range(blocks):
                    rows_own[i, pl.ds(first, SUB), pl.ds(128 * c, 128)] = raw[
                        c, pl.ds(j * (SUB * tile_rows) + i, SUB, stride=tile_rows), :
                    ]
            return carry

        lax.fori_loop(k * (part // SUB), (k + 1) * (part // SUB), turn, 0)

        send_halo(k, True)
        send_halo(k, False)
        return none

    lax.fori_loop(0, CHUNKS, prepare, 0)

    @pl.when(has_up)
    def _():
        class_copy(False).wait_recv()

    @pl.when(has_dn)
    def _():
        class_copy(True).wait_recv()

    keep_up = jnp.where(has_up, 1.0, 0.0).astype(jnp.float32)
    keep_dn = jnp.where(has_dn, 1.0, 0.0).astype(jnp.float32)
    lane = lax.broadcasted_iota(jnp.int32, (SUB, 128), 1)
    left, right = lane == 0, lane == 127
    edge = width - 128

    def next_column(x):
        turned = jnp.where(right, 0.0, pltpu.roll(x[:, :128], 127, 1))
        return jnp.concatenate([x[:, 128:], turned], axis=1)

    def last_column(x, outermost):
        turned = jnp.where(left, outermost[:, :128], pltpu.roll(x[:, edge:], 1, 1))
        return jnp.concatenate([turned, x[:, :edge]], axis=1)

    span_rows = tile_rows + 2 * STEPS

    def advance(k, half_chunk):
        first = pl.multiple_of(k * part + half_chunk * SUB, SUB)
        runs_here = pl.ds(first, SUB)
        picked_here = pl.ds(pl.multiple_of(half_chunk * SUB, SUB), SUB)
        about = about_ref[pl.ds(pl.multiple_of(group * runs + first, SUB), SUB)]
        table = 0.015 * jnp.exp(about[:, :CLASSES] * math.log(1.35))
        steep = jnp.broadcast_to(about[:, CLASSES : CLASSES + 1], (SUB, width))
        pick = jnp.broadcast_to(about[:, CLASSES + 1 : CLASSES + 2], (SUB, width))
        rest = 1.0 - steep
        half = [jnp.broadcast_to(table[:, c : c + 1], (SUB, width)) for c in range(CLASSES)]
        for i in range(span_rows):
            if i < STEPS:
                klass = class_up[i]
            elif i < STEPS + tile_rows:
                klass = class_ref[i - STEPS]
            else:
                klass = class_dn[i - STEPS - tile_rows]
            value = jnp.zeros((SUB, width), jnp.float32)
            for c in range(CLASSES):
                value = jnp.where(klass == float(c), half[c], value)
            kappa[i] = value

        def start_row(i):
            if i < STEPS:
                return halo_up[i, runs_here]
            if i < STEPS + tile_rows:
                return rows_own[i - STEPS, runs_here]
            return halo_dn[i - STEPS - tile_rows, runs_here]

        for step in range(STEPS):
            source = (None, wide_a, wide_b, wide_a)[step]
            sink = (wide_a, wide_b, wide_a, None)[step]

            def row(i):
                return start_row(i) if step == 0 else source[i]

            def spread_of(i, value):
                bottom = 1.0 + value * value
                guess = pl.reciprocal(bottom, approx=True)
                guess = guess * (2.0 - bottom * guess)
                return kappa[i] * (steep + rest * guess)

            above = row(step)
            above_spread = spread_of(step, above)
            centre = row(step + 1)
            spread = spread_of(step + 1, centre)
            flow_in = (above_spread + spread) * (centre - above)
            for i in range(step + 1, span_rows - step - 1):
                below = row(i + 1)
                below_spread = spread_of(i + 1, below)
                flow_out = (spread + below_spread) * (below - centre)
                flow = (spread + next_column(spread)) * (next_column(centre) - centre)
                back = last_column(flow, spread * centre)
                total = centre + (flow_out - flow_in) + (flow - back)
                if i < STEPS:
                    total = total * keep_up
                if i >= STEPS + tile_rows:
                    total = total * keep_dn
                if sink is not None:
                    sink[i] = total
                if STEPS <= i < STEPS + tile_rows:
                    if step > 0:
                        total = jnp.where(pick == step + 1.0, total, picked[i - STEPS, picked_here])
                    picked[i - STEPS, picked_here] = total
                flow_in, centre, spread = flow_out, below, below_spread

    back_order = jnp.where(second == (first % 128) * blocks + first // 128, 1.0, 0.0)
    back_order = back_order.astype(jnp.bfloat16)

    def one_chunk(k, none):
        for upward in (False, True):
            for slot in range(CHUNKS // 4):
                @pl.when(is_relay & (xl == int(upward)) & (k == 2 * slot))
                def _():
                    passed = relay_path + 4 * slot
                    forward = forward_copy(passed, upward)
                    detour_copy(passed, upward).wait_recv()
                    forward.start()

        @pl.when(has_up)
        def _():
            halo_copy(k, False).wait_recv()

        @pl.when(has_dn)
        def _():
            halo_copy(k, True).wait_recv()

        def half_of(half_chunk, carry):
            advance(k, half_chunk)
            return carry

        lax.fori_loop(0, part // SUB, half_of, 0)
        lined = dot_parts(picked[...].reshape(tile_rows * part, width), back_order)
        span = pl.ds(pl.multiple_of(k * part, part), part)
        for i in range(tile_rows):
            sent[i // 4, span, pl.ds((i % 4) * width, width)] = lined[i * part : (i + 1) * part]
        for j in range(3):
            out_copy(k, j).start()
        return none

    lax.fori_loop(0, CHUNKS, one_chunk, 0)

    cells = weight.shape[1]
    hid = weight.shape[0]
    all_runs = hidden.shape[0]
    block = 256
    f32, bf16 = jnp.float32, jnp.bfloat16
    eye = lax.broadcasted_iota(jnp.int32, (block, block), 0) == lax.broadcasted_iota(
        jnp.int32, (block, block), 1
    )
    share = 2.0 / all_runs
    eye = jnp.where(eye, -0.5 * share, 0.0).astype(bf16)
    about = about_ref[...]
    steep_all = about[:, CLASSES : CLASSES + 1]
    feats = input_ref.shape[0]
    onehots = CLASSES * LEVELS
    entry = lax.broadcasted_iota(jnp.int32, (16, feats), 0)
    column = lax.broadcasted_iota(jnp.int32, (16, feats), 1)
    source = jnp.where(column < onehots, column // LEVELS, CLASSES + 1)
    spread_out = dot(about.astype(bf16), jnp.where(entry == source, 1.0, 0.0).astype(bf16))
    column = lax.broadcasted_iota(jnp.int32, (all_runs, feats), 1)
    wanted = jnp.where(column < onehots, column % LEVELS, column - onehots + 1)
    wanted = jnp.where(column < onehots + STEPS, wanted, -1).astype(f32)
    onehot = jnp.where(spread_out == wanted, 1.0, 0.0).astype(bf16)

    def independent(rows):
        count = rows.shape[0]
        kept = LEVELS - 1
        levels_end, moments_end = CLASSES * kept, CLASSES * kept + STEPS - 1
        high, middle = two_parts(rows)
        low = (rows - high.astype(f32) - middle.astype(f32)).astype(bf16)
        line = lax.broadcasted_iota(jnp.int32, (64, 16), 0)
        entry = lax.broadcasted_iota(jnp.int32, (64, 16), 1)
        source = jnp.where(line < levels_end, line // kept, CLASSES + 1)
        source = jnp.where(line > moments_end, CLASSES, source)

        def chosen(last, extra):
            keep = (entry == source) & ((line < last) | (line == extra))
            return jnp.where(keep, 1.0, 0.0).astype(bf16)

        value = (
            dot_turned(chosen(moments_end, moments_end + 1), high)
            + dot_turned(chosen(0, moments_end + 2), middle)
            + dot_turned(chosen(0, moments_end + 3), low)
        )
        line = lax.broadcasted_iota(jnp.int32, (64, count), 0)
        wanted = jnp.where(line < levels_end, line % kept, line - levels_end + 1).astype(f32)
        marks = jnp.where(value == wanted, 1.0, 0.0)
        value = jnp.where(line < moments_end, marks, value)
        return jnp.where(line == moments_end, 1.0, value).astype(bf16)

    def hidden_block(n, none):
        span = pl.ds(pl.multiple_of(n * block, block), block)
        value = input_ref[:, span]
        high, low = two_parts(value)
        rest = (value - high.astype(f32) - low.astype(f32)).astype(bf16)
        pre = dot(onehot, high) + (dot(onehot, low) + dot(onehot, rest))
        pre = pre + steep_all * value[value.shape[0] - 1 :, :]
        logistic = 1.0 / (1.0 + jnp.exp(-pre))
        active = (pre * logistic).astype(bf16)
        hidden[:, span] = active
        gain[:, span] = logistic * (1.0 + pre * (1.0 - logistic)) * share
        turned[span, :] = dot_turned(eye, active).astype(bf16)
        return none

    lax.fori_loop(0, hid // block, hidden_block, 0)
    turned_copy = pltpu.make_async_copy(turned, turned_ref, keep_sem.at[0])
    turned_copy.start()
    weight_load.wait()

    def pred_block(n, none):
        span = pl.ds(pl.multiple_of(n * block, block), block)
        pred[:, span] = dot(hidden[...], weight[:, span]) + bias_ref[:, span]
        return none

    lax.fori_loop(0, cells // block, pred_block, 0)

    def compare(source, group_at, start, count, copy_row):
        def some(b, none):
            inner = pl.multiple_of(start + b * 16, 16)
            at_run = pl.ds(pl.multiple_of(group_at * runs + inner, 16), 16)
            value = (pred[at_run] - source[pl.ds(inner, 16)]).astype(bf16)
            misfit[at_run] = value
            if copy_row is not None:
                misfit_far[pl.ds(pl.multiple_of(copy_row + b * 16, 16), 16)] = value
            return none

        lax.fori_loop(0, count // 16, some, 0)

    for k in range(CHUNKS):
        out_copy(k, 0).wait_recv()
    compare(sent.at[group], group, 0, runs, None)
    compare(got.at[0], mates[0][0], 0, runs, None)
    near = pl.ds(pl.multiple_of(here["xh"] * (2 * runs), 2 * runs), 2 * runs)
    far = (1 - here["xh"]) * (2 * runs)

    near_mix = independent(about_ref[near])

    def near_block(n, none):
        span = pl.ds(pl.multiple_of(n * block, block), block)
        back = dot_turned(misfit[near], weight[span, :]) * gain[near, span]
        high, low = two_parts(back)
        grad[:, span] = dot(near_mix, high) + dot(near_mix, low)
        return none

    lax.fori_loop(0, hid // block, near_block, 0)
    near_copy = pltpu.make_async_copy(misfit.at[near], misfit_ref.at[near], keep_sem.at[1])
    near_copy.start()

    half = runs // 2
    for h in range(2):
        for k in range(h * CHUNKS // 2, (h + 1) * CHUNKS // 2):
            out_copy(k, 1).wait_recv()
            out_copy(k, 2).wait_recv()
        for j in (1, 2):
            at_row = here["core"] if j == 1 else 1 - here["core"]
            compare(got.at[j], mates[j][0], h * half, half, at_row * half)

        far_rows = [pl.ds(pl.multiple_of(far + g * runs + h * half, half), half) for g in range(2)]
        mix = independent(jnp.concatenate([about_ref[rows] for rows in far_rows], axis=0))

        def far_block(n, none):
            span = pl.ds(pl.multiple_of(n * block, block), block)
            factor = jnp.concatenate([gain[rows, span] for rows in far_rows], axis=0)
            back = dot_turned(misfit_far[...], weight[span, :]) * factor
            high, low = two_parts(back)
            grad[:, span] += dot(mix, high) + dot(mix, low)
            return none

        lax.fori_loop(0, hid // block, far_block, 0)

    far_span = pl.ds(pl.multiple_of(far, 2 * runs), 2 * runs)
    far_copy = pltpu.make_async_copy(misfit.at[far_span], misfit_ref.at[far_span], keep_sem.at[2])
    far_copy.start()
    for i in range(tiles.shape[0]):
        r, c = i // (hid // 128), i % (hid // 128)
        tiles[i] = grad[8 * r : 8 * r + 8, 128 * c : 128 * c + 128]

    def sum_copy(stage, source, sink, device):
        return pltpu.make_async_remote_copy(
            src_ref=source,
            dst_ref=sink,
            send_sem=sum_send.at[stage],
            recv_sem=sum_recv.at[stage],
            device_id=device,
            device_id_type=BY_ID,
        )

    core, z = here["core"], here["z"]
    mate = at(here, core=1 - core)
    share_of = 4
    chips = own.shape[0]
    swap = sum_copy(0, tiles.at[pl.ds((1 - core) * chips, chips)], pair, mate)
    swap.start()
    swap.wait_recv()
    own[...] = tiles[pl.ds(core * chips, chips)] + pair[...]

    def scatter(j, none):
        other = (plane + j) % 16
        sum_copy(
            1,
            own.at[pl.ds(other * share_of, share_of)],
            landed.at[pl.ds((j - 1) * share_of, share_of)],
            in_plane(other),
        ).start()
        return none

    lax.fori_loop(1, 16, scatter, 0)
    scattered = sum_copy(1, own.at[pl.ds(0, 15 * share_of)], landed, mate)
    scattered.wait_recv()
    total = own[pl.ds(plane * share_of, share_of)]
    for j in range(15):
        total = total + landed[j * share_of : (j + 1) * share_of]
    middle[...] = total
    for j in range(1, 4):
        other = (z + j) % 4
        sum_copy(2, middle.at[other], landed_z.at[j - 1], at(here, z=other)).start()
    scattered_z = sum_copy(2, middle.at[pl.ds(0, 3)], landed_z, mate)
    scattered_z.wait_recv()
    mine[...] = middle[z] + (landed_z[0] + landed_z[1] + landed_z[2])
    slot = core * chips + plane * share_of
    sums_ref[slot + z] = mine[...]
    for j in range(1, 4):
        sum_copy(3, mine, sums_ref.at[slot + z], at(here, z=(z + j) % 4)).start()
    gathered_z = sum_copy(3, middle.at[pl.ds(0, 3)], landed_z, mate)
    gathered_z.wait_recv()
    quad = pl.ds(slot, share_of)

    def gather(j, none):
        sum_copy(4, sums_ref.at[quad], sums_ref.at[quad], in_plane((plane + j) % 16)).start()
        return none

    lax.fori_loop(1, 16, gather, 0)
    gathered = sum_copy(4, own.at[pl.ds(0, 15 * share_of)], landed, mate)
    gathered.wait_recv()
    half_sums = sums_ref.at[pl.ds(core * chips, chips)]
    last = sum_copy(5, half_sums, half_sums, mate)
    last.start()
    last.wait()
    for copy in (swap, scattered, scattered_z, gathered_z, gathered):
        copy.wait_send()

    @pl.when(is_relay)
    def _():
        for slot in range(CHUNKS // 4):
            forward_copy(relay_path + 4 * slot, False).wait_send()

    turned_copy.wait()
    near_copy.wait()
    far_copy.wait()
    for k in range(CHUNKS):
        for j in range(3):
            out_copy(k, j).wait_send()

    @pl.when(has_up)
    def _():
        class_copy(True).wait_send()
        for k in range(CHUNKS):
            halo_copy(k, True).wait_send()

    @pl.when(has_dn)
    def _():
        class_copy(False).wait_send()
        for k in range(CHUNKS):
            halo_copy(k, False).wait_send()


def solve(field, classes, levels, steep, pick, input_layer, bias, weight):
    runs, rows, width = field.shape
    hid, cells = weight.shape
    all_runs = levels.shape[1]
    f32, bf16 = jnp.float32, jnp.bfloat16
    dma = pltpu.SemaphoreType.DMA
    vmem = pl.BlockSpec(memory_space=pltpu.VMEM)
    anywhere = pl.BlockSpec(memory_space=pl.ANY)
    span = rows + 2 * STEPS
    part = runs // CHUNKS
    return pl.pallas_call(
        solve_kernel,
        out_shape=(
            jax.ShapeDtypeStruct((all_runs, cells), bf16),
            jax.ShapeDtypeStruct((hid, all_runs), bf16),
            jax.ShapeDtypeStruct((hid // 16, 8, 128), f32),
        ),
        in_specs=[anywhere] + [vmem] * 6 + [anywhere],
        out_specs=(anywhere, anywhere, vmem),
        scratch_shapes=[
            pltpu.VMEM((all_runs, 16), f32),
            pltpu.VMEM((width // 128, runs * rows, 128), f32),
            pltpu.VMEM((rows, runs, width), f32),
            pltpu.VMEM((rows, SUB, width), f32),
            pltpu.VMEM((STEPS, runs, width), f32),
            pltpu.VMEM((STEPS, runs, width), f32),
            pltpu.VMEM((STEPS, SUB, width), f32),
            pltpu.VMEM((STEPS, SUB, width), f32),
            pltpu.VMEM((span, SUB, width), f32),
            pltpu.VMEM((span, SUB, width), f32),
            pltpu.VMEM((span, SUB, width), f32),
            pltpu.VMEM((rows, part, width), f32),
            pltpu.VMEM((4, runs, 4 * width), f32),
            pltpu.VMEM((3, runs, 4 * width), f32),
            pltpu.VMEM((CHUNKS // 4, STEPS, part, width), f32),
            pltpu.VMEM((hid, cells), bf16),
            pltpu.VMEM((all_runs, hid), bf16),
            pltpu.VMEM((hid, all_runs), bf16),
            pltpu.VMEM((all_runs, hid), f32),
            pltpu.VMEM((all_runs, cells), f32),
            pltpu.VMEM((all_runs, cells), bf16),
            pltpu.VMEM((runs, cells), bf16),
            pltpu.VMEM((64, hid), f32),
            pltpu.VMEM((hid // 16, 8, 128), f32),
            pltpu.VMEM((hid // 32, 8, 128), f32),
            pltpu.VMEM((hid // 32, 8, 128), f32),
            pltpu.VMEM((60, 8, 128), f32),
            pltpu.VMEM((4, 8, 128), f32),
            pltpu.VMEM((3, 8, 128), f32),
            pltpu.VMEM((8, 128), f32),
            dma((CHUNKS, 4)),
            dma((CHUNKS, 2)),
            dma((CHUNKS, 2)),
            dma((2,)),
            dma((2,)),
            dma((CHUNKS, 3)),
            dma((CHUNKS, 3)),
            dma((3,)),
            dma,
            dma((CHUNKS // 4,)),
            dma((CHUNKS // 4,)),
            dma((6,)),
            dma((6,)),
        ],
        compiler_params=pltpu.CompilerParams(
            collective_id=1, has_side_effects=True, vmem_limit_bytes=58 * MIB
        ),
        name="solve",
    )(
        field.reshape(runs * rows, width), classes, levels, steep, pick, input_layer, bias, weight,
    )


def update_kernel(
    turned_ref, misfit_ref, weight_ref, bias_ref, sums_ref, input_ref,
    next_ref, misfit_out_ref, bias_out_ref, input_out_ref,
):
    f32, bf16 = jnp.float32, jnp.bfloat16
    step = 1.0 / misfit_ref.shape[0]
    block = 256

    def columns(n, none):
        span = pl.ds(pl.multiple_of(n * block, block), block)
        change = dot(turned_ref[...], misfit_ref[:, span])
        next_ref[:, span] = (weight_ref[:, span].astype(f32) + change).astype(bf16)
        return none

    lax.fori_loop(0, misfit_ref.shape[1] // block, columns, 0, unroll=True)
    rows = misfit_out_ref.shape[0]
    here = pl.multiple_of(pl.program_id(0) * rows, rows)
    value = misfit_ref[pl.ds(here, rows)]
    misfit_out_ref[...] = value

    @pl.when(pl.program_id(0) == 0)
    def _():
        bias_out_ref[...] = bias_ref[...]
        feats, hid = input_ref.shape
        kept = LEVELS - 1
        levels_end, moments_end = CLASSES * kept, CLASSES * kept + STEPS - 1
        row = lax.broadcasted_iota(jnp.int32, (feats, 64), 0)
        line = lax.broadcasted_iota(jnp.int32, (feats, 64), 1)
        group = jnp.where(row < CLASSES * LEVELS, row // LEVELS, CLASSES)
        inner = row - group * LEVELS
        length = jnp.where(group < CLASSES, kept, STEPS - 1)
        line_group = jnp.where(line < levels_end, line // kept, CLASSES)
        line_inner = line - line_group * kept
        same = (group == line_group) & (line < moments_end)
        mix = jnp.where(same & (inner == line_inner), 1.0, 0.0)
        mix = jnp.where(inner == length, jnp.where(same, -1.0, mix), mix)
        mix = jnp.where((inner == length) & (line == moments_end), 1.0, mix)
        steep = jnp.where((line > moments_end) & (line <= moments_end + 3), 1.0, 0.0)
        mix = jnp.where(row == feats - 1, steep, mix).astype(bf16)
        across = hid // 128
        for c in range(across):
            sums = jnp.concatenate([sums_ref[r * across + c] for r in range(8)], axis=0)
            high, middle = two_parts(sums)
            low = (sums - high.astype(f32) - middle.astype(f32)).astype(bf16)
            grad = dot(mix, high) + (dot(mix, middle) + dot(mix, low))
            span = slice(128 * c, 128 * c + 128)
            input_out_ref[:, span] = input_ref[:, span] - 2.0 * grad

    bias_out_ref[...] -= step * jnp.sum(value.astype(f32), axis=0, keepdims=True)


def update(turned, misfit, weight, bias, sums, input_layer):
    hid, cells = weight.shape
    runs = misfit.shape[0]
    steps = 4
    whole = pl.BlockSpec((runs, cells), lambda i: (0, 0))
    line = pl.BlockSpec((1, cells), lambda i: (0, 0))
    layer = pl.BlockSpec(input_layer.shape, lambda i: (0, 0))
    all_sums = pl.BlockSpec(sums.shape, lambda i: (0, 0, 0))
    tile = pl.BlockSpec((hid // steps, cells), lambda i: (i, 0))
    return pl.pallas_call(
        update_kernel,
        grid=(steps,),
        out_shape=(
            jax.ShapeDtypeStruct(weight.shape, weight.dtype),
            jax.ShapeDtypeStruct(misfit.shape, misfit.dtype),
            jax.ShapeDtypeStruct(bias.shape, bias.dtype),
            jax.ShapeDtypeStruct(input_layer.shape, input_layer.dtype),
        ),
        in_specs=[pl.BlockSpec((hid // steps, runs), lambda i: (i, 0)), whole, tile, line, all_sums, layer],
        out_specs=(tile, pl.BlockSpec((runs // steps, cells), lambda i: (i, 0)), line, layer),
        compiler_params=pltpu.CompilerParams(vmem_limit_bytes=60 * MIB),
        cost_estimate=pl.CostEstimate(
            flops=2 * hid * cells * runs, bytes_accessed=4 * hid * cells, transcendentals=0
        ),
        name="update",
    )(turned, misfit, weight, bias, sums, input_layer)


def update_kernel(
    turned_ref, misfit_ref, weight_ref, bias_ref, sums_ref, input_ref,
    next_ref, misfit_out_ref, bias_out_ref, input_out_ref,
):
    f32, bf16 = jnp.float32, jnp.bfloat16
    step = 1.0 / misfit_ref.shape[0]
    block = 256

    def columns(n, none):
        span = pl.ds(pl.multiple_of(n * block, block), block)
        change = dot(turned_ref[...], misfit_ref[:, span])
        next_ref[:, span] = (weight_ref[:, span].astype(f32) + change).astype(bf16)
        return none

    lax.fori_loop(0, misfit_ref.shape[1] // block, columns, 0, unroll=True)
    rows = misfit_out_ref.shape[0]
    here = pl.multiple_of(pl.program_id(0) * rows, rows)
    value = misfit_ref[pl.ds(here, rows)]
    misfit_out_ref[...] = value

    @pl.when(pl.program_id(0) == 0)
    def _():
        bias_out_ref[...] = bias_ref[...]
        feats, hid = input_ref.shape
        kept = LEVELS - 1
        levels_end, moments_end = CLASSES * kept, CLASSES * kept + STEPS - 1
        row = lax.broadcasted_iota(jnp.int32, (feats, 64), 0)
        line = lax.broadcasted_iota(jnp.int32, (feats, 64), 1)
        group = jnp.where(row < CLASSES * LEVELS, row // LEVELS, CLASSES)
        inner = row - group * LEVELS
        length = jnp.where(group < CLASSES, kept, STEPS - 1)
        line_group = jnp.where(line < levels_end, line // kept, CLASSES)
        line_inner = line - line_group * kept
        same = (group == line_group) & (line < moments_end)
        mix = jnp.where(same & (inner == line_inner), 1.0, 0.0)
        mix = jnp.where(inner == length, jnp.where(same, -1.0, mix), mix)
        mix = jnp.where((inner == length) & (line == moments_end), 1.0, mix)
        steep = jnp.where((line > moments_end) & (line <= moments_end + 3), 1.0, 0.0)
        mix = jnp.where(row == feats - 1, steep, mix).astype(bf16)
        across = hid // 128
        for c in range(across):
            sums = jnp.concatenate([sums_ref[r * across + c] for r in range(8)], axis=0)
            high, middle = two_parts(sums)
            low = (sums - high.astype(f32) - middle.astype(f32)).astype(bf16)
            grad = dot(mix, high) + (dot(mix, middle) + dot(mix, low))
            span = slice(128 * c, 128 * c + 128)
            input_out_ref[:, span] = input_ref[:, span] - 2.0 * grad

    bias_out_ref[...] -= step * jnp.sum(value.astype(f32), axis=0, keepdims=True)


def update(turned, misfit, weight, bias, sums, input_layer):
    hid, cells = weight.shape
    runs = misfit.shape[0]
    steps = 4
    whole = pl.BlockSpec((runs, cells), lambda i: (0, 0))
    line = pl.BlockSpec((1, cells), lambda i: (0, 0))
    layer = pl.BlockSpec(input_layer.shape, lambda i: (0, 0))
    all_sums = pl.BlockSpec(sums.shape, lambda i: (0, 0, 0))
    tile = pl.BlockSpec((hid // steps, cells), lambda i: (i, 0))
    return pl.pallas_call(
        update_kernel,
        grid=(steps,),
        out_shape=(
            jax.ShapeDtypeStruct(weight.shape, weight.dtype),
            jax.ShapeDtypeStruct(misfit.shape, misfit.dtype),
            jax.ShapeDtypeStruct(bias.shape, bias.dtype),
            jax.ShapeDtypeStruct(input_layer.shape, input_layer.dtype),
        ),
        in_specs=[pl.BlockSpec((hid // steps, runs), lambda i: (i, 0)), whole, tile, line, all_sums, layer],
        out_specs=(tile, pl.BlockSpec((runs // steps, cells), lambda i: (i, 0)), line, layer),
        compiler_params=pltpu.CompilerParams(vmem_limit_bytes=60 * MIB),
        cost_estimate=pl.CostEstimate(
            flops=2 * hid * cells * runs, bytes_accessed=4 * hid * cells, transcendentals=0
        ),
        name="update",
    )(turned, misfit, weight, bias, sums, input_layer)


def sum_kernel(
    part_ref, out_ref, pair, own, landed, mine,
    pair_send, pair_recv, part_send, part_recv, back_send, back_recv, last_send, last_recv,
):
    here = place()
    core = here["core"]
    chips = own.shape[0]
    chip = here["xh"] * 32 + here["xl"] * 16 + here["y"] * 4 + here["z"]
    mate = at(here, core=1 - core)

    def device(k):
        return (k // 32, core, (k // 16) % 2, (k // 4) % 4, k % 4)

    barrier = pltpu.get_barrier_semaphore()
    pl.semaphore_signal(barrier, inc=1, device_id=mate, device_id_type=BY_ID)

    def greet(j, carry):
        pl.semaphore_signal(
            barrier, inc=1, device_id=device((chip + j) % chips), device_id_type=BY_ID
        )
        return carry

    lax.fori_loop(1, chips, greet, 0)
    pl.semaphore_wait(barrier, chips)

    swap = pltpu.make_async_remote_copy(
        src_ref=part_ref.at[pl.ds((1 - core) * chips, chips)],
        dst_ref=pair,
        send_sem=pair_send,
        recv_sem=pair_recv,
        device_id=mate,
        device_id_type=BY_ID,
    )
    swap.start()
    swap.wait_recv()
    own[...] = part_ref[pl.ds(core * chips, chips)] + pair[...]

    def scatter(j, carry):
        other = (chip + j) % chips
        pltpu.make_async_remote_copy(
            src_ref=own.at[other],
            dst_ref=landed.at[j - 1],
            send_sem=part_send,
            recv_sem=part_recv,
            device_id=device(other),
            device_id_type=BY_ID,
        ).start()
        return carry

    lax.fori_loop(1, chips, scatter, 0)
    total = own[chip]
    whole = pltpu.make_async_remote_copy(
        src_ref=own.at[pl.ds(0, chips - 1)],
        dst_ref=landed,
        send_sem=part_send,
        recv_sem=part_recv,
        device_id=mate,
        device_id_type=BY_ID,
    )
    whole.wait_recv()
    mine[...] = total + jnp.sum(landed[...], axis=0)

    slot = core * chips + chip
    out_ref[slot] = mine[...]

    def spread(j, carry):
        pltpu.make_async_remote_copy(
            src_ref=mine,
            dst_ref=out_ref.at[slot],
            send_sem=back_send,
            recv_sem=back_recv,
            device_id=device((chip + j) % chips),
            device_id_type=BY_ID,
        ).start()
        return carry

    lax.fori_loop(1, chips, spread, 0)
    gathered = pltpu.make_async_remote_copy(
        src_ref=own.at[pl.ds(0, chips - 1)],
        dst_ref=landed,
        send_sem=back_send,
        recv_sem=back_recv,
        device_id=mate,
        device_id_type=BY_ID,
    )
    gathered.wait_recv()
    half = pl.ds(core * chips, chips)
    last = pltpu.make_async_remote_copy(
        src_ref=out_ref.at[half],
        dst_ref=out_ref.at[half],
        send_sem=last_send,
        recv_sem=last_recv,
        device_id=mate,
        device_id_type=BY_ID,
    )
    last.start()
    last.wait()
    swap.wait_send()
    whole.wait_send()
    gathered.wait_send()


def sum_everywhere(part):
    tiles = part.shape[0]
    f32 = jnp.float32
    dma = pltpu.SemaphoreType.DMA
    vmem = pl.BlockSpec(memory_space=pltpu.VMEM)
    tile = part.shape[1:]
    return pl.pallas_call(
        sum_kernel,
        out_shape=jax.ShapeDtypeStruct(part.shape, f32),
        in_specs=[vmem],
        out_specs=vmem,
        scratch_shapes=[
            pltpu.VMEM((tiles // 2,) + tile, f32),
            pltpu.VMEM((tiles // 2,) + tile, f32),
            pltpu.VMEM((tiles // 2 - 1,) + tile, f32),
            pltpu.VMEM(tile, f32),
        ] + [dma] * 8,
        compiler_params=pltpu.CompilerParams(
            collective_id=2, has_side_effects=True, vmem_limit_bytes=16 * MIB
        ),
        name="sum_everywhere",
    )(part)


def on_device(
    start_field, class_ids, run_levels, steepness, step_pick, input_layer, output_layer, output_bias
):
    bias = output_bias[None, :]
    misfit, turned, sums = solve(
        start_field, class_ids, run_levels.T, steepness[None, :], step_pick[None, :],
        input_layer, bias, output_layer,
    )
    output_next, misfit, bias_next, input_next = update(
        turned, misfit, output_layer, bias, sums, input_layer
    )
    return (misfit, output_next, bias_next[0], input_next)


def solution(mesh):
    split = Mesh(mesh.devices.reshape(2, 2, 2, 4, 4), AXES)
    return jax.shard_map(
        on_device,
        mesh=split,
        in_specs=(
            P(GRP, TILE, None),
            P(TILE, None),
            P(),
            P(),
            P(),
            P(),
            P(None, GRP + TILE),
            P(GRP + TILE),
        ),
        out_specs=(P(None, GRP + TILE), P(None, GRP + TILE), P(GRP + TILE), P()),
        check_vma=False,
    )
```

```python
import math

import jax
import jax.numpy as jnp
from jax import lax
from jax.experimental import pallas as pl
from jax.experimental.pallas import tpu as pltpu
from jax.sharding import Mesh
from jax.sharding import PartitionSpec as P

STEPS = 4
LEVELS = 8
CLASSES = 8
AXES = ("xh", "core", "xl", "y", "z")
GRP = ("xh", "core")
TILE = ("xl", "y", "z")
BY_ID = pl.DeviceIdType.MESH
MIB = 2**20
CHUNKS = 8
SUB = 8


def place():
    return {axis: lax.axis_index(axis) for axis in AXES}


def at(here, **moved):
    return tuple(moved.get(axis, here[axis]) for axis in AXES)


def beside(here, step):
    tile = here["xl"] * 16 + here["y"] * 4 + here["z"] + step
    tile = (tile + 32) % 32
    return at(here, xl=tile // 16, y=(tile // 4) % 4, z=tile % 4)


def dot(a, b):
    return lax.dot_general(a, b, (((1,), (0,)), ((), ())), preferred_element_type=jnp.float32)


def dot_turned(a, b):
    return lax.dot_general(a, b, (((1,), (1,)), ((), ())), preferred_element_type=jnp.float32)


def two_parts(x):
    high = x.astype(jnp.bfloat16)
    return high, (x - high.astype(jnp.float32)).astype(jnp.bfloat16)


def dot_parts(x, order):
    high, low = two_parts(x)
    return dot(high, order) + dot(low, order)


def solve_kernel(
    field_ref, ids_ref, levels_ref, steep_ref, pick_ref, input_ref, bias_ref, weight_ref,
    misfit_ref, turned_ref, sums_ref,
    about_ref, raw, rows_own, class_ref, halo_up, halo_dn, class_up, class_dn, kappa, wide_a, wide_b, picked, sent, got,
    relay, weight, hidden, turned, gain, pred, misfit, misfit_far, grad,
    tiles, pair, own, landed, middle, landed_z, mine,
    load_sem, halo_send, halo_recv, class_send, class_recv, out_send, out_recv, keep_sem, weight_sem,
    relay_send, relay_recv, sum_send, sum_recv,
):
    here = place()
    runs = rows_own.shape[1]
    tile_rows = rows_own.shape[0]
    width = rows_own.shape[2]
    part = runs // CHUNKS
    tile = here["xl"] * 16 + here["y"] * 4 + here["z"]
    group = here["xh"] * 2 + here["core"]
    up, dn = beside(here, -1), beside(here, 1)
    has_up, has_dn = tile > 0, tile < 31
    mates = (
        (here["xh"] * 2 + 1 - here["core"], at(here, core=1 - here["core"])),
        ((1 - here["xh"]) * 2 + here["core"], at(here, xh=1 - here["xh"])),
        ((1 - here["xh"]) * 2 + 1 - here["core"], at(here, xh=1 - here["xh"], core=1 - here["core"])),
    )

    def load(k):
        lines = part * tile_rows
        return [
            pltpu.make_async_copy(
                field_ref.at[pl.ds(k * lines, lines), pl.ds(128 * c, 128)],
                raw.at[c, pl.ds(k * lines, lines)],
                load_sem.at[k, c],
            )
            for c in range(width // 128)
        ]

    for k in range(CHUNKS):
        for copy in load(k):
            copy.start()
    weight_load = pltpu.make_async_copy(weight_ref, weight, weight_sem)
    weight_load.start()

    barrier = pltpu.get_barrier_semaphore()
    for _, mate in mates:
        pl.semaphore_signal(barrier, inc=1, device_id=mate, device_id_type=BY_ID)

    @pl.when(has_up)
    def _():
        pl.semaphore_signal(barrier, inc=1, device_id=up, device_id_type=BY_ID)

    @pl.when(has_dn)
    def _():
        pl.semaphore_signal(barrier, inc=1, device_id=dn, device_id_type=BY_ID)

    xl = here["xl"]
    ends_dn, ends_up = tile == 15, tile == 16
    corner = 3 * (1 - xl)
    relay_path = (here["y"] - corner + 4) % 4
    is_relay = (here["z"] == corner) & (relay_path > 0)
    relay_from = at(here, y=corner)
    relay_to = at(here, xl=1 - xl, y=3 * xl, z=3 * xl)

    @pl.when(is_relay)
    def _():
        for other in (relay_from, relay_to):
            pl.semaphore_signal(barrier, inc=1, device_id=other, device_id_type=BY_ID)

    @pl.when(ends_dn | ends_up)
    def _():
        for side in range(2):
            for p in range(1, 4):
                edge_at = 3 * (1 - side)
                other = at(here, xl=side, y=(edge_at + p) % 4, z=edge_at)
                pl.semaphore_signal(barrier, inc=1, device_id=other, device_id_type=BY_ID)

    plane = here["xh"] * 8 + here["xl"] * 4 + here["y"]

    def in_plane(k):
        return at(here, xh=k // 8, xl=(k // 4) % 2, y=k % 4)

    def greet(j, none):
        other = in_plane((plane + j) % 16)
        pl.semaphore_signal(barrier, inc=1, device_id=other, device_id_type=BY_ID)
        return none

    lax.fori_loop(1, 16, greet, 0)
    for j in range(1, 4):
        other = at(here, z=(here["z"] + j) % 4)
        pl.semaphore_signal(barrier, inc=1, device_id=other, device_id_type=BY_ID)

    callers = 3 + 18 + jnp.where(has_up, 1, 0) + jnp.where(has_dn, 1, 0)
    callers = callers + jnp.where(is_relay, 2, 0)
    callers = callers + jnp.where(ends_dn | ends_up, 6, 0)
    pl.semaphore_wait(barrier, callers)

    def class_copy(upward):
        return pltpu.make_async_remote_copy(
            src_ref=class_ref.at[pl.ds(0 if upward else tile_rows - STEPS, STEPS)],
            dst_ref=class_dn if upward else class_up,
            send_sem=class_send.at[0 if upward else 1],
            recv_sem=class_recv.at[0 if upward else 1],
            device_id=up if upward else dn,
            device_id_type=BY_ID,
        )

    def halo_copy(k, upward):
        span = pl.ds(pl.multiple_of(k * part, part), part)
        return pltpu.make_async_remote_copy(
            src_ref=rows_own.at[pl.ds(0 if upward else tile_rows - STEPS, STEPS), span],
            dst_ref=(halo_dn if upward else halo_up).at[:, span],
            send_sem=halo_send.at[k, 0 if upward else 1],
            recv_sem=halo_recv.at[k, 0 if upward else 1],
            device_id=up if upward else dn,
            device_id_type=BY_ID,
        )

    def detour_copy(k, upward):
        span = pl.ds(pl.multiple_of(k * part, part), part)
        return pltpu.make_async_remote_copy(
            src_ref=rows_own.at[pl.ds(0 if upward else tile_rows - STEPS, STEPS), span],
            dst_ref=relay.at[k // 4],
            send_sem=halo_send.at[k, 0 if upward else 1],
            recv_sem=relay_recv.at[k // 4],
            device_id=at(here, y=(here["y"] + k % 4) % 4),
            device_id_type=BY_ID,
        )

    def forward_copy(k, upward):
        span = pl.ds(pl.multiple_of(k * part, part), part)
        return pltpu.make_async_remote_copy(
            src_ref=relay.at[k // 4],
            dst_ref=(halo_dn if upward else halo_up).at[:, span],
            send_sem=relay_send.at[k // 4],
            recv_sem=halo_recv.at[k, 0 if upward else 1],
            device_id=relay_to,
            device_id_type=BY_ID,
        )

    def send_halo(k, upward):
        detour = (ends_up if upward else ends_dn) & (k % 4 > 0)

        @pl.when((has_up if upward else has_dn) & jnp.logical_not(detour))
        def _():
            halo_copy(k, upward).start()

        @pl.when(detour)
        def _():
            detour_copy(k, upward).start()

    def out_copy(k, j):
        span = pl.ds(pl.multiple_of(k * part, part), part)
        owner, mate = mates[j]
        return pltpu.make_async_remote_copy(
            src_ref=sent.at[owner, span],
            dst_ref=got.at[j, span],
            send_sem=out_send.at[k, j],
            recv_sem=out_recv.at[k, j],
            device_id=mate,
            device_id_type=BY_ID,
        )

    @pl.when(jnp.logical_not(has_up))
    def _():
        halo_up[...] = jnp.zeros_like(halo_up)
        class_up[...] = jnp.full_like(class_up, -1.0)

    @pl.when(jnp.logical_not(has_dn))
    def _():
        halo_dn[...] = jnp.zeros_like(halo_dn)
        class_dn[...] = jnp.full_like(class_dn, -1.0)

    first = lax.broadcasted_iota(jnp.int32, (width, width), 0)
    second = lax.broadcasted_iota(jnp.int32, (width, width), 1)
    blocks = width // 128
    order = jnp.where(first == (second % 128) * blocks + second // 128, 1.0, 0.0)
    order = order.astype(jnp.bfloat16)
    lines = part * tile_rows
    of_run = [
        levels_ref[...].astype(jnp.float32),
        steep_ref[...],
        pick_ref[...].astype(jnp.float32),
        jnp.zeros((128 - CLASSES - 2, about_ref.shape[0]), jnp.float32),
    ]
    about_ref[...] = jnp.concatenate(of_run, axis=0).T[:, : about_ref.shape[1]]
    class_rows = dot(ids_ref[...].astype(jnp.float32).astype(jnp.bfloat16), order)
    for i in range(tile_rows):
        class_ref[i] = jnp.broadcast_to(class_rows[i : i + 1], (SUB, width))

    @pl.when(has_up)
    def _():
        class_copy(True).start()

    @pl.when(has_dn)
    def _():
        class_copy(False).start()

    def prepare(k, none):
        for copy in load(k):
            copy.wait()
        span = pl.ds(pl.multiple_of(k * lines, lines), lines)
        lined = jnp.concatenate([raw[c, span] for c in range(blocks)], axis=1)
        lined = dot_parts(lined, order)
        for c in range(blocks):
            raw[c, span] = lined[:, 128 * c : 128 * c + 128]

        def turn(j, carry):
            first = pl.multiple_of(j * SUB, SUB)
            for i in range(tile_rows):
                for c in range(blocks):
                    rows_own[i, pl.ds(first, SUB), pl.ds(128 * c, 128)] = raw[
                        c, pl.ds(j * (SUB * tile_rows) + i, SUB, stride=tile_rows), :
                    ]
            return carry

        lax.fori_loop(k * (part // SUB), (k + 1) * (part // SUB), turn, 0)

        send_halo(k, True)
        send_halo(k, False)
        return none

    lax.fori_loop(0, CHUNKS, prepare, 0)

    @pl.when(has_up)
    def _():
        class_copy(False).wait_recv()

    @pl.when(has_dn)
    def _():
        class_copy(True).wait_recv()

    keep_up = jnp.where(has_up, 1.0, 0.0).astype(jnp.float32)
    keep_dn = jnp.where(has_dn, 1.0, 0.0).astype(jnp.float32)
    lane = lax.broadcasted_iota(jnp.int32, (SUB, 128), 1)
    left, right = lane == 0, lane == 127
    edge = width - 128

    def next_column(x):
        turned = jnp.where(right, 0.0, pltpu.roll(x[:, :128], 127, 1))
        return jnp.concatenate([x[:, 128:], turned], axis=1)

    def last_column(x, outermost):
        turned = jnp.where(left, outermost[:, :128], pltpu.roll(x[:, edge:], 1, 1))
        return jnp.concatenate([turned, x[:, :edge]], axis=1)

    span_rows = tile_rows + 2 * STEPS

    def advance(k, half_chunk):
        first = pl.multiple_of(k * part + half_chunk * SUB, SUB)
        runs_here = pl.ds(first, SUB)
        picked_here = pl.ds(pl.multiple_of(half_chunk * SUB, SUB), SUB)
        about = about_ref[pl.ds(pl.multiple_of(group * runs + first, SUB), SUB)]
        table = 0.015 * jnp.exp(about[:, :CLASSES] * math.log(1.35))
        steep = jnp.broadcast_to(about[:, CLASSES : CLASSES + 1], (SUB, width))
        pick = jnp.broadcast_to(about[:, CLASSES + 1 : CLASSES + 2], (SUB, width))
        rest = 1.0 - steep
        half = [jnp.broadcast_to(table[:, c : c + 1], (SUB, width)) for c in range(CLASSES)]
        for i in range(span_rows):
            if i < STEPS:
                klass = class_up[i]
            elif i < STEPS + tile_rows:
                klass = class_ref[i - STEPS]
            else:
                klass = class_dn[i - STEPS - tile_rows]
            value = jnp.zeros((SUB, width), jnp.float32)
            for c in range(CLASSES):
                value = jnp.where(klass == float(c), half[c], value)
            kappa[i] = value

        def start_row(i):
            if i < STEPS:
                return halo_up[i, runs_here]
            if i < STEPS + tile_rows:
                return rows_own[i - STEPS, runs_here]
            return halo_dn[i - STEPS - tile_rows, runs_here]

        for step in range(STEPS):
            source = (None, wide_a, wide_b, wide_a)[step]
            sink = (wide_a, wide_b, wide_a, None)[step]

            def row(i):
                return start_row(i) if step == 0 else source[i]

            def spread_of(i, value):
                bottom = 1.0 + value * value
                guess = pl.reciprocal(bottom, approx=True)
                guess = guess * (2.0 - bottom * guess)
                return kappa[i] * (steep + rest * guess)

            above = row(step)
            above_spread = spread_of(step, above)
            centre = row(step + 1)
            spread = spread_of(step + 1, centre)
            flow_in = (above_spread + spread) * (centre - above)
            for i in range(step + 1, span_rows - step - 1):
                below = row(i + 1)
                below_spread = spread_of(i + 1, below)
                flow_out = (spread + below_spread) * (below - centre)
                flow = (spread + next_column(spread)) * (next_column(centre) - centre)
                back = last_column(flow, spread * centre)
                total = centre + (flow_out - flow_in) + (flow - back)
                if i < STEPS:
                    total = total * keep_up
                if i >= STEPS + tile_rows:
                    total = total * keep_dn
                if sink is not None:
                    sink[i] = total
                if STEPS <= i < STEPS + tile_rows:
                    if step > 0:
                        total = jnp.where(pick == step + 1.0, total, picked[i - STEPS, picked_here])
                    picked[i - STEPS, picked_here] = total
                flow_in, centre, spread = flow_out, below, below_spread

    back_order = jnp.where(second == (first % 128) * blocks + first // 128, 1.0, 0.0)
    back_order = back_order.astype(jnp.bfloat16)

    def one_chunk(k, none):
        for upward in (False, True):
            for slot in range(CHUNKS // 4):
                @pl.when(is_relay & (xl == int(upward)) & (k == 2 * slot))
                def _():
                    passed = relay_path + 4 * slot
                    forward = forward_copy(passed, upward)
                    detour_copy(passed, upward).wait_recv()
                    forward.start()

        @pl.when(has_up)
        def _():
            halo_copy(k, False).wait_recv()

        @pl.when(has_dn)
        def _():
            halo_copy(k, True).wait_recv()

        def half_of(half_chunk, carry):
            advance(k, half_chunk)
            return carry

        lax.fori_loop(0, part // SUB, half_of, 0)
        lined = dot_parts(picked[...].reshape(tile_rows * part, width), back_order)
        span = pl.ds(pl.multiple_of(k * part, part), part)
        for i in range(tile_rows):
            sent[i // 4, span, pl.ds((i % 4) * width, width)] = lined[i * part : (i + 1) * part]
        for j in range(3):
            out_copy(k, j).start()
        return none

    lax.fori_loop(0, CHUNKS, one_chunk, 0)

    cells = weight.shape[1]
    hid = weight.shape[0]
    all_runs = hidden.shape[0]
    block = 256
    f32, bf16 = jnp.float32, jnp.bfloat16
    eye = lax.broadcasted_iota(jnp.int32, (block, block), 0) == lax.broadcasted_iota(
        jnp.int32, (block, block), 1
    )
    share = 2.0 / all_runs
    eye = jnp.where(eye, -0.5 * share, 0.0).astype(bf16)
    about = about_ref[...]
    steep_all = about[:, CLASSES : CLASSES + 1]
    feats = input_ref.shape[0]
    onehots = CLASSES * LEVELS
    entry = lax.broadcasted_iota(jnp.int32, (16, feats), 0)
    column = lax.broadcasted_iota(jnp.int32, (16, feats), 1)
    source = jnp.where(column < onehots, column // LEVELS, CLASSES + 1)
    spread_out = dot(about.astype(bf16), jnp.where(entry == source, 1.0, 0.0).astype(bf16))
    column = lax.broadcasted_iota(jnp.int32, (all_runs, feats), 1)
    wanted = jnp.where(column < onehots, column % LEVELS, column - onehots + 1)
    wanted = jnp.where(column < onehots + STEPS, wanted, -1).astype(f32)
    onehot = jnp.where(spread_out == wanted, 1.0, 0.0).astype(bf16)

    def independent(rows):
        count = rows.shape[0]
        kept = LEVELS - 1
        levels_end, moments_end = CLASSES * kept, CLASSES * kept + STEPS - 1
        high, middle = two_parts(rows)
        low = (rows - high.astype(f32) - middle.astype(f32)).astype(bf16)
        line = lax.broadcasted_iota(jnp.int32, (64, 16), 0)
        entry = lax.broadcasted_iota(jnp.int32, (64, 16), 1)
        source = jnp.where(line < levels_end, line // kept, CLASSES + 1)
        source = jnp.where(line > moments_end, CLASSES, source)

        def chosen(last, extra):
            keep = (entry == source) & ((line < last) | (line == extra))
            return jnp.where(keep, 1.0, 0.0).astype(bf16)

        value = (
            dot_turned(chosen(moments_end, moments_end + 1), high)
            + dot_turned(chosen(0, moments_end + 2), middle)
            + dot_turned(chosen(0, moments_end + 3), low)
        )
        line = lax.broadcasted_iota(jnp.int32, (64, count), 0)
        wanted = jnp.where(line < levels_end, line % kept, line - levels_end + 1).astype(f32)
        marks = jnp.where(value == wanted, 1.0, 0.0)
        value = jnp.where(line < moments_end, marks, value)
        return jnp.where(line == moments_end, 1.0, value).astype(bf16)

    def hidden_block(n, none):
        span = pl.ds(pl.multiple_of(n * block, block), block)
        value = input_ref[:, span]
        high, low = two_parts(value)
        rest = (value - high.astype(f32) - low.astype(f32)).astype(bf16)
        pre = dot(onehot, high) + (dot(onehot, low) + dot(onehot, rest))
        pre = pre + steep_all * value[value.shape[0] - 1 :, :]
        logistic = 1.0 / (1.0 + jnp.exp(-pre))
        active = (pre * logistic).astype(bf16)
        hidden[:, span] = active
        gain[:, span] = logistic * (1.0 + pre * (1.0 - logistic)) * share
        turned[span, :] = dot_turned(eye, active).astype(bf16)
        return none

    lax.fori_loop(0, hid // block, hidden_block, 0)
    turned_copy = pltpu.make_async_copy(turned, turned_ref, keep_sem.at[0])
    turned_copy.start()
    weight_load.wait()

    def pred_block(n, none):
        span = pl.ds(pl.multiple_of(n * block, block), block)
        pred[:, span] = dot(hidden[...], weight[:, span]) + bias_ref[:, span]
        return none

    lax.fori_loop(0, cells // block, pred_block, 0)

    def compare(source, group_at, start, count, copy_row):
        def some(b, none):
            inner = pl.multiple_of(start + b * 16, 16)
            at_run = pl.ds(pl.multiple_of(group_at * runs + inner, 16), 16)
            value = (pred[at_run] - source[pl.ds(inner, 16)]).astype(bf16)
            misfit[at_run] = value
            if copy_row is not None:
                misfit_far[pl.ds(pl.multiple_of(copy_row + b * 16, 16), 16)] = value
            return none

        lax.fori_loop(0, count // 16, some, 0)

    for k in range(CHUNKS):
        out_copy(k, 0).wait_recv()
    compare(sent.at[group], group, 0, runs, None)
    compare(got.at[0], mates[0][0], 0, runs, None)
    near = pl.ds(pl.multiple_of(here["xh"] * (2 * runs), 2 * runs), 2 * runs)
    far = (1 - here["xh"]) * (2 * runs)

    near_mix = independent(about_ref[near])

    def near_block(n, none):
        span = pl.ds(pl.multiple_of(n * block, block), block)
        back = dot_turned(misfit[near], weight[span, :]) * gain[near, span]
        high, low = two_parts(back)
        grad[:, span] = dot(near_mix, high) + dot(near_mix, low)
        return none

    lax.fori_loop(0, hid // block, near_block, 0, unroll=4)
    near_copy = pltpu.make_async_copy(misfit.at[near], misfit_ref.at[near], keep_sem.at[1])
    near_copy.start()

    half = runs // 2
    for h in range(2):
        for k in range(h * CHUNKS // 2, (h + 1) * CHUNKS // 2):
            out_copy(k, 1).wait_recv()
            out_copy(k, 2).wait_recv()
        for j in (1, 2):
            at_row = here["core"] if j == 1 else 1 - here["core"]
            compare(got.at[j], mates[j][0], h * half, half, at_row * half)

        far_rows = [pl.ds(pl.multiple_of(far + g * runs + h * half, half), half) for g in range(2)]
        mix = independent(jnp.concatenate([about_ref[rows] for rows in far_rows], axis=0))

        def far_block(n, none):
            span = pl.ds(pl.multiple_of(n * block, block), block)
            factor = jnp.concatenate([gain[rows, span] for rows in far_rows], axis=0)
            back = dot_turned(misfit_far[...], weight[span, :]) * factor
            high, low = two_parts(back)
            grad[:, span] += dot(mix, high) + dot(mix, low)
            return none

        lax.fori_loop(0, hid // block, far_block, 0, unroll=True)

    far_span = pl.ds(pl.multiple_of(far, 2 * runs), 2 * runs)
    far_copy = pltpu.make_async_copy(misfit.at[far_span], misfit_ref.at[far_span], keep_sem.at[2])
    far_copy.start()
    for i in range(tiles.shape[0]):
        r, c = i // (hid // 128), i % (hid // 128)
        tiles[i] = grad[8 * r : 8 * r + 8, 128 * c : 128 * c + 128]

    def sum_copy(stage, source, sink, device):
        return pltpu.make_async_remote_copy(
            src_ref=source,
            dst_ref=sink,
            send_sem=sum_send.at[stage],
            recv_sem=sum_recv.at[stage],
            device_id=device,
            device_id_type=BY_ID,
        )

    core, z = here["core"], here["z"]
    mate = at(here, core=1 - core)
    share_of = 4
    chips = own.shape[0]
    swap = sum_copy(0, tiles.at[pl.ds((1 - core) * chips, chips)], pair, mate)
    swap.start()
    swap.wait_recv()
    own[...] = tiles[pl.ds(core * chips, chips)] + pair[...]

    def scatter(j, none):
        other = (plane + j) % 16
        sum_copy(
            1,
            own.at[pl.ds(other * share_of, share_of)],
            landed.at[pl.ds((j - 1) * share_of, share_of)],
            in_plane(other),
        ).start()
        return none

    lax.fori_loop(1, 16, scatter, 0)
    scattered = sum_copy(1, own.at[pl.ds(0, 15 * share_of)], landed, mate)
    scattered.wait_recv()
    total = own[pl.ds(plane * share_of, share_of)]
    for j in range(15):
        total = total + landed[j * share_of : (j + 1) * share_of]
    middle[...] = total
    for j in range(1, 4):
        other = (z + j) % 4
        sum_copy(2, middle.at[other], landed_z.at[j - 1], at(here, z=other)).start()
    scattered_z = sum_copy(2, middle.at[pl.ds(0, 3)], landed_z, mate)
    scattered_z.wait_recv()
    mine[...] = middle[z] + (landed_z[0] + landed_z[1] + landed_z[2])
    slot = core * chips + plane * share_of
    sums_ref[slot + z] = mine[...]
    for j in range(1, 4):
        sum_copy(3, mine, sums_ref.at[slot + z], at(here, z=(z + j) % 4)).start()
    gathered_z = sum_copy(3, middle.at[pl.ds(0, 3)], landed_z, mate)
    gathered_z.wait_recv()
    quad = pl.ds(slot, share_of)

    def gather(j, none):
        sum_copy(4, sums_ref.at[quad], sums_ref.at[quad], in_plane((plane + j) % 16)).start()
        return none

    lax.fori_loop(1, 16, gather, 0)
    gathered = sum_copy(4, own.at[pl.ds(0, 15 * share_of)], landed, mate)
    gathered.wait_recv()
    half_sums = sums_ref.at[pl.ds(core * chips, chips)]
    last = sum_copy(5, half_sums, half_sums, mate)
    last.start()
    last.wait()
    for copy in (swap, scattered, scattered_z, gathered_z, gathered):
        copy.wait_send()

    @pl.when(is_relay)
    def _():
        for slot in range(CHUNKS // 4):
            forward_copy(relay_path + 4 * slot, False).wait_send()

    turned_copy.wait()
    near_copy.wait()
    far_copy.wait()
    for k in range(CHUNKS):
        for j in range(3):
            out_copy(k, j).wait_send()

    @pl.when(has_up)
    def _():
        class_copy(True).wait_send()
        for k in range(CHUNKS):
            halo_copy(k, True).wait_send()

    @pl.when(has_dn)
    def _():
        class_copy(False).wait_send()
        for k in range(CHUNKS):
            halo_copy(k, False).wait_send()


def solve(field, classes, levels, steep, pick, input_layer, bias, weight):
    runs, rows, width = field.shape
    hid, cells = weight.shape
    all_runs = levels.shape[1]
    f32, bf16 = jnp.float32, jnp.bfloat16
    dma = pltpu.SemaphoreType.DMA
    vmem = pl.BlockSpec(memory_space=pltpu.VMEM)
    anywhere = pl.BlockSpec(memory_space=pl.ANY)
    span = rows + 2 * STEPS
    part = runs // CHUNKS
    return pl.pallas_call(
        solve_kernel,
        out_shape=(
            jax.ShapeDtypeStruct((all_runs, cells), bf16),
            jax.ShapeDtypeStruct((hid, all_runs), bf16),
            jax.ShapeDtypeStruct((hid // 16, 8, 128), f32),
        ),
        in_specs=[anywhere] + [vmem] * 6 + [anywhere],
        out_specs=(anywhere, anywhere, vmem),
        scratch_shapes=[
            pltpu.VMEM((all_runs, 16), f32),
            pltpu.VMEM((width // 128, runs * rows, 128), f32),
            pltpu.VMEM((rows, runs, width), f32),
            pltpu.VMEM((rows, SUB, width), f32),
            pltpu.VMEM((STEPS, runs, width), f32),
            pltpu.VMEM((STEPS, runs, width), f32),
            pltpu.VMEM((STEPS, SUB, width), f32),
            pltpu.VMEM((STEPS, SUB, width), f32),
            pltpu.VMEM((span, SUB, width), f32),
            pltpu.VMEM((span, SUB, width), f32),
            pltpu.VMEM((span, SUB, width), f32),
            pltpu.VMEM((rows, part, width), f32),
            pltpu.VMEM((4, runs, 4 * width), f32),
            pltpu.VMEM((3, runs, 4 * width), f32),
            pltpu.VMEM((CHUNKS // 4, STEPS, part, width), f32),
            pltpu.VMEM((hid, cells), bf16),
            pltpu.VMEM((all_runs, hid), bf16),
            pltpu.VMEM((hid, all_runs), bf16),
            pltpu.VMEM((all_runs, hid), f32),
            pltpu.VMEM((all_runs, cells), f32),
            pltpu.VMEM((all_runs, cells), bf16),
            pltpu.VMEM((runs, cells), bf16),
            pltpu.VMEM((64, hid), f32),
            pltpu.VMEM((hid // 16, 8, 128), f32),
            pltpu.VMEM((hid // 32, 8, 128), f32),
            pltpu.VMEM((hid // 32, 8, 128), f32),
            pltpu.VMEM((60, 8, 128), f32),
            pltpu.VMEM((4, 8, 128), f32),
            pltpu.VMEM((3, 8, 128), f32),
            pltpu.VMEM((8, 128), f32),
            dma((CHUNKS, 4)),
            dma((CHUNKS, 2)),
            dma((CHUNKS, 2)),
            dma((2,)),
            dma((2,)),
            dma((CHUNKS, 3)),
            dma((CHUNKS, 3)),
            dma((3,)),
            dma,
            dma((CHUNKS // 4,)),
            dma((CHUNKS // 4,)),
            dma((6,)),
            dma((6,)),
        ],
        compiler_params=pltpu.CompilerParams(
            collective_id=1, has_side_effects=True, vmem_limit_bytes=58 * MIB
        ),
        name="solve",
    )(
        field.reshape(runs * rows, width), classes, levels, steep, pick, input_layer, bias, weight,
    )


def update_kernel(
    turned_ref, misfit_ref, weight_ref, bias_ref, sums_ref, input_ref,
    next_ref, misfit_out_ref, bias_out_ref, input_out_ref,
):
    f32, bf16 = jnp.float32, jnp.bfloat16
    step = 1.0 / misfit_ref.shape[0]
    block = 256

    def columns(n, none):
        span = pl.ds(pl.multiple_of(n * block, block), block)
        change = dot(turned_ref[...], misfit_ref[:, span])
        next_ref[:, span] = (weight_ref[:, span].astype(f32) + change).astype(bf16)
        return none

    lax.fori_loop(0, misfit_ref.shape[1] // block, columns, 0, unroll=True)
    rows = misfit_out_ref.shape[0]
    here = pl.multiple_of(pl.program_id(0) * rows, rows)
    value = misfit_ref[pl.ds(here, rows)]
    misfit_out_ref[...] = value

    @pl.when(pl.program_id(0) == 0)
    def _():
        bias_out_ref[...] = bias_ref[...]
        feats, hid = input_ref.shape
        kept = LEVELS - 1
        levels_end, moments_end = CLASSES * kept, CLASSES * kept + STEPS - 1
        row = lax.broadcasted_iota(jnp.int32, (feats, 64), 0)
        line = lax.broadcasted_iota(jnp.int32, (feats, 64), 1)
        group = jnp.where(row < CLASSES * LEVELS, row // LEVELS, CLASSES)
        inner = row - group * LEVELS
        length = jnp.where(group < CLASSES, kept, STEPS - 1)
        line_group = jnp.where(line < levels_end, line // kept, CLASSES)
        line_inner = line - line_group * kept
        same = (group == line_group) & (line < moments_end)
        mix = jnp.where(same & (inner == line_inner), 1.0, 0.0)
        mix = jnp.where(inner == length, jnp.where(same, -1.0, mix), mix)
        mix = jnp.where((inner == length) & (line == moments_end), 1.0, mix)
        steep = jnp.where((line > moments_end) & (line <= moments_end + 3), 1.0, 0.0)
        mix = jnp.where(row == feats - 1, steep, mix).astype(bf16)
        across = hid // 128
        for c in range(across):
            sums = jnp.concatenate([sums_ref[r * across + c] for r in range(8)], axis=0)
            high, middle = two_parts(sums)
            low = (sums - high.astype(f32) - middle.astype(f32)).astype(bf16)
            grad = dot(mix, high) + (dot(mix, middle) + dot(mix, low))
            span = slice(128 * c, 128 * c + 128)
            input_out_ref[:, span] = input_ref[:, span] - 2.0 * grad

    bias_out_ref[...] -= step * jnp.sum(value.astype(f32), axis=0, keepdims=True)


def update(turned, misfit, weight, bias, sums, input_layer):
    hid, cells = weight.shape
    runs = misfit.shape[0]
    steps = 4
    whole = pl.BlockSpec((runs, cells), lambda i: (0, 0))
    line = pl.BlockSpec((1, cells), lambda i: (0, 0))
    layer = pl.BlockSpec(input_layer.shape, lambda i: (0, 0))
    all_sums = pl.BlockSpec(sums.shape, lambda i: (0, 0, 0))
    tile = pl.BlockSpec((hid // steps, cells), lambda i: (i, 0))
    return pl.pallas_call(
        update_kernel,
        grid=(steps,),
        out_shape=(
            jax.ShapeDtypeStruct(weight.shape, weight.dtype),
            jax.ShapeDtypeStruct(misfit.shape, misfit.dtype),
            jax.ShapeDtypeStruct(bias.shape, bias.dtype),
            jax.ShapeDtypeStruct(input_layer.shape, input_layer.dtype),
        ),
        in_specs=[pl.BlockSpec((hid // steps, runs), lambda i: (i, 0)), whole, tile, line, all_sums, layer],
        out_specs=(tile, pl.BlockSpec((runs // steps, cells), lambda i: (i, 0)), line, layer),
        compiler_params=pltpu.CompilerParams(vmem_limit_bytes=60 * MIB),
        cost_estimate=pl.CostEstimate(
            flops=2 * hid * cells * runs, bytes_accessed=4 * hid * cells, transcendentals=0
        ),
        name="update",
    )(turned, misfit, weight, bias, sums, input_layer)


def update_kernel(
    turned_ref, misfit_ref, weight_ref, bias_ref, sums_ref, input_ref,
    next_ref, misfit_out_ref, bias_out_ref, input_out_ref,
):
    f32, bf16 = jnp.float32, jnp.bfloat16
    step = 1.0 / misfit_ref.shape[0]
    block = 256

    def columns(n, none):
        span = pl.ds(pl.multiple_of(n * block, block), block)
        change = dot(turned_ref[...], misfit_ref[:, span])
        next_ref[:, span] = (weight_ref[:, span].astype(f32) + change).astype(bf16)
        return none

    lax.fori_loop(0, misfit_ref.shape[1] // block, columns, 0, unroll=True)
    rows = misfit_out_ref.shape[0]
    here = pl.multiple_of(pl.program_id(0) * rows, rows)
    value = misfit_ref[pl.ds(here, rows)]
    misfit_out_ref[...] = value

    @pl.when(pl.program_id(0) == 0)
    def _():
        bias_out_ref[...] = bias_ref[...]
        feats, hid = input_ref.shape
        kept = LEVELS - 1
        levels_end, moments_end = CLASSES * kept, CLASSES * kept + STEPS - 1
        row = lax.broadcasted_iota(jnp.int32, (feats, 64), 0)
        line = lax.broadcasted_iota(jnp.int32, (feats, 64), 1)
        group = jnp.where(row < CLASSES * LEVELS, row // LEVELS, CLASSES)
        inner = row - group * LEVELS
        length = jnp.where(group < CLASSES, kept, STEPS - 1)
        line_group = jnp.where(line < levels_end, line // kept, CLASSES)
        line_inner = line - line_group * kept
        same = (group == line_group) & (line < moments_end)
        mix = jnp.where(same & (inner == line_inner), 1.0, 0.0)
        mix = jnp.where(inner == length, jnp.where(same, -1.0, mix), mix)
        mix = jnp.where((inner == length) & (line == moments_end), 1.0, mix)
        steep = jnp.where((line > moments_end) & (line <= moments_end + 3), 1.0, 0.0)
        mix = jnp.where(row == feats - 1, steep, mix).astype(bf16)
        across = hid // 128
        for c in range(across):
            sums = jnp.concatenate([sums_ref[r * across + c] for r in range(8)], axis=0)
            high, middle = two_parts(sums)
            low = (sums - high.astype(f32) - middle.astype(f32)).astype(bf16)
            grad = dot(mix, high) + (dot(mix, middle) + dot(mix, low))
            span = slice(128 * c, 128 * c + 128)
            input_out_ref[:, span] = input_ref[:, span] - 2.0 * grad

    bias_out_ref[...] -= step * jnp.sum(value.astype(f32), axis=0, keepdims=True)


def update(turned, misfit, weight, bias, sums, input_layer):
    hid, cells = weight.shape
    runs = misfit.shape[0]
    steps = 4
    whole = pl.BlockSpec((runs, cells), lambda i: (0, 0))
    line = pl.BlockSpec((1, cells), lambda i: (0, 0))
    layer = pl.BlockSpec(input_layer.shape, lambda i: (0, 0))
    all_sums = pl.BlockSpec(sums.shape, lambda i: (0, 0, 0))
    tile = pl.BlockSpec((hid // steps, cells), lambda i: (i, 0))
    return pl.pallas_call(
        update_kernel,
        grid=(steps,),
        out_shape=(
            jax.ShapeDtypeStruct(weight.shape, weight.dtype),
            jax.ShapeDtypeStruct(misfit.shape, misfit.dtype),
            jax.ShapeDtypeStruct(bias.shape, bias.dtype),
            jax.ShapeDtypeStruct(input_layer.shape, input_layer.dtype),
        ),
        in_specs=[pl.BlockSpec((hid // steps, runs), lambda i: (i, 0)), whole, tile, line, all_sums, layer],
        out_specs=(tile, pl.BlockSpec((runs // steps, cells), lambda i: (i, 0)), line, layer),
        compiler_params=pltpu.CompilerParams(vmem_limit_bytes=60 * MIB),
        cost_estimate=pl.CostEstimate(
            flops=2 * hid * cells * runs, bytes_accessed=4 * hid * cells, transcendentals=0
        ),
        name="update",
    )(turned, misfit, weight, bias, sums, input_layer)


def sum_kernel(
    part_ref, out_ref, pair, own, landed, mine,
    pair_send, pair_recv, part_send, part_recv, back_send, back_recv, last_send, last_recv,
):
    here = place()
    core = here["core"]
    chips = own.shape[0]
    chip = here["xh"] * 32 + here["xl"] * 16 + here["y"] * 4 + here["z"]
    mate = at(here, core=1 - core)

    def device(k):
        return (k // 32, core, (k // 16) % 2, (k // 4) % 4, k % 4)

    barrier = pltpu.get_barrier_semaphore()
    pl.semaphore_signal(barrier, inc=1, device_id=mate, device_id_type=BY_ID)

    def greet(j, carry):
        pl.semaphore_signal(
            barrier, inc=1, device_id=device((chip + j) % chips), device_id_type=BY_ID
        )
        return carry

    lax.fori_loop(1, chips, greet, 0)
    pl.semaphore_wait(barrier, chips)

    swap = pltpu.make_async_remote_copy(
        src_ref=part_ref.at[pl.ds((1 - core) * chips, chips)],
        dst_ref=pair,
        send_sem=pair_send,
        recv_sem=pair_recv,
        device_id=mate,
        device_id_type=BY_ID,
    )
    swap.start()
    swap.wait_recv()
    own[...] = part_ref[pl.ds(core * chips, chips)] + pair[...]

    def scatter(j, carry):
        other = (chip + j) % chips
        pltpu.make_async_remote_copy(
            src_ref=own.at[other],
            dst_ref=landed.at[j - 1],
            send_sem=part_send,
            recv_sem=part_recv,
            device_id=device(other),
            device_id_type=BY_ID,
        ).start()
        return carry

    lax.fori_loop(1, chips, scatter, 0)
    total = own[chip]
    whole = pltpu.make_async_remote_copy(
        src_ref=own.at[pl.ds(0, chips - 1)],
        dst_ref=landed,
        send_sem=part_send,
        recv_sem=part_recv,
        device_id=mate,
        device_id_type=BY_ID,
    )
    whole.wait_recv()
    mine[...] = total + jnp.sum(landed[...], axis=0)

    slot = core * chips + chip
    out_ref[slot] = mine[...]

    def spread(j, carry):
        pltpu.make_async_remote_copy(
            src_ref=mine,
            dst_ref=out_ref.at[slot],
            send_sem=back_send,
            recv_sem=back_recv,
            device_id=device((chip + j) % chips),
            device_id_type=BY_ID,
        ).start()
        return carry

    lax.fori_loop(1, chips, spread, 0)
    gathered = pltpu.make_async_remote_copy(
        src_ref=own.at[pl.ds(0, chips - 1)],
        dst_ref=landed,
        send_sem=back_send,
        recv_sem=back_recv,
        device_id=mate,
        device_id_type=BY_ID,
    )
    gathered.wait_recv()
    half = pl.ds(core * chips, chips)
    last = pltpu.make_async_remote_copy(
        src_ref=out_ref.at[half],
        dst_ref=out_ref.at[half],
        send_sem=last_send,
        recv_sem=last_recv,
        device_id=mate,
        device_id_type=BY_ID,
    )
    last.start()
    last.wait()
    swap.wait_send()
    whole.wait_send()
    gathered.wait_send()


def sum_everywhere(part):
    tiles = part.shape[0]
    f32 = jnp.float32
    dma = pltpu.SemaphoreType.DMA
    vmem = pl.BlockSpec(memory_space=pltpu.VMEM)
    tile = part.shape[1:]
    return pl.pallas_call(
        sum_kernel,
        out_shape=jax.ShapeDtypeStruct(part.shape, f32),
        in_specs=[vmem],
        out_specs=vmem,
        scratch_shapes=[
            pltpu.VMEM((tiles // 2,) + tile, f32),
            pltpu.VMEM((tiles // 2,) + tile, f32),
            pltpu.VMEM((tiles // 2 - 1,) + tile, f32),
            pltpu.VMEM(tile, f32),
        ] + [dma] * 8,
        compiler_params=pltpu.CompilerParams(
            collective_id=2, has_side_effects=True, vmem_limit_bytes=16 * MIB
        ),
        name="sum_everywhere",
    )(part)


def on_device(
    start_field, class_ids, run_levels, steepness, step_pick, input_layer, output_layer, output_bias
):
    bias = output_bias[None, :]
    misfit, turned, sums = solve(
        start_field, class_ids, run_levels.T, steepness[None, :], step_pick[None, :],
        input_layer, bias, output_layer,
    )
    output_next, misfit, bias_next, input_next = update(
        turned, misfit, output_layer, bias, sums, input_layer
    )
    return (misfit, output_next, bias_next[0], input_next)


def solution(mesh):
    split = Mesh(mesh.devices.reshape(2, 2, 2, 4, 4), AXES)
    return jax.shard_map(
        on_device,
        mesh=split,
        in_specs=(
            P(GRP, TILE, None),
            P(TILE, None),
            P(),
            P(),
            P(),
            P(),
            P(None, GRP + TILE),
            P(GRP + TILE),
        ),
        out_specs=(P(None, GRP + TILE), P(None, GRP + TILE), P(GRP + TILE), P()),
        check_vma=False,
    )
```

```python
import math

import jax
import jax.numpy as jnp
from jax import lax
from jax.experimental import pallas as pl
from jax.experimental.pallas import tpu as pltpu
from jax.sharding import Mesh
from jax.sharding import PartitionSpec as P

STEPS = 4
LEVELS = 8
CLASSES = 8
AXES = ("xh", "core", "xl", "y", "z")
GRP = ("xh", "core")
TILE = ("xl", "y", "z")
BY_ID = pl.DeviceIdType.MESH
MIB = 2**20
CHUNKS = 8
SUB = 8


def place():
    return {axis: lax.axis_index(axis) for axis in AXES}


def at(here, **moved):
    return tuple(moved.get(axis, here[axis]) for axis in AXES)


def beside(here, step):
    tile = here["xl"] * 16 + here["y"] * 4 + here["z"] + step
    tile = (tile + 32) % 32
    return at(here, xl=tile // 16, y=(tile // 4) % 4, z=tile % 4)


def dot(a, b):
    return lax.dot_general(a, b, (((1,), (0,)), ((), ())), preferred_element_type=jnp.float32)


def dot_turned(a, b):
    return lax.dot_general(a, b, (((1,), (1,)), ((), ())), preferred_element_type=jnp.float32)


def two_parts(x):
    high = x.astype(jnp.bfloat16)
    return high, (x - high.astype(jnp.float32)).astype(jnp.bfloat16)


def dot_parts(x, order):
    high, low = two_parts(x)
    return dot(high, order) + dot(low, order)


def solve_kernel(
    field_ref, ids_ref, levels_ref, steep_ref, pick_ref, input_ref, bias_ref, weight_ref,
    misfit_ref, turned_ref, sums_ref,
    about_ref, raw, rows_own, class_ref, halo_up, halo_dn, class_up, class_dn, kappa, wide_a, wide_b, picked, sent, got,
    relay, weight, hidden, turned, gain, pred, misfit, misfit_far, grad,
    tiles, pair, own, landed, middle, landed_z, mine,
    load_sem, halo_send, halo_recv, class_send, class_recv, out_send, out_recv, keep_sem, weight_sem,
    relay_send, relay_recv, sum_send, sum_recv,
):
    here = place()
    runs = rows_own.shape[1]
    tile_rows = rows_own.shape[0]
    width = rows_own.shape[2]
    part = runs // CHUNKS
    tile = here["xl"] * 16 + here["y"] * 4 + here["z"]
    group = here["xh"] * 2 + here["core"]
    up, dn = beside(here, -1), beside(here, 1)
    has_up, has_dn = tile > 0, tile < 31
    mates = (
        (here["xh"] * 2 + 1 - here["core"], at(here, core=1 - here["core"])),
        ((1 - here["xh"]) * 2 + here["core"], at(here, xh=1 - here["xh"])),
        ((1 - here["xh"]) * 2 + 1 - here["core"], at(here, xh=1 - here["xh"], core=1 - here["core"])),
    )

    def load(k):
        lines = part * tile_rows
        return [
            pltpu.make_async_copy(
                field_ref.at[pl.ds(k * lines, lines), pl.ds(128 * c, 128)],
                raw.at[c, pl.ds(k * lines, lines)],
                load_sem.at[k, c],
            )
            for c in range(width // 128)
        ]

    for k in range(CHUNKS):
        for copy in load(k):
            copy.start()
    weight_load = pltpu.make_async_copy(weight_ref, weight, weight_sem)
    weight_load.start()

    barrier = pltpu.get_barrier_semaphore()
    for _, mate in mates:
        pl.semaphore_signal(barrier, inc=1, device_id=mate, device_id_type=BY_ID)

    @pl.when(has_up)
    def _():
        pl.semaphore_signal(barrier, inc=1, device_id=up, device_id_type=BY_ID)

    @pl.when(has_dn)
    def _():
        pl.semaphore_signal(barrier, inc=1, device_id=dn, device_id_type=BY_ID)

    xl = here["xl"]
    ends_dn, ends_up = tile == 15, tile == 16
    corner = 3 * (1 - xl)
    relay_path = (here["y"] - corner + 4) % 4
    is_relay = (here["z"] == corner) & (relay_path > 0)
    relay_from = at(here, y=corner)
    relay_to = at(here, xl=1 - xl, y=3 * xl, z=3 * xl)

    @pl.when(is_relay)
    def _():
        for other in (relay_from, relay_to):
            pl.semaphore_signal(barrier, inc=1, device_id=other, device_id_type=BY_ID)

    @pl.when(ends_dn | ends_up)
    def _():
        for side in range(2):
            for p in range(1, 4):
                edge_at = 3 * (1 - side)
                other = at(here, xl=side, y=(edge_at + p) % 4, z=edge_at)
                pl.semaphore_signal(barrier, inc=1, device_id=other, device_id_type=BY_ID)

    plane = here["xh"] * 8 + here["xl"] * 4 + here["y"]

    def in_plane(k):
        return at(here, xh=k // 8, xl=(k // 4) % 2, y=k % 4)

    def greet(j, none):
        other = in_plane((plane + j) % 16)
        pl.semaphore_signal(barrier, inc=1, device_id=other, device_id_type=BY_ID)
        return none

    lax.fori_loop(1, 16, greet, 0)
    for j in range(1, 4):
        other = at(here, z=(here["z"] + j) % 4)
        pl.semaphore_signal(barrier, inc=1, device_id=other, device_id_type=BY_ID)

    callers = 3 + 18 + jnp.where(has_up, 1, 0) + jnp.where(has_dn, 1, 0)
    callers = callers + jnp.where(is_relay, 2, 0)
    callers = callers + jnp.where(ends_dn | ends_up, 6, 0)
    pl.semaphore_wait(barrier, callers)

    def class_copy(upward):
        return pltpu.make_async_remote_copy(
            src_ref=class_ref.at[pl.ds(0 if upward else tile_rows - STEPS, STEPS)],
            dst_ref=class_dn if upward else class_up,
            send_sem=class_send.at[0 if upward else 1],
            recv_sem=class_recv.at[0 if upward else 1],
            device_id=up if upward else dn,
            device_id_type=BY_ID,
        )

    def halo_copy(k, upward):
        span = pl.ds(pl.multiple_of(k * part, part), part)
        return pltpu.make_async_remote_copy(
            src_ref=rows_own.at[pl.ds(0 if upward else tile_rows - STEPS, STEPS), span],
            dst_ref=(halo_dn if upward else halo_up).at[:, span],
            send_sem=halo_send.at[k, 0 if upward else 1],
            recv_sem=halo_recv.at[k, 0 if upward else 1],
            device_id=up if upward else dn,
            device_id_type=BY_ID,
        )

    def detour_copy(k, upward):
        span = pl.ds(pl.multiple_of(k * part, part), part)
        return pltpu.make_async_remote_copy(
            src_ref=rows_own.at[pl.ds(0 if upward else tile_rows - STEPS, STEPS), span],
            dst_ref=relay.at[k // 4],
            send_sem=halo_send.at[k, 0 if upward else 1],
            recv_sem=relay_recv.at[k // 4],
            device_id=at(here, y=(here["y"] + k % 4) % 4),
            device_id_type=BY_ID,
        )

    def forward_copy(k, upward):
        span = pl.ds(pl.multiple_of(k * part, part), part)
        return pltpu.make_async_remote_copy(
            src_ref=relay.at[k // 4],
            dst_ref=(halo_dn if upward else halo_up).at[:, span],
            send_sem=relay_send.at[k // 4],
            recv_sem=halo_recv.at[k, 0 if upward else 1],
            device_id=relay_to,
            device_id_type=BY_ID,
        )

    def send_halo(k, upward):
        detour = (ends_up if upward else ends_dn) & (k % 4 > 0)

        @pl.when((has_up if upward else has_dn) & jnp.logical_not(detour))
        def _():
            halo_copy(k, upward).start()

        @pl.when(detour)
        def _():
            detour_copy(k, upward).start()

    def out_copy(k, j):
        span = pl.ds(pl.multiple_of(k * part, part), part)
        owner, mate = mates[j]
        return pltpu.make_async_remote_copy(
            src_ref=sent.at[owner, span],
            dst_ref=got.at[j, span],
            send_sem=out_send.at[k, j],
            recv_sem=out_recv.at[k, j],
            device_id=mate,
            device_id_type=BY_ID,
        )

    @pl.when(jnp.logical_not(has_up))
    def _():
        halo_up[...] = jnp.zeros_like(halo_up)
        class_up[...] = jnp.full_like(class_up, -1.0)

    @pl.when(jnp.logical_not(has_dn))
    def _():
        halo_dn[...] = jnp.zeros_like(halo_dn)
        class_dn[...] = jnp.full_like(class_dn, -1.0)

    first = lax.broadcasted_iota(jnp.int32, (width, width), 0)
    second = lax.broadcasted_iota(jnp.int32, (width, width), 1)
    blocks = width // 128
    order = jnp.where(first == (second % 128) * blocks + second // 128, 1.0, 0.0)
    order = order.astype(jnp.bfloat16)
    lines = part * tile_rows
    of_run = [
        levels_ref[...].astype(jnp.float32),
        steep_ref[...],
        pick_ref[...].astype(jnp.float32),
        jnp.zeros((128 - CLASSES - 2, about_ref.shape[0]), jnp.float32),
    ]
    about_ref[...] = jnp.concatenate(of_run, axis=0).T[:, : about_ref.shape[1]]
    class_rows = dot(ids_ref[...].astype(jnp.float32).astype(jnp.bfloat16), order)
    for i in range(tile_rows):
        class_ref[i] = jnp.broadcast_to(class_rows[i : i + 1], (SUB, width))

    @pl.when(has_up)
    def _():
        class_copy(True).start()

    @pl.when(has_dn)
    def _():
        class_copy(False).start()

    def prepare(k, none):
        for copy in load(k):
            copy.wait()
        span = pl.ds(pl.multiple_of(k * lines, lines), lines)
        lined = jnp.concatenate([raw[c, span] for c in range(blocks)], axis=1)
        lined = dot_parts(lined, order)
        for c in range(blocks):
            raw[c, span] = lined[:, 128 * c : 128 * c + 128]

        def turn(j, carry):
            first = pl.multiple_of(j * SUB, SUB)
            for i in range(tile_rows):
                for c in range(blocks):
                    rows_own[i, pl.ds(first, SUB), pl.ds(128 * c, 128)] = raw[
                        c, pl.ds(j * (SUB * tile_rows) + i, SUB, stride=tile_rows), :
                    ]
            return carry

        lax.fori_loop(k * (part // SUB), (k + 1) * (part // SUB), turn, 0)

        send_halo(k, True)
        send_halo(k, False)
        return none

    lax.fori_loop(0, CHUNKS, prepare, 0)

    @pl.when(has_up)
    def _():
        class_copy(False).wait_recv()

    @pl.when(has_dn)
    def _():
        class_copy(True).wait_recv()

    keep_up = jnp.where(has_up, 1.0, 0.0).astype(jnp.float32)
    keep_dn = jnp.where(has_dn, 1.0, 0.0).astype(jnp.float32)
    lane = lax.broadcasted_iota(jnp.int32, (SUB, 128), 1)
    left, right = lane == 0, lane == 127
    edge = width - 128

    def next_column(x):
        turned = jnp.where(right, 0.0, pltpu.roll(x[:, :128], 127, 1))
        return jnp.concatenate([x[:, 128:], turned], axis=1)

    def last_column(x, outermost):
        turned = jnp.where(left, outermost[:, :128], pltpu.roll(x[:, edge:], 1, 1))
        return jnp.concatenate([turned, x[:, :edge]], axis=1)

    span_rows = tile_rows + 2 * STEPS

    def advance(k, half_chunk):
        first = pl.multiple_of(k * part + half_chunk * SUB, SUB)
        runs_here = pl.ds(first, SUB)
        picked_here = pl.ds(pl.multiple_of(half_chunk * SUB, SUB), SUB)
        about = about_ref[pl.ds(pl.multiple_of(group * runs + first, SUB), SUB)]
        table = 0.015 * jnp.exp(about[:, :CLASSES] * math.log(1.35))
        steep = jnp.broadcast_to(about[:, CLASSES : CLASSES + 1], (SUB, width))
        pick = jnp.broadcast_to(about[:, CLASSES + 1 : CLASSES + 2], (SUB, width))
        rest = 1.0 - steep
        half = [jnp.broadcast_to(table[:, c : c + 1], (SUB, width)) for c in range(CLASSES)]
        for i in range(span_rows):
            if i < STEPS:
                klass = class_up[i]
            elif i < STEPS + tile_rows:
                klass = class_ref[i - STEPS]
            else:
                klass = class_dn[i - STEPS - tile_rows]
            value = jnp.zeros((SUB, width), jnp.float32)
            for c in range(CLASSES):
                value = jnp.where(klass == float(c), half[c], value)
            kappa[i] = value

        def start_row(i):
            if i < STEPS:
                return halo_up[i, runs_here]
            if i < STEPS + tile_rows:
                return rows_own[i - STEPS, runs_here]
            return halo_dn[i - STEPS - tile_rows, runs_here]

        for step in range(STEPS):
            source = (None, wide_a, wide_b, wide_a)[step]
            sink = (wide_a, wide_b, wide_a, None)[step]

            def row(i):
                return start_row(i) if step == 0 else source[i]

            def spread_of(i, value):
                bottom = 1.0 + value * value
                guess = pl.reciprocal(bottom, approx=True)
                guess = guess * (2.0 - bottom * guess)
                return kappa[i] * (steep + rest * guess)

            above = row(step)
            above_spread = spread_of(step, above)
            centre = row(step + 1)
            spread = spread_of(step + 1, centre)
            flow_in = (above_spread + spread) * (centre - above)
            for i in range(step + 1, span_rows - step - 1):
                below = row(i + 1)
                below_spread = spread_of(i + 1, below)
                flow_out = (spread + below_spread) * (below - centre)
                flow = (spread + next_column(spread)) * (next_column(centre) - centre)
                back = last_column(flow, spread * centre)
                total = centre + (flow_out - flow_in) + (flow - back)
                if i < STEPS:
                    total = total * keep_up
                if i >= STEPS + tile_rows:
                    total = total * keep_dn
                if sink is not None:
                    sink[i] = total
                if STEPS <= i < STEPS + tile_rows:
                    if step > 0:
                        total = jnp.where(pick == step + 1.0, total, picked[i - STEPS, picked_here])
                    picked[i - STEPS, picked_here] = total
                flow_in, centre, spread = flow_out, below, below_spread

    back_order = jnp.where(second == (first % 128) * blocks + first // 128, 1.0, 0.0)
    back_order = back_order.astype(jnp.bfloat16)

    def one_chunk(k, none):
        for upward in (False, True):
            for slot in range(CHUNKS // 4):
                @pl.when(is_relay & (xl == int(upward)) & (k == 2 * slot))
                def _():
                    passed = relay_path + 4 * slot
                    forward = forward_copy(passed, upward)
                    detour_copy(passed, upward).wait_recv()
                    forward.start()

        @pl.when(has_up)
        def _():
            halo_copy(k, False).wait_recv()

        @pl.when(has_dn)
        def _():
            halo_copy(k, True).wait_recv()

        def half_of(half_chunk, carry):
            advance(k, half_chunk)
            return carry

        lax.fori_loop(0, part // SUB, half_of, 0)
        lined = dot_parts(picked[...].reshape(tile_rows * part, width), back_order)
        span = pl.ds(pl.multiple_of(k * part, part), part)
        for i in range(tile_rows):
            sent[i // 4, span, pl.ds((i % 4) * width, width)] = lined[i * part : (i + 1) * part]
        for j in range(3):
            out_copy(k, j).start()
        return none

    lax.fori_loop(0, CHUNKS, one_chunk, 0)

    cells = weight.shape[1]
    hid = weight.shape[0]
    all_runs = hidden.shape[0]
    block = 256
    f32, bf16 = jnp.float32, jnp.bfloat16
    eye = lax.broadcasted_iota(jnp.int32, (block, block), 0) == lax.broadcasted_iota(
        jnp.int32, (block, block), 1
    )
    share = 2.0 / all_runs
    eye = jnp.where(eye, -0.5 * share, 0.0).astype(bf16)
    about = about_ref[...]
    steep_all = about[:, CLASSES : CLASSES + 1]
    feats = input_ref.shape[0]
    onehots = CLASSES * LEVELS
    entry = lax.broadcasted_iota(jnp.int32, (16, feats), 0)
    column = lax.broadcasted_iota(jnp.int32, (16, feats), 1)
    source = jnp.where(column < onehots, column // LEVELS, CLASSES + 1)
    spread_out = dot(about.astype(bf16), jnp.where(entry == source, 1.0, 0.0).astype(bf16))
    column = lax.broadcasted_iota(jnp.int32, (all_runs, feats), 1)
    wanted = jnp.where(column < onehots, column % LEVELS, column - onehots + 1)
    wanted = jnp.where(column < onehots + STEPS, wanted, -1).astype(f32)
    onehot = jnp.where(spread_out == wanted, 1.0, 0.0).astype(bf16)

    def independent(rows):
        count = rows.shape[0]
        kept = LEVELS - 1
        levels_end, moments_end = CLASSES * kept, CLASSES * kept + STEPS - 1
        high, middle = two_parts(rows)
        low = (rows - high.astype(f32) - middle.astype(f32)).astype(bf16)
        line = lax.broadcasted_iota(jnp.int32, (64, 16), 0)
        entry = lax.broadcasted_iota(jnp.int32, (64, 16), 1)
        source = jnp.where(line < levels_end, line // kept, CLASSES + 1)
        source = jnp.where(line > moments_end, CLASSES, source)

        def chosen(last, extra):
            keep = (entry == source) & ((line < last) | (line == extra))
            return jnp.where(keep, 1.0, 0.0).astype(bf16)

        value = (
            dot_turned(chosen(moments_end, moments_end + 1), high)
            + dot_turned(chosen(0, moments_end + 2), middle)
            + dot_turned(chosen(0, moments_end + 3), low)
        )
        line = lax.broadcasted_iota(jnp.int32, (64, count), 0)
        wanted = jnp.where(line < levels_end, line % kept, line - levels_end + 1).astype(f32)
        marks = jnp.where(value == wanted, 1.0, 0.0)
        value = jnp.where(line < moments_end, marks, value)
        return jnp.where(line == moments_end, 1.0, value).astype(bf16)

    def hidden_block(n, none):
        span = pl.ds(pl.multiple_of(n * block, block), block)
        value = input_ref[:, span]
        high, low = two_parts(value)
        rest = (value - high.astype(f32) - low.astype(f32)).astype(bf16)
        pre = dot(onehot, high) + (dot(onehot, low) + dot(onehot, rest))
        pre = pre + steep_all * value[value.shape[0] - 1 :, :]
        logistic = 1.0 / (1.0 + jnp.exp(-pre))
        active = (pre * logistic).astype(bf16)
        hidden[:, span] = active
        gain[:, span] = logistic * (1.0 + pre * (1.0 - logistic)) * share
        turned[span, :] = dot_turned(eye, active).astype(bf16)
        return none

    lax.fori_loop(0, hid // block, hidden_block, 0)
    turned_copy = pltpu.make_async_copy(turned, turned_ref, keep_sem.at[0])
    turned_copy.start()
    weight_load.wait()

    def pred_block(n, none):
        span = pl.ds(pl.multiple_of(n * block, block), block)
        pred[:, span] = dot(hidden[...], weight[:, span]) + bias_ref[:, span]
        return none

    lax.fori_loop(0, cells // block, pred_block, 0)

    def compare(source, group_at, start, count, copy_row):
        def some(b, none):
            inner = pl.multiple_of(start + b * 16, 16)
            at_run = pl.ds(pl.multiple_of(group_at * runs + inner, 16), 16)
            value = (pred[at_run] - source[pl.ds(inner, 16)]).astype(bf16)
            misfit[at_run] = value
            if copy_row is not None:
                misfit_far[pl.ds(pl.multiple_of(copy_row + b * 16, 16), 16)] = value
            return none

        lax.fori_loop(0, count // 16, some, 0)

    for k in range(CHUNKS):
        out_copy(k, 0).wait_recv()
    compare(sent.at[group], group, 0, runs, None)
    compare(got.at[0], mates[0][0], 0, runs, None)
    near = pl.ds(pl.multiple_of(here["xh"] * (2 * runs), 2 * runs), 2 * runs)
    far = (1 - here["xh"]) * (2 * runs)

    near_mix = independent(about_ref[near])

    def near_block(n, none):
        span = pl.ds(pl.multiple_of(n * block, block), block)
        back = dot_turned(misfit[near], weight[span, :]) * gain[near, span]
        high, low = two_parts(back)
        grad[:, span] = dot(near_mix, high) + dot(near_mix, low)
        return none

    lax.fori_loop(0, hid // block, near_block, 0, unroll=4)
    near_copy = pltpu.make_async_copy(misfit.at[near], misfit_ref.at[near], keep_sem.at[1])
    near_copy.start()

    half = runs // 2
    for h in range(2):
        for k in range(h * CHUNKS // 2, (h + 1) * CHUNKS // 2):
            out_copy(k, 1).wait_recv()
            out_copy(k, 2).wait_recv()
        for j in (1, 2):
            at_row = here["core"] if j == 1 else 1 - here["core"]
            compare(got.at[j], mates[j][0], h * half, half, at_row * half)

        far_rows = [pl.ds(pl.multiple_of(far + g * runs + h * half, half), half) for g in range(2)]
        mix = independent(jnp.concatenate([about_ref[rows] for rows in far_rows], axis=0))

        def far_block(n, none):
            span = pl.ds(pl.multiple_of(n * block, block), block)
            factor = jnp.concatenate([gain[rows, span] for rows in far_rows], axis=0)
            back = dot_turned(misfit_far[...], weight[span, :]) * factor
            high, low = two_parts(back)
            grad[:, span] += dot(mix, high) + dot(mix, low)
            return none

        lax.fori_loop(0, hid // block, far_block, 0, unroll=True)

    far_span = pl.ds(pl.multiple_of(far, 2 * runs), 2 * runs)
    far_copy = pltpu.make_async_copy(misfit.at[far_span], misfit_ref.at[far_span], keep_sem.at[2])
    far_copy.start()
    for i in range(tiles.shape[0]):
        r, c = i // (hid // 128), i % (hid // 128)
        tiles[i] = grad[8 * r : 8 * r + 8, 128 * c : 128 * c + 128]

    def sum_copy(stage, source, sink, device):
        return pltpu.make_async_remote_copy(
            src_ref=source,
            dst_ref=sink,
            send_sem=sum_send.at[stage],
            recv_sem=sum_recv.at[stage],
            device_id=device,
            device_id_type=BY_ID,
        )

    core, z = here["core"], here["z"]
    mate = at(here, core=1 - core)
    share_of = 4
    chips = own.shape[0]
    swap = sum_copy(0, tiles.at[pl.ds((1 - core) * chips, chips)], pair, mate)
    swap.start()
    swap.wait_recv()
    own[...] = tiles[pl.ds(core * chips, chips)] + pair[...]

    def scatter(j, none):
        other = (plane + j) % 16
        sum_copy(
            1,
            own.at[pl.ds(other * share_of, share_of)],
            landed.at[pl.ds((j - 1) * share_of, share_of)],
            in_plane(other),
        ).start()
        return none

    lax.fori_loop(1, 16, scatter, 0)
    scattered = sum_copy(1, own.at[pl.ds(0, 15 * share_of)], landed, mate)
    scattered.wait_recv()
    total = own[pl.ds(plane * share_of, share_of)]
    for j in range(15):
        total = total + landed[j * share_of : (j + 1) * share_of]
    middle[...] = total
    for j in range(1, 4):
        other = (z + j) % 4
        sum_copy(2, middle.at[other], landed_z.at[j - 1], at(here, z=other)).start()
    scattered_z = sum_copy(2, middle.at[pl.ds(0, 3)], landed_z, mate)
    scattered_z.wait_recv()
    mine[...] = middle[z] + (landed_z[0] + landed_z[1] + landed_z[2])
    slot = core * chips + plane * share_of
    sums_ref[slot + z] = mine[...]
    for j in range(1, 4):
        sum_copy(3, mine, sums_ref.at[slot + z], at(here, z=(z + j) % 4)).start()
    gathered_z = sum_copy(3, middle.at[pl.ds(0, 3)], landed_z, mate)
    gathered_z.wait_recv()
    quad = pl.ds(slot, share_of)

    def gather(j, none):
        sum_copy(4, sums_ref.at[quad], sums_ref.at[quad], in_plane((plane + j) % 16)).start()
        return none

    lax.fori_loop(1, 16, gather, 0)
    gathered = sum_copy(4, own.at[pl.ds(0, 15 * share_of)], landed, mate)
    gathered.wait_recv()
    half_sums = sums_ref.at[pl.ds(core * chips, chips)]
    last = sum_copy(5, half_sums, half_sums, mate)
    last.start()
    last.wait()
    for copy in (swap, scattered, scattered_z, gathered_z, gathered):
        copy.wait_send()

    @pl.when(is_relay)
    def _():
        for slot in range(CHUNKS // 4):
            forward_copy(relay_path + 4 * slot, False).wait_send()

    turned_copy.wait()
    near_copy.wait()
    far_copy.wait()
    for k in range(CHUNKS):
        for j in range(3):
            out_copy(k, j).wait_send()

    @pl.when(has_up)
    def _():
        class_copy(True).wait_send()
        for k in range(CHUNKS):
            halo_copy(k, True).wait_send()

    @pl.when(has_dn)
    def _():
        class_copy(False).wait_send()
        for k in range(CHUNKS):
            halo_copy(k, False).wait_send()


def solve(field, classes, levels, steep, pick, input_layer, bias, weight):
    runs, rows, width = field.shape
    hid, cells = weight.shape
    all_runs = levels.shape[1]
    f32, bf16 = jnp.float32, jnp.bfloat16
    dma = pltpu.SemaphoreType.DMA
    vmem = pl.BlockSpec(memory_space=pltpu.VMEM)
    anywhere = pl.BlockSpec(memory_space=pl.ANY)
    span = rows + 2 * STEPS
    part = runs // CHUNKS
    return pl.pallas_call(
        solve_kernel,
        out_shape=(
            jax.ShapeDtypeStruct((all_runs, cells), bf16),
            jax.ShapeDtypeStruct((hid, all_runs), bf16),
            jax.ShapeDtypeStruct((hid // 16, 8, 128), f32),
        ),
        in_specs=[anywhere] + [vmem] * 6 + [anywhere],
        out_specs=(anywhere, anywhere, vmem),
        scratch_shapes=[
            pltpu.VMEM((all_runs, 16), f32),
            pltpu.VMEM((width // 128, runs * rows, 128), f32),
            pltpu.VMEM((rows, runs, width), f32),
            pltpu.VMEM((rows, SUB, width), f32),
            pltpu.VMEM((STEPS, runs, width), f32),
            pltpu.VMEM((STEPS, runs, width), f32),
            pltpu.VMEM((STEPS, SUB, width), f32),
            pltpu.VMEM((STEPS, SUB, width), f32),
            pltpu.VMEM((span, SUB, width), f32),
            pltpu.VMEM((span, SUB, width), f32),
            pltpu.VMEM((span, SUB, width), f32),
            pltpu.VMEM((rows, part, width), f32),
            pltpu.VMEM((4, runs, 4 * width), f32),
            pltpu.VMEM((3, runs, 4 * width), f32),
            pltpu.VMEM((CHUNKS // 4, STEPS, part, width), f32),
            pltpu.VMEM((hid, cells), bf16),
            pltpu.VMEM((all_runs, hid), bf16),
            pltpu.VMEM((hid, all_runs), bf16),
            pltpu.VMEM((all_runs, hid), f32),
            pltpu.VMEM((all_runs, cells), f32),
            pltpu.VMEM((all_runs, cells), bf16),
            pltpu.VMEM((runs, cells), bf16),
            pltpu.VMEM((64, hid), f32),
            pltpu.VMEM((hid // 16, 8, 128), f32),
            pltpu.VMEM((hid // 32, 8, 128), f32),
            pltpu.VMEM((hid // 32, 8, 128), f32),
            pltpu.VMEM((60, 8, 128), f32),
            pltpu.VMEM((4, 8, 128), f32),
            pltpu.VMEM((3, 8, 128), f32),
            pltpu.VMEM((8, 128), f32),
            dma((CHUNKS, 4)),
            dma((CHUNKS, 2)),
            dma((CHUNKS, 2)),
            dma((2,)),
            dma((2,)),
            dma((CHUNKS, 3)),
            dma((CHUNKS, 3)),
            dma((3,)),
            dma,
            dma((CHUNKS // 4,)),
            dma((CHUNKS // 4,)),
            dma((6,)),
            dma((6,)),
        ],
        compiler_params=pltpu.CompilerParams(
            collective_id=1, has_side_effects=True, vmem_limit_bytes=58 * MIB
        ),
        name="solve",
    )(
        field.reshape(runs * rows, width), classes, levels, steep, pick, input_layer, bias, weight,
    )


def update_kernel(
    turned_ref, misfit_ref, weight_ref, bias_ref, sums_ref, input_ref,
    next_ref, misfit_out_ref, bias_out_ref, input_out_ref,
):
    f32, bf16 = jnp.float32, jnp.bfloat16
    step = 1.0 / misfit_ref.shape[0]
    block = 256

    def columns(n, none):
        span = pl.ds(pl.multiple_of(n * block, block), block)
        change = dot(turned_ref[...], misfit_ref[:, span])
        next_ref[:, span] = (weight_ref[:, span].astype(f32) + change).astype(bf16)
        return none

    lax.fori_loop(0, misfit_ref.shape[1] // block, columns, 0, unroll=True)
    rows = misfit_out_ref.shape[0]
    here = pl.multiple_of(pl.program_id(0) * rows, rows)
    value = misfit_ref[pl.ds(here, rows)]
    misfit_out_ref[...] = value

    @pl.when(pl.program_id(0) == 0)
    def _():
        bias_out_ref[...] = bias_ref[...]
        feats, hid = input_ref.shape
        kept = LEVELS - 1
        levels_end, moments_end = CLASSES * kept, CLASSES * kept + STEPS - 1
        row = lax.broadcasted_iota(jnp.int32, (feats, 192), 0)
        line = lax.broadcasted_iota(jnp.int32, (feats, 192), 1) % 64
        group = jnp.where(row < CLASSES * LEVELS, row // LEVELS, CLASSES)
        inner = row - group * LEVELS
        length = jnp.where(group < CLASSES, kept, STEPS - 1)
        line_group = jnp.where(line < levels_end, line // kept, CLASSES)
        line_inner = line - line_group * kept
        same = (group == line_group) & (line < moments_end)
        mix = jnp.where(same & (inner == line_inner), 1.0, 0.0)
        mix = jnp.where(inner == length, jnp.where(same, -1.0, mix), mix)
        mix = jnp.where((inner == length) & (line == moments_end), 1.0, mix)
        steep = jnp.where((line > moments_end) & (line <= moments_end + 3), 1.0, 0.0)
        mix = jnp.where(row == feats - 1, steep, mix).astype(bf16)
        across = hid // 128
        for c in range(0, across, 2):
            sums = jnp.concatenate(
                [
                    jnp.concatenate([sums_ref[r * across + c + d] for r in range(8)], axis=0)
                    for d in range(2)
                ],
                axis=1,
            )
            high, middle = two_parts(sums)
            low = (sums - high.astype(f32) - middle.astype(f32)).astype(bf16)
            grad = dot(mix, jnp.concatenate([high, middle, low], axis=0))
            span = slice(128 * c, 128 * c + 256)
            input_out_ref[:, span] = input_ref[:, span] - 2.0 * grad

    bias_out_ref[...] -= step * jnp.sum(value.astype(f32), axis=0, keepdims=True)


def update(turned, misfit, weight, bias, sums, input_layer):
    hid, cells = weight.shape
    runs = misfit.shape[0]
    steps = 4
    whole = pl.BlockSpec((runs, cells), lambda i: (0, 0))
    line = pl.BlockSpec((1, cells), lambda i: (0, 0))
    layer = pl.BlockSpec(input_layer.shape, lambda i: (0, 0))
    all_sums = pl.BlockSpec(sums.shape, lambda i: (0, 0, 0))
    tile = pl.BlockSpec((hid // steps, cells), lambda i: (i, 0))
    return pl.pallas_call(
        update_kernel,
        grid=(steps,),
        out_shape=(
            jax.ShapeDtypeStruct(weight.shape, weight.dtype),
            jax.ShapeDtypeStruct(misfit.shape, misfit.dtype),
            jax.ShapeDtypeStruct(bias.shape, bias.dtype),
            jax.ShapeDtypeStruct(input_layer.shape, input_layer.dtype),
        ),
        in_specs=[pl.BlockSpec((hid // steps, runs), lambda i: (i, 0)), whole, tile, line, all_sums, layer],
        out_specs=(tile, pl.BlockSpec((runs // steps, cells), lambda i: (i, 0)), line, layer),
        compiler_params=pltpu.CompilerParams(vmem_limit_bytes=60 * MIB),
        cost_estimate=pl.CostEstimate(
            flops=2 * hid * cells * runs, bytes_accessed=4 * hid * cells, transcendentals=0
        ),
        name="update",
    )(turned, misfit, weight, bias, sums, input_layer)


def sum_kernel(
    part_ref, out_ref, pair, own, landed, mine,
    pair_send, pair_recv, part_send, part_recv, back_send, back_recv, last_send, last_recv,
):
    here = place()
    core = here["core"]
    chips = own.shape[0]
    chip = here["xh"] * 32 + here["xl"] * 16 + here["y"] * 4 + here["z"]
    mate = at(here, core=1 - core)

    def device(k):
        return (k // 32, core, (k // 16) % 2, (k // 4) % 4, k % 4)

    barrier = pltpu.get_barrier_semaphore()
    pl.semaphore_signal(barrier, inc=1, device_id=mate, device_id_type=BY_ID)

    def greet(j, carry):
        pl.semaphore_signal(
            barrier, inc=1, device_id=device((chip + j) % chips), device_id_type=BY_ID
        )
        return carry

    lax.fori_loop(1, chips, greet, 0)
    pl.semaphore_wait(barrier, chips)

    swap = pltpu.make_async_remote_copy(
        src_ref=part_ref.at[pl.ds((1 - core) * chips, chips)],
        dst_ref=pair,
        send_sem=pair_send,
        recv_sem=pair_recv,
        device_id=mate,
        device_id_type=BY_ID,
    )
    swap.start()
    swap.wait_recv()
    own[...] = part_ref[pl.ds(core * chips, chips)] + pair[...]

    def scatter(j, carry):
        other = (chip + j) % chips
        pltpu.make_async_remote_copy(
            src_ref=own.at[other],
            dst_ref=landed.at[j - 1],
            send_sem=part_send,
            recv_sem=part_recv,
            device_id=device(other),
            device_id_type=BY_ID,
        ).start()
        return carry

    lax.fori_loop(1, chips, scatter, 0)
    total = own[chip]
    whole = pltpu.make_async_remote_copy(
        src_ref=own.at[pl.ds(0, chips - 1)],
        dst_ref=landed,
        send_sem=part_send,
        recv_sem=part_recv,
        device_id=mate,
        device_id_type=BY_ID,
    )
    whole.wait_recv()
    mine[...] = total + jnp.sum(landed[...], axis=0)

    slot = core * chips + chip
    out_ref[slot] = mine[...]

    def spread(j, carry):
        pltpu.make_async_remote_copy(
            src_ref=mine,
            dst_ref=out_ref.at[slot],
            send_sem=back_send,
            recv_sem=back_recv,
            device_id=device((chip + j) % chips),
            device_id_type=BY_ID,
        ).start()
        return carry

    lax.fori_loop(1, chips, spread, 0)
    gathered = pltpu.make_async_remote_copy(
        src_ref=own.at[pl.ds(0, chips - 1)],
        dst_ref=landed,
        send_sem=back_send,
        recv_sem=back_recv,
        device_id=mate,
        device_id_type=BY_ID,
    )
    gathered.wait_recv()
    half = pl.ds(core * chips, chips)
    last = pltpu.make_async_remote_copy(
        src_ref=out_ref.at[half],
        dst_ref=out_ref.at[half],
        send_sem=last_send,
        recv_sem=last_recv,
        device_id=mate,
        device_id_type=BY_ID,
    )
    last.start()
    last.wait()
    swap.wait_send()
    whole.wait_send()
    gathered.wait_send()


def sum_everywhere(part):
    tiles = part.shape[0]
    f32 = jnp.float32
    dma = pltpu.SemaphoreType.DMA
    vmem = pl.BlockSpec(memory_space=pltpu.VMEM)
    tile = part.shape[1:]
    return pl.pallas_call(
        sum_kernel,
        out_shape=jax.ShapeDtypeStruct(part.shape, f32),
        in_specs=[vmem],
        out_specs=vmem,
        scratch_shapes=[
            pltpu.VMEM((tiles // 2,) + tile, f32),
            pltpu.VMEM((tiles // 2,) + tile, f32),
            pltpu.VMEM((tiles // 2 - 1,) + tile, f32),
            pltpu.VMEM(tile, f32),
        ] + [dma] * 8,
        compiler_params=pltpu.CompilerParams(
            collective_id=2, has_side_effects=True, vmem_limit_bytes=16 * MIB
        ),
        name="sum_everywhere",
    )(part)


def on_device(
    start_field, class_ids, run_levels, steepness, step_pick, input_layer, output_layer, output_bias
):
    bias = output_bias[None, :]
    misfit, turned, sums = solve(
        start_field, class_ids, run_levels.T, steepness[None, :], step_pick[None, :],
        input_layer, bias, output_layer,
    )
    output_next, misfit, bias_next, input_next = update(
        turned, misfit, output_layer, bias, sums, input_layer
    )
    return (misfit, output_next, bias_next[0], input_next)


def solution(mesh):
    split = Mesh(mesh.devices.reshape(2, 2, 2, 4, 4), AXES)
    return jax.shard_map(
        on_device,
        mesh=split,
        in_specs=(
            P(GRP, TILE, None),
            P(TILE, None),
            P(),
            P(),
            P(),
            P(),
            P(None, GRP + TILE),
            P(GRP + TILE),
        ),
        out_specs=(P(None, GRP + TILE), P(None, GRP + TILE), P(GRP + TILE), P()),
        check_vma=False,
    )
```
